32 devices in a mesh: rows: 16 (over z, x, core), img: 2 (over y).
Axes of the slice: x: 2, y: 2, z: 4, core: 2. Of those that a mesh axis runs over, the one named last changes fastest.
Arguments:
- triplane: bfloat16 [12288, 1024], P(('rows', 'img')), may hold values from -6 to 6
- cotangent: bfloat16 [12288, 1024], P(('rows', 'img')), may hold values from -6 to 6
- image_tokens: bfloat16 [16640, 768], P(('rows', 'img')), may hold values from -6 to 6
- modulation: float32 [16, 6, 1024], replicated, may hold values from -1.75 to 1.75
- image_counts: int32 [16], replicated, may hold values from 257 to 1025, as said below
- owner_slots: int32 [248], replicated, may hold values from 0 to 255, as said below
- master_weights: float32 [256, 256, 256], P(('rows', 'img')), as said below
- first_moment: float32 [256, 256, 256], P(('rows', 'img')), as said below
- second_moment: float32 [256, 256, 256], P(('rows', 'img')), as said below
- left_basis: float32 [256, 256, 256], P(('rows', 'img')), may hold values from -0.375 to 0.375
- right_basis: float32 [256, 256, 256], P(('rows', 'img')), may hold values from -0.375 to 0.375
Outputs:
- layer_out: bfloat16 [12288, 1024], P(('rows', 'img'))
- grad_triplane: float32 [12288, 1024], P(('rows', 'img'))
- grad_image: float32 [16640, 768], P(('rows', 'img'))
- weight_grads: float32 [256, 256, 256], P(('rows', 'img'))
- new_first_moment: float32 [256, 256, 256], P(('rows', 'img'))
- new_second_moment: float32 [256, 256, 256], P(('rows', 'img'))
- new_master: float32 [256, 256, 256], P(('rows', 'img'))
- new_weights: bfloat16 [256, 256, 256], P(('rows', 'img'))
The draws below stay inside these ranges and needn't reach their ends.
Inputs may be any that keep to these rules, and one draw needn't show every extreme that they name: `image_counts`: each count is 257 or 1025. `owner_slots`: distinct slots; slot s lies on device s // 8 of rows+img. `master_weights`: float32 values. `first_moment`: float32 values. `second_moment`: positive float32 values.
All inputs are finite; a program needn't handle non-finite values.
Results may differ from the reference program's by a relative error of at most 0.017.
Values may be sent and summed in bfloat16 or wider, within the bound.
A program may use at most 320 MiB of HBM per device.

```python
import jax
import jax.numpy as jnp
import numpy as np
from jax import lax

D = 1024
HEADS = 16
FF = 4096
DIMG = 768
TOK_DEV = 384
IMG_MAX = 1025
IMG_MIN = 257
BLOCK = 256
STEP = 5
CAP = 520
OBJ = 16
TRI_ROWS = 12288
IMG_ROWS = 16640
NBLK = 248
SLOTS = 256
N_ROWS = 16
N_IMG = 2


def shapes_list_drawn():
    return [(D, D), (DIMG, D), (DIMG, D), (D, D), (D, D), (D, D), (D, D), (D, D), (D, FF), (FF, D)]


def weight_scales_drawn():
    self_root = (2.0 * TOK_DEV) ** 0.5
    cross_root = (IMG_MAX / 2.0) ** 0.5
    return [D ** (-0.5), DIMG ** (-0.5), DIMG ** (-0.5), 0.5 * cross_root * D ** (-0.5), D ** (-0.5), D ** (-0.5), D ** (-0.5), 0.5 * self_root * D ** (-0.5), D ** (-0.5), 2.0 * FF ** (-0.5)]


def grad_scales():
    root_tokens = (1.0 * TRI_ROWS) ** 0.5
    self_root = (2.0 * TOK_DEV) ** 0.5
    cross_root = (IMG_MAX / 2.0) ** 0.5
    return [0.3 * root_tokens, 0.3 * root_tokens, 0.3 * root_tokens, 2.0 / cross_root * root_tokens, 0.3 * root_tokens, 0.3 * root_tokens, 0.5 * root_tokens, 2.0 / self_root * root_tokens, root_tokens, 0.6 * root_tokens]


def block_table_drawn(scales):
    pieces = []
    for shape_pair, scale_value in zip(shapes_list_drawn(), scales):
        amount = shape_pair[0] * shape_pair[1] // (BLOCK * BLOCK)
        pieces.append(np.full((amount,), scale_value, np.float32))
    return np.concatenate(pieces)


def place_value(order, wanted, position):
    where_now = jnp.argmax(order == wanted).astype(jnp.int32)
    moved = where_now >= NBLK
    previous = order[position]
    order = order.at[where_now].set(jnp.where(moved, previous, wanted))
    return order.at[position].set(jnp.where(moved, wanted, previous))


def slot_list(key):
    order = jax.random.permutation(jax.random.fold_in(key, 11), SLOTS).astype(jnp.int32)
    order = place_value(order, SLOTS - 1, 0)
    order = place_value(order, 0, 1)
    return order[:NBLK]


def slot_scales(key, scales):
    table = block_table_drawn(scales)
    filler = float(np.mean(table))
    return jnp.full((SLOTS,), filler, jnp.float32).at[slot_list(key)].set(jnp.asarray(table))


def draw_owner_slots(key, part):
    return slot_list(key)


def draw_image_counts(key, part):
    key = jax.random.fold_in(key, 5)
    split_keys = jax.random.split(key, 3)
    larger = jax.random.randint(split_keys[0], (OBJ,), 0, 5) < 3
    counts_out = jnp.where(larger, IMG_MAX, IMG_MIN).astype(jnp.int32)
    first_pick = jax.random.randint(split_keys[1], (), 0, OBJ)
    second_pick = (first_pick + 1 + jax.random.randint(split_keys[2], (), 0, OBJ - 1)) % OBJ
    return counts_out.at[first_pick].set(IMG_MAX).at[second_pick].set(IMG_MIN)


def draw_master_weights(key, part):
    scales = slot_scales(key, weight_scales_drawn())
    key = jax.random.fold_in(key, 21)
    noise = jnp.clip(jax.random.normal(key, (SLOTS, BLOCK, BLOCK), jnp.float32), -4.0, 4.0)
    return noise * scales[:, None, None]


def draw_first_moment(key, part):
    scales = slot_scales(key, grad_scales())
    key = jax.random.fold_in(key, 31)
    noise = jnp.clip(jax.random.normal(key, (SLOTS, BLOCK, BLOCK), jnp.float32), -4.0, 4.0)
    return noise * scales[:, None, None]


def draw_second_moment(key, part):
    scales = slot_scales(key, grad_scales())
    key = jax.random.fold_in(key, 41)
    factor = jax.random.uniform(key, (SLOTS, BLOCK, BLOCK), jnp.float32, minval=1.0, maxval=4.0)
    return factor * (scales * scales)[:, None, None]


def block_levels(rng, dims, cuts, smallest, high):
    loudness = 1.0
    for dim, blocks in cuts:
        draws = jax.random.uniform(jax.random.fold_in(jax.random.fold_in(rng, 6), dim), (blocks,), jnp.float32, smallest / len(cuts), high / len(cuts))
        loudness = loudness * jnp.repeat(jnp.exp(draws), dims[dim] // blocks).reshape((-1,) + (1,) * (len(dims) - 1 - dim))
    return loudness


def normal_values(own_key, dims, deviation, most, shards=(), kind=jnp.bfloat16):
    gain = block_levels(own_key, dims, shards, -0.22, 0.18) if shards else 1.0
    drawn = jax.random.normal(own_key, dims, jnp.float32) * deviation * gain
    return jnp.minimum(jnp.maximum(drawn, -most), most).astype(kind)


def setup_inputs(seed: int = 0) -> dict:
    key_of = jax.random.split(jax.random.key(seed), 12)
    return {
        "triplane": normal_values(key_of[0], (TRI_ROWS, D), 1.0, 6.0, ((0, 32),)),
        "cotangent": normal_values(key_of[1], (TRI_ROWS, D), 1.0, 6.0, ((0, 32),)),
        "image_tokens": normal_values(key_of[2], (IMG_ROWS, DIMG), 1.0, 6.0, ((0, 32),)),
        "modulation": normal_values(key_of[3], (OBJ, 6, D), 0.3, 1.75, (), jnp.float32),
        "image_counts": draw_image_counts(jax.random.fold_in(key_of[11], 71), 0),
        "owner_slots": draw_owner_slots(jax.random.fold_in(key_of[11], 71), 0),
        "master_weights": draw_master_weights(jax.random.fold_in(key_of[11], 71), 0),
        "first_moment": draw_first_moment(jax.random.fold_in(key_of[11], 71), 0),
        "second_moment": draw_second_moment(jax.random.fold_in(key_of[11], 71), 0),
        "left_basis": normal_values(key_of[9], (SLOTS, BLOCK, BLOCK), BLOCK ** -0.5, 0.375, ((0, 32),), jnp.float32),
        "right_basis": normal_values(key_of[10], (SLOTS, BLOCK, BLOCK), BLOCK ** -0.5, 0.375, ((0, 32),), jnp.float32),
    }


highest = lax.Precision.HIGHEST
moment_decay = 0.5

@jax.custom_vjp
def low(v):
    return lax.optimization_barrier(v.astype(jnp.bfloat16)).astype(jnp.float32)

@jax.custom_vjp
def low_back(v):
    return v

def low_keep(v):
    return (low(v), None)

def low_pass(kept, grad):
    return (grad,)

def back_keep(v):
    return (v, None)

def back_low(kept, grad):
    return (low(grad),)
low.defvjp(low_keep, low_pass)
low_back.defvjp(back_keep, back_low)

def shapes_list():
    return [(D, D), (DIMG, D), (DIMG, D), (D, D), (D, D), (D, D), (D, D), (D, D), (D, FF), (FF, D)]

def weight_scales():
    self_root = (2.0 * TOK_DEV) ** 0.5
    cross_root = (IMG_MAX / 2.0) ** 0.5
    return [D ** (-0.5), DIMG ** (-0.5), DIMG ** (-0.5), 0.5 * cross_root * D ** (-0.5), D ** (-0.5), D ** (-0.5), D ** (-0.5), 0.5 * self_root * D ** (-0.5), D ** (-0.5), 2.0 * FF ** (-0.5)]

def block_table(scales):
    pieces = []
    for shape_pair, scale_value in zip(shapes_list(), scales):
        amount = shape_pair[0] * shape_pair[1] // (BLOCK * BLOCK)
        pieces.append(np.full((amount,), scale_value, np.float32))
    return np.concatenate(pieces)

def split_blocks(blocks):
    matrices = []
    begin_at = 0
    for rows_in, cols_out in shapes_list():
        amount = rows_in * cols_out // (BLOCK * BLOCK)
        grid = blocks[begin_at:begin_at + amount].reshape(rows_in // BLOCK, cols_out // BLOCK, BLOCK, BLOCK)
        matrices.append(grid.transpose(0, 2, 1, 3).reshape(rows_in, cols_out))
        begin_at = begin_at + amount
    return matrices

def join_blocks(matrices):
    pieces = []
    for matrix in matrices:
        rows_in, cols_out = matrix.shape
        grid = matrix.reshape(rows_in // BLOCK, BLOCK, cols_out // BLOCK, BLOCK).transpose(0, 2, 1, 3)
        pieces.append(grid.reshape(-1, BLOCK, BLOCK))
    return jnp.concatenate(pieces, 0)

def modulated_norm(values, shift, scale):
    centered = values - lax.optimization_barrier(jnp.mean(values, axis=-1, keepdims=True))
    variance = lax.optimization_barrier(jnp.mean(centered * centered, axis=-1, keepdims=True))
    return centered * lax.rsqrt(variance + 1e-06) * (1.0 + scale) + shift

def both_round(values):
    return low_back(low(values))

def matmul(left, right):
    return jnp.dot(left, right, precision=highest)

def attention(queries, key_rows, value_rows, key_valid):
    head_dim = D // HEADS
    query_heads = queries.reshape(queries.shape[0], HEADS, head_dim)
    key_heads = key_rows.reshape(key_rows.shape[0], HEADS, head_dim)
    value_heads = value_rows.reshape(value_rows.shape[0], HEADS, head_dim)
    scores = low_back(jnp.einsum('qhd,khd->hqk', query_heads, key_heads, precision=highest) * head_dim ** (-0.5))
    scores = jnp.where(key_valid[None, None, :], scores, -1e+30)
    softmax_out = jax.nn.softmax(scores, axis=-1)
    mixed = jnp.einsum('hqk,khd->qhd', low(softmax_out), value_heads, precision=highest)
    return both_round(mixed.reshape(queries.shape[0], D))

def object_layer(params, triplane_rows, pixels, shifts, key_valid):
    q_cross, k_cross, v_cross, o_cross, q_self, k_self, v_self, o_self, w_up, w_down = params
    normed = low(modulated_norm(triplane_rows, shifts[0], shifts[1]))
    cross_queries = both_round(matmul(normed, q_cross))
    cross_keys = both_round(matmul(pixels, k_cross))
    cross_values = both_round(matmul(pixels, v_cross))
    crossed = attention(cross_queries, cross_keys, cross_values, key_valid)
    after_cross = triplane_rows + low_back(matmul(crossed, o_cross))
    normed = low(modulated_norm(after_cross, shifts[2], shifts[3]))
    self_queries = both_round(matmul(normed, q_self))
    self_keys = both_round(matmul(normed, k_self))
    self_values = both_round(matmul(normed, v_self))
    every_key = jnp.ones((triplane_rows.shape[0],), dtype=jnp.bool_)
    selfed = attention(self_queries, self_keys, self_values, every_key)
    after_self = after_cross + low_back(matmul(selfed, o_self))
    normed = low(modulated_norm(after_self, shifts[4], shifts[5]))
    hidden = low_back(matmul(normed, w_up))
    activated = low(jax.nn.gelu(hidden))
    return after_self + low_back(matmul(activated, w_down))

def soap_update(slot_grads, first_moment, second_moment, left_basis, right_basis, master_weights, slot_rates, slot_used):
    rotated = jnp.matmul(jnp.matmul(jnp.swapaxes(left_basis, 1, 2), slot_grads, precision=highest), right_basis, precision=highest)
    first_new = moment_decay * first_moment + (1.0 - moment_decay) * rotated
    second_new = moment_decay * second_moment + (1.0 - moment_decay) * rotated * rotated
    correction = 1.0 - moment_decay ** STEP
    normalized = first_new / correction / (jnp.sqrt(second_new / correction) + 1e-08)
    rotated_back = jnp.matmul(jnp.matmul(left_basis, normalized, precision=highest), jnp.swapaxes(right_basis, 1, 2), precision=highest)
    fresh_master = master_weights - slot_rates[:, None, None] * (rotated_back + 0.01 * master_weights)
    keep_mask = slot_used[:, None, None]
    fresh_master = fresh_master * keep_mask
    return (slot_grads * keep_mask, first_new * keep_mask, second_new * keep_mask, fresh_master, fresh_master.astype(jnp.bfloat16))

def reference(triplane, cotangent, image_tokens, modulation, image_counts, owner_slots, master_weights, first_moment, second_moment, left_basis, right_basis):
    params = split_blocks(low(master_weights[owner_slots]))
    triplane_rows = triplane.astype(jnp.float32).reshape(OBJ, 2 * TOK_DEV, D)
    pixels = image_tokens.astype(jnp.float32).reshape(N_ROWS, N_IMG, N_IMG // 2, CAP, DIMG)
    pixels = pixels.transpose(0, 2, 1, 3, 4).reshape(OBJ, N_IMG * CAP, DIMG)
    key_slot = jnp.arange(N_IMG * CAP, dtype=jnp.int32)
    token_index = key_slot % CAP * N_IMG + key_slot // CAP
    key_valid = token_index[None, :] < image_counts[:, None]

    def forward(layer_params, rows_all, pixels_all):

        def per_object(inputs):
            rows_in, pixel_rows, shifts, valid_rows = inputs
            return object_layer(layer_params, rows_in, pixel_rows, shifts, valid_rows)
        return lax.map(jax.checkpoint(per_object), (rows_all, pixels_all, modulation, key_valid))
    layer_out, pullback = jax.vjp(forward, params, triplane_rows, pixels)
    grad_params, grad_rows, grad_pixels = pullback(cotangent.astype(jnp.float32).reshape(OBJ, 2 * TOK_DEV, D))
    grad_image = grad_pixels.reshape(N_ROWS, N_IMG // 2, N_IMG, CAP, DIMG).transpose(0, 2, 1, 3, 4).reshape(IMG_ROWS, DIMG)
    slot_grads = jnp.zeros((SLOTS, BLOCK, BLOCK), jnp.float32).at[owner_slots].set(join_blocks(grad_params))
    slot_used = jnp.zeros((SLOTS,), jnp.float32).at[owner_slots].set(1.0)
    slot_rates = jnp.zeros((SLOTS,), jnp.float32).at[owner_slots].set(jnp.asarray(block_table(weight_scales())))
    updated = soap_update(slot_grads, first_moment, second_moment, left_basis, right_basis, master_weights, slot_rates, slot_used)
    return (layer_out.reshape(TRI_ROWS, D).astype(jnp.bfloat16), grad_rows.reshape(TRI_ROWS, D), grad_image, updated[0], updated[1], updated[2], updated[3], updated[4])
```

```python
import functools

import jax
import jax.numpy as jnp
import numpy as np
from jax import lax
from jax.experimental import pallas as pl
from jax.experimental.pallas import tpu as pltpu
from jax.sharding import PartitionSpec as P

D = 1024
HEADS = 16
FF = 4096
DIMG = 768
TOK_DEV = 384
IMG_MAX = 1025
BLOCK = 256
STEP = 5


MESH=pl.DeviceIdType.MESH
VLIM=60*1024*1024

def coords():
    r = lax.axis_index("rows"); y = lax.axis_index("img")
    z = lax.div(r, 4); rest = lax.rem(r, 4)
    return z, lax.div(rest, 2), lax.rem(rest, 2), y

def neighbour(kind):
    z, x, c, y = coords()
    if kind == "c": c = 1 - c
    if kind == "x": x = 1 - x
    if kind == "y": y = 1 - y
    if kind == "lo": z = z + 1 - 2 * lax.rem(z, 2)
    if kind == "hi": z = lax.rem(z + 2, 4)
    return (z * 4 + x * 2 + c, y)

def place(j):
    z, x, c, y = coords()
    lo = lax.rem(z, 2); hi = lax.div(z, 2)
    if j % 2 == 0: return ((x * 2 + lo) * 2 + y) * 2 + hi
    return ((y * 2 + lo) * 2 + x) * 2 + hi

WAYS = (("hi", "y", "lo", "x", "c"), ("hi", "x", "lo", "y", "c"))

def greet():
    bar = pltpu.get_barrier_semaphore()
    for kind in ("c", "x", "y", "lo", "hi"):
        pl.semaphore_signal(bar, inc=1, device_id=neighbour(kind), device_id_type=MESH)
    pl.semaphore_wait(bar, 5)

def gather_kernel(order, master, out, own, f32, lsem, csem, ssem, rsem):
    z, x, c, y = coords()
    load = pltpu.make_async_copy(master, f32, lsem)
    load.start()
    greet()
    load.wait()
    keeps = []
    copies = {}
    def start(j, k):
        base = place(j)
        if k < 4:
            n = 2 ** k
            first = lax.div(base, n) * n
        else:
            n, first = 16, 0
        src = own.at[pl.ds(j, 1)] if k == 0 else out.at[c, j, pl.ds(first, n)]
        cp = pltpu.make_async_remote_copy(src, out.at[c, j, pl.ds(first, n)], ssem.at[j, k], rsem.at[j, k],
              device_id=neighbour(WAYS[j % 2][k]), device_id_type=MESH)
        cp.start()
        copies[j, k] = cp
    for j in range(8):
        own[j] = f32[j].astype(jnp.bfloat16)
        start(j, 0)
        keep = pltpu.make_async_copy(own.at[pl.ds(j,1)], out.at[c, j, pl.ds(place(j), 1)], csem.at[j])
        keep.start(); keeps.append(keep)
    for keep in keeps: keep.wait()
    for j, k in order:
        copies[j, k - 1].wait_recv()
        start(j, k)
    for j in range(8): copies[j, 4].wait_recv()
    for cp in copies.values(): cp.wait_send()

def gather(master, order, cid=11):
    return pl.pallas_call(functools.partial(gather_kernel, order),
        out_shape=jax.ShapeDtypeStruct((2, 8, 16, BLOCK, BLOCK), jnp.bfloat16),
        in_specs=[pl.BlockSpec(memory_space=pl.ANY)], out_specs=pl.BlockSpec(memory_space=pl.ANY),
        scratch_shapes=[pltpu.VMEM((8, BLOCK, BLOCK), jnp.bfloat16), pltpu.VMEM((8, BLOCK, BLOCK), jnp.float32),
            pltpu.SemaphoreType.DMA, pltpu.SemaphoreType.DMA((8,)), pltpu.SemaphoreType.DMA((8, 5)), pltpu.SemaphoreType.DMA((8, 5))],
        compiler_params=pltpu.CompilerParams(collective_id=cid, has_side_effects=True, vmem_limit_bytes=VLIM))(master)

def scatter_kernel(order, grads, out, own, r0, r1, r2, r3, r4, lsem, ssem, rsem):
    z, x, c, y = coords()
    got = (r0, r1, r2, r3, r4)
    loads = []
    for j in range(8):
        load = pltpu.make_async_copy(grads.at[c, j], own.at[j], lsem.at[j])
        load.start(); loads.append(load)
    greet()
    copies = {}
    for j in range(8):
        cp = pltpu.make_async_remote_copy(grads.at[1 - c, j], r0.at[j], ssem.at[j, 0], rsem.at[j, 0],
              device_id=neighbour("c"), device_id_type=MESH)
        cp.start(); copies[j, 0] = cp
    def add(j, s):
        n = 16 >> s
        first = lax.div(place(j), n) * n if s else 0
        def body(b, carry):
            own[j, first + b] = (own[j, first + b].astype(jnp.float32) + got[s][j, b].astype(jnp.float32)).astype(jnp.bfloat16)
            return carry
        lax.fori_loop(0, n, body, 0)
    def send(j, s):
        n = 16 >> s
        base = place(j)
        half = lax.div(base, n)
        other = (half + 1 - 2 * lax.rem(half, 2)) * n
        cp = pltpu.make_async_remote_copy(own.at[j, pl.ds(other, n)], got[s].at[j], ssem.at[j, s], rsem.at[j, s],
              device_id=neighbour(WAYS[j % 2][4 - s]), device_id_type=MESH)
        cp.start(); copies[j, s] = cp
    for j, s in order:
        if s == 1: loads[j].wait()
        copies[j, s - 1].wait_recv()
        add(j, s - 1)
        if s < 5: send(j, s)
        else: out[j] = own[j, place(j)].astype(jnp.float32)
    for cp in copies.values(): cp.wait_send()

def scatter(grads, order, cid=12):
    bf = jnp.bfloat16
    return pl.pallas_call(functools.partial(scatter_kernel, order),
        out_shape=jax.ShapeDtypeStruct((8, BLOCK, BLOCK), jnp.float32),
        in_specs=[pl.BlockSpec(memory_space=pl.ANY)], out_specs=pl.BlockSpec(memory_space=pltpu.VMEM),
        scratch_shapes=[pltpu.VMEM((8, 16, BLOCK, BLOCK), bf), pltpu.VMEM((8, 16, BLOCK, BLOCK), bf), pltpu.VMEM((8, 8, BLOCK, BLOCK), bf),
            pltpu.VMEM((8, 4, BLOCK, BLOCK), bf), pltpu.VMEM((8, 2, BLOCK, BLOCK), bf), pltpu.VMEM((8, 1, BLOCK, BLOCK), bf),
            pltpu.SemaphoreType.DMA((8,)), pltpu.SemaphoreType.DMA((8, 5)), pltpu.SemaphoreType.DMA((8, 5))],
        compiler_params=pltpu.CompilerParams(collective_id=cid, has_side_effects=True, vmem_limit_bytes=VLIM))(grads)

WAVE_OUT = sorted(
    [(j, k) for k in range(1, 5) for j in range(8)], key=lambda t: (t[0] // 2 + t[1], t[1], t[0])
)
WAVE_IN = sorted(
    [(j, k) for k in range(1, 6) for j in range(8)], key=lambda t: (t[0] // 2 + t[1], t[1], t[0])
)


def positions(slot):
    owner = slot // 8; j = slot % 8
    z = owner // 8; x = owner // 4 % 2; c = owner // 2 % 2; y = owner % 2
    lo = z % 2; hi = z // 2
    a = ((x * 2 + lo) * 2 + y) * 2 + hi
    b = ((y * 2 + lo) * 2 + x) * 2 + hi
    return (c * 8 + j) * 16 + jnp.where(j % 2 == 0, a, b)


highest = lax.Precision.HIGHEST
moment_decay = 0.5


def partner(block, axis, apart):
    count = lax.axis_size(axis)
    route = []
    for low in range(count):
        high = low | 1 << apart
        if high != low and high < count:
            route += [(low, high), (high, low)]
    return lax.ppermute(block, axis, route)


def shapes_list():
    return [(D, D), (DIMG, D), (DIMG, D), (D, D), (D, D), (D, D), (D, D), (D, D), (D, FF), (FF, D)]


def weight_scales():
    self_root = (2.0 * TOK_DEV) ** 0.5
    cross_root = (IMG_MAX / 2.0) ** 0.5
    return [
        D ** (-0.5),
        DIMG ** (-0.5),
        DIMG ** (-0.5),
        0.5 * cross_root * D ** (-0.5),
        D ** (-0.5),
        D ** (-0.5),
        D ** (-0.5),
        0.5 * self_root * D ** (-0.5),
        D ** (-0.5),
        2.0 * FF ** (-0.5),
    ]


def block_table(scales):
    pieces = []
    for shape_pair, scale_value in zip(shapes_list(), scales):
        amount = shape_pair[0] * shape_pair[1] // (BLOCK * BLOCK)
        pieces.append(np.full((amount,), scale_value, np.float32))
    return np.concatenate(pieces)


def split_blocks(blocks):
    matrices = []
    begin_at = 0
    for rows_in, cols_out in shapes_list():
        amount = rows_in * cols_out // (BLOCK * BLOCK)
        grid = blocks[begin_at : begin_at + amount].reshape(
            rows_in // BLOCK, cols_out // BLOCK, BLOCK, BLOCK
        )
        matrices.append(grid.transpose(0, 2, 1, 3).reshape(rows_in, cols_out))
        begin_at = begin_at + amount
    return matrices


def join_blocks(matrices):
    pieces = []
    for matrix in matrices:
        rows_in, cols_out = matrix.shape
        grid = matrix.reshape(rows_in // BLOCK, BLOCK, cols_out // BLOCK, BLOCK).transpose(
            0, 2, 1, 3
        )
        pieces.append(grid.reshape(-1, BLOCK, BLOCK))
    return jnp.concatenate(pieces, 0)


def modulated_norm(values, shift, scale):
    centered = values - jnp.mean(values, axis=-1, keepdims=True)
    variance = jnp.mean(centered * centered, axis=-1, keepdims=True)
    return centered * lax.rsqrt(variance + 1e-06) * (1.0 + scale) + shift


def norm_back(values, shift, scale, grad_normed):
    unused_out, pullback = jax.vjp(lambda inner: modulated_norm(inner, shift, scale), values)
    return pullback(grad_normed)[0]


def project(left, right):
    return jnp.dot(left, right, preferred_element_type=jnp.float32)


def heads_view(matrix):
    return matrix.reshape(matrix.shape[0], HEADS, D // HEADS).transpose(1, 0, 2)


def merge_heads(stacked):
    return stacked.transpose(1, 0, 2).reshape(stacked.shape[1], D)


def attend(queries, key_rows, value_rows, key_valid):
    scale_factor = (D // HEADS) ** (-0.5)

    def per_head(operands):
        head_query, head_key, head_value = operands
        scores = project(head_query, head_key.T) * scale_factor
        scores = jnp.where(key_valid[None, :], scores, -1e30)
        row_max = jnp.max(scores, axis=-1, keepdims=True)
        exponent = jnp.exp(scores - row_max)
        row_total = jnp.sum(exponent, axis=-1, keepdims=True)
        weights_low = (exponent / row_total).astype(jnp.bfloat16)
        mixed_out = project(weights_low, head_value)
        return (mixed_out, (row_max + jnp.log(row_total))[:, 0])

    mixed_out, log_total = lax.map(
        per_head, (heads_view(queries), heads_view(key_rows), heads_view(value_rows))
    )
    return (merge_heads(mixed_out).astype(jnp.bfloat16), log_total)


def attend_back(queries, key_rows, value_rows, key_valid, log_total, grad_mixed):
    scale_factor = (D // HEADS) ** (-0.5)

    def per_head(operands):
        head_query, head_key, head_value, head_total, head_grad = operands
        scores = project(head_query, head_key.T) * scale_factor
        scores = jnp.where(key_valid[None, :], scores, -1e30)
        weights_full = jnp.exp(scores - head_total[:, None])
        grad_weights = project(head_grad, head_value.T)
        inner_sum = jnp.sum(weights_full * grad_weights, axis=-1, keepdims=True)
        grad_scores = (weights_full * (grad_weights - inner_sum)).astype(jnp.bfloat16)
        grad_query = project(grad_scores, head_key) * scale_factor
        grad_key = project(grad_scores.T, head_query) * scale_factor
        grad_value = project(weights_full.astype(jnp.bfloat16).T, head_grad)
        return (grad_query, grad_key, grad_value)

    grad_query, grad_key, grad_value = lax.map(
        per_head,
        (
            heads_view(queries),
            heads_view(key_rows),
            heads_view(value_rows),
            log_total,
            heads_view(grad_mixed),
        ),
    )
    return (merge_heads(grad_query), merge_heads(grad_key), merge_heads(grad_value))


def soap_update(
    slot_grads,
    first_moment,
    second_moment,
    left_basis,
    right_basis,
    master_weights,
    slot_rates,
    slot_used,
):
    rotated = jnp.matmul(
        jnp.matmul(jnp.swapaxes(left_basis, 1, 2), slot_grads, precision=highest),
        right_basis,
        precision=highest,
    )
    first_new = moment_decay * first_moment + (1.0 - moment_decay) * rotated
    second_new = moment_decay * second_moment + (1.0 - moment_decay) * rotated * rotated
    correction = 1.0 - moment_decay**STEP
    normalized = first_new / correction / (jnp.sqrt(second_new / correction) + 1e-08)
    rotated_back = jnp.matmul(
        jnp.matmul(left_basis, normalized, precision=highest),
        jnp.swapaxes(right_basis, 1, 2),
        precision=highest,
    )
    fresh_master = master_weights - slot_rates[:, None, None] * (
        rotated_back + 0.01 * master_weights
    )
    keep_mask = slot_used[:, None, None]
    fresh_master = fresh_master * keep_mask
    return (
        slot_grads * keep_mask,
        first_new * keep_mask,
        second_new * keep_mask,
        fresh_master,
        fresh_master.astype(jnp.bfloat16),
    )


def shards(
    triplane,
    cotangent,
    image_tokens,
    modulation,
    image_counts,
    owner_slots,
    master_weights,
    first_moment,
    second_moment,
    left_basis,
    right_basis,
):
    img_size = lax.axis_size("img")
    rows_size = lax.axis_size("rows")
    flat_index = lax.axis_index("rows") * img_size + lax.axis_index("img")
    object_index = flat_index // 2
    pair_index = lax.axis_index("img") // 2
    tok_rows = triplane.shape[0]
    slot_cap = image_tokens.shape[0] // (img_size // 2)
    own_count = master_weights.shape[0]
    fits = rows_size == 16 and img_size == 2 and own_count == 8
    if fits:
        gathered_weights = gather(master_weights, WAVE_OUT).reshape(-1, BLOCK, BLOCK)
        where = positions(owner_slots)
    else:
        gathered_weights = lax.all_gather(
            master_weights.astype(jnp.bfloat16), ("rows", "img"), axis=0, tiled=True
        )
        where = owner_slots
    q_cross, k_cross, v_cross, o_cross, q_self, k_self, v_self, o_self, w_up, w_down = split_blocks(
        gathered_weights[where]
    )
    shifts = lax.dynamic_index_in_dim(modulation, object_index, 0, keepdims=False)
    count_here = lax.dynamic_index_in_dim(image_counts, object_index, 0, keepdims=False)
    kv_weight = jnp.concatenate([k_cross, v_cross], 1)
    kv_local = project(image_tokens, kv_weight).astype(jnp.bfloat16)
    gathered = lax.all_gather(kv_local, "img", axis=0, tiled=True).reshape(
        img_size, img_size // 2, slot_cap, 2 * D
    )
    kv_object = lax.dynamic_index_in_dim(gathered, pair_index, 1, keepdims=False)
    kv_object = kv_object.reshape(img_size * slot_cap, 2 * D)
    key_slot = jnp.arange(img_size * slot_cap, dtype=jnp.int32)
    token_index = key_slot % slot_cap * img_size + key_slot // slot_cap
    key_valid = token_index < count_here
    residual = triplane.astype(jnp.float32)
    normed_one = modulated_norm(residual, shifts[0], shifts[1]).astype(jnp.bfloat16)
    cross_queries = project(normed_one, q_cross).astype(jnp.bfloat16)
    cross_out, cross_logsum = attend(cross_queries, kv_object[:, :D], kv_object[:, D:], key_valid)
    after_cross = residual + project(cross_out, o_cross)
    normed_two = modulated_norm(after_cross, shifts[2], shifts[3]).astype(jnp.bfloat16)
    qkv_weight = jnp.concatenate([q_self, k_self, v_self], 1)
    self_proj = project(normed_two, qkv_weight).astype(jnp.bfloat16)
    kv_mine = self_proj[:, D:]
    kv_partner = partner(kv_mine, "img", 0)
    kv_all = jnp.concatenate([kv_mine, kv_partner], 0)
    all_valid = jnp.ones((2 * tok_rows,), dtype=jnp.bool_)
    self_out, self_logsum = attend(self_proj[:, :D], kv_all[:, :D], kv_all[:, D:], all_valid)
    after_self = after_cross + project(self_out, o_self)
    normed_three = modulated_norm(after_self, shifts[4], shifts[5]).astype(jnp.bfloat16)
    hidden = project(normed_three, w_up)
    activated = jax.nn.gelu(hidden).astype(jnp.bfloat16)
    result = (after_self + project(activated, w_down)).astype(jnp.bfloat16)
    grad_out = cotangent.astype(jnp.float32)
    grad_low = grad_out.astype(jnp.bfloat16)
    grad_down = project(activated.T, grad_low)
    grad_act = project(grad_low, w_down.T)
    unused_act, gelu_back = jax.vjp(jax.nn.gelu, hidden)
    grad_hidden = gelu_back(grad_act)[0].astype(jnp.bfloat16)
    grad_up = project(normed_three.T, grad_hidden)
    grad_after_self = grad_out + norm_back(
        after_self, shifts[4], shifts[5], project(grad_hidden, w_up.T)
    )
    grad_self_branch = grad_after_self.astype(jnp.bfloat16)
    grad_o_self = project(self_out.T, grad_self_branch)
    grad_self_out = project(grad_self_branch, o_self.T).astype(jnp.bfloat16)
    grad_sq, grad_sk, grad_sv = attend_back(
        self_proj[:, :D], kv_all[:, :D], kv_all[:, D:], all_valid, self_logsum, grad_self_out
    )
    grad_kv_rows = jnp.concatenate([grad_sk, grad_sv], 1)
    grad_kv_mine = grad_kv_rows[:tok_rows] + partner(
        grad_kv_rows[tok_rows:].astype(jnp.bfloat16), "img", 0
    ).astype(jnp.float32)
    grad_qkv = jnp.concatenate([grad_sq, grad_kv_mine], 1).astype(jnp.bfloat16)
    grad_qkv_weight = project(normed_two.T, grad_qkv)
    grad_after_cross = grad_after_self + norm_back(
        after_cross, shifts[2], shifts[3], project(grad_qkv, qkv_weight.T)
    )
    grad_cross_branch = grad_after_cross.astype(jnp.bfloat16)
    grad_o_cross = project(cross_out.T, grad_cross_branch)
    grad_cross_out = project(grad_cross_branch, o_cross.T).astype(jnp.bfloat16)
    grad_cq, grad_ck, grad_cv = attend_back(
        cross_queries, kv_object[:, :D], kv_object[:, D:], key_valid, cross_logsum, grad_cross_out
    )
    grad_object = jnp.concatenate([grad_ck, grad_cv], 1)
    pick_pair = (jnp.arange(img_size // 2, dtype=jnp.int32) == pair_index).astype(jnp.float32)
    spread = grad_object.reshape(img_size, 1, slot_cap, 2 * D) * pick_pair[None, :, None, None]
    grad_kv_local = lax.psum_scatter(
        spread.reshape(img_size * (img_size // 2) * slot_cap, 2 * D).astype(jnp.bfloat16),
        "img",
        scatter_dimension=0,
        tiled=True,
    )
    grad_kv_weight = project(image_tokens.T, grad_kv_local)
    grad_image = project(grad_kv_local, kv_weight.T)
    grad_cq_low = grad_cq.astype(jnp.bfloat16)
    grad_q_cross = project(normed_one.T, grad_cq_low)
    grad_triplane = grad_after_cross + norm_back(
        residual, shifts[0], shifts[1], project(grad_cq_low, q_cross.T)
    )
    weight_list = [
        grad_q_cross,
        grad_kv_weight[:, :D],
        grad_kv_weight[:, D:],
        grad_o_cross,
        grad_qkv_weight[:, :D],
        grad_qkv_weight[:, D : 2 * D],
        grad_qkv_weight[:, 2 * D :],
        grad_o_self,
        grad_up,
        grad_down,
    ]
    slot_total = rows_size * img_size * own_count
    block_grads = join_blocks([part.astype(jnp.bfloat16) for part in weight_list])
    placed = jnp.zeros((slot_total, BLOCK, BLOCK), jnp.bfloat16).at[where].set(block_grads)
    if fits:
        slot_grads = scatter(placed.reshape(2, 8, 16, BLOCK, BLOCK), WAVE_IN)
    else:
        slot_grads = lax.psum_scatter(
            placed, ("rows", "img"), scatter_dimension=0, tiled=True
        ).astype(jnp.float32)
    my_slots = flat_index * own_count + jnp.arange(own_count, dtype=jnp.int32)
    matched = (owner_slots[:, None] == my_slots[None, :]).astype(jnp.float32)
    slot_used = jnp.sum(matched, axis=0)
    slot_rates = jnp.sum(matched * jnp.asarray(block_table(weight_scales()))[:, None], axis=0)
    updated = soap_update(
        slot_grads,
        first_moment,
        second_moment,
        left_basis,
        right_basis,
        master_weights,
        slot_rates,
        slot_used,
    )
    return (
        result,
        grad_triplane,
        grad_image,
        updated[0],
        updated[1],
        updated[2],
        updated[3],
        updated[4],
    )


def solution(mesh):
    in_specs = (
        P(("rows", "img"), None),
        P(("rows", "img"), None),
        P(("rows", "img"), None),
        P(),
        P(),
        P(),
        P(("rows", "img"), None, None),
        P(("rows", "img"), None, None),
        P(("rows", "img"), None, None),
        P(("rows", "img"), None, None),
        P(("rows", "img"), None, None),
    )
    out_specs = (
        P(("rows", "img"), None),
        P(("rows", "img"), None),
        P(("rows", "img"), None),
        P(("rows", "img"), None, None),
        P(("rows", "img"), None, None),
        P(("rows", "img"), None, None),
        P(("rows", "img"), None, None),
        P(("rows", "img"), None, None),
    )
    return jax.shard_map(shards, mesh=mesh, in_specs=in_specs, out_specs=out_specs, check_vma=False)
```

```python
import functools

import jax
import jax.numpy as jnp
import numpy as np
from jax import lax
from jax.experimental import pallas as pl
from jax.experimental.pallas import tpu as pltpu
from jax.sharding import PartitionSpec as P

D = 1024
HEADS = 16
FF = 4096
DIMG = 768
TOK_DEV = 384
IMG_MAX = 1025
BLOCK = 256
STEP = 5
HEAD = D // HEADS

MESH=pl.DeviceIdType.MESH
VLIM=60*1024*1024

def coords():
    r = lax.axis_index("rows"); y = lax.axis_index("img")
    z = lax.div(r, 4); rest = lax.rem(r, 4)
    return z, lax.div(rest, 2), lax.rem(rest, 2), y

def neighbour(kind):
    z, x, c, y = coords()
    if kind == "c": c = 1 - c
    if kind == "x": x = 1 - x
    if kind == "y": y = 1 - y
    if kind == "lo": z = z + 1 - 2 * lax.rem(z, 2)
    if kind == "hi": z = lax.rem(z + 2, 4)
    return (z * 4 + x * 2 + c, y)

def place(j):
    z, x, c, y = coords()
    lo = lax.rem(z, 2); hi = lax.div(z, 2)
    if j % 2 == 0: return ((x * 2 + lo) * 2 + y) * 2 + hi
    return ((y * 2 + lo) * 2 + x) * 2 + hi

WAYS = (("hi", "y", "lo", "x", "c"), ("hi", "x", "lo", "y", "c"))

def greet():
    bar = pltpu.get_barrier_semaphore()
    for kind in ("c", "x", "y", "lo", "hi"):
        pl.semaphore_signal(bar, inc=1, device_id=neighbour(kind), device_id_type=MESH)
    pl.semaphore_wait(bar, 5)

def gather_kernel(order, master, out, own, f32, lsem, csem, ssem, rsem):
    z, x, c, y = coords()
    load = pltpu.make_async_copy(master, f32, lsem)
    load.start()
    greet()
    load.wait()
    keeps = []
    copies = {}
    def start(j, k):
        base = place(j)
        if k < 4:
            n = 2 ** k
            first = lax.div(base, n) * n
        else:
            n, first = 16, 0
        src = own.at[pl.ds(j, 1)] if k == 0 else out.at[c, j, pl.ds(first, n)]
        cp = pltpu.make_async_remote_copy(src, out.at[c, j, pl.ds(first, n)], ssem.at[j, k], rsem.at[j, k],
              device_id=neighbour(WAYS[j % 2][k]), device_id_type=MESH)
        cp.start()
        copies[j, k] = cp
    for j in range(8):
        own[j] = f32[j].astype(jnp.bfloat16)
        start(j, 0)
        keep = pltpu.make_async_copy(own.at[pl.ds(j,1)], out.at[c, j, pl.ds(place(j), 1)], csem.at[j])
        keep.start(); keeps.append(keep)
    for keep in keeps: keep.wait()
    for j, k in order:
        copies[j, k - 1].wait_recv()
        start(j, k)
    for j in range(8): copies[j, 4].wait_recv()
    for cp in copies.values(): cp.wait_send()

def gather(master, order, cid=11):
    return pl.pallas_call(functools.partial(gather_kernel, order),
        out_shape=jax.ShapeDtypeStruct((2, 8, 16, BLOCK, BLOCK), jnp.bfloat16),
        in_specs=[pl.BlockSpec(memory_space=pl.ANY)], out_specs=pl.BlockSpec(memory_space=pl.ANY),
        scratch_shapes=[pltpu.VMEM((8, BLOCK, BLOCK), jnp.bfloat16), pltpu.VMEM((8, BLOCK, BLOCK), jnp.float32),
            pltpu.SemaphoreType.DMA, pltpu.SemaphoreType.DMA((8,)), pltpu.SemaphoreType.DMA((8, 5)), pltpu.SemaphoreType.DMA((8, 5))],
        compiler_params=pltpu.CompilerParams(collective_id=cid, has_side_effects=True, vmem_limit_bytes=VLIM))(master)

def scatter_kernel(order, grads, out, own, r0, r1, r2, r3, r4, lsem, ssem, rsem):
    z, x, c, y = coords()
    got = (r0, r1, r2, r3, r4)
    loads = []
    for j in range(8):
        load = pltpu.make_async_copy(grads.at[c, j], own.at[j], lsem.at[j])
        load.start(); loads.append(load)
    greet()
    copies = {}
    for j in range(8):
        cp = pltpu.make_async_remote_copy(grads.at[1 - c, j], r0.at[j], ssem.at[j, 0], rsem.at[j, 0],
              device_id=neighbour("c"), device_id_type=MESH)
        cp.start(); copies[j, 0] = cp
    def add(j, s):
        n = 16 >> s
        first = lax.div(place(j), n) * n if s else 0
        def body(b, carry):
            own[j, first + b] = (own[j, first + b].astype(jnp.float32) + got[s][j, b].astype(jnp.float32)).astype(jnp.bfloat16)
            return carry
        lax.fori_loop(0, n, body, 0)
    def send(j, s):
        n = 16 >> s
        base = place(j)
        half = lax.div(base, n)
        other = (half + 1 - 2 * lax.rem(half, 2)) * n
        cp = pltpu.make_async_remote_copy(own.at[j, pl.ds(other, n)], got[s].at[j], ssem.at[j, s], rsem.at[j, s],
              device_id=neighbour(WAYS[j % 2][4 - s]), device_id_type=MESH)
        cp.start(); copies[j, s] = cp
    for j, s in order:
        if s == 1: loads[j].wait()
        copies[j, s - 1].wait_recv()
        add(j, s - 1)
        if s < 5: send(j, s)
        else: out[j] = own[j, place(j)].astype(jnp.float32)
    for cp in copies.values(): cp.wait_send()

def scatter(grads, order, cid=12):
    bf = jnp.bfloat16
    return pl.pallas_call(functools.partial(scatter_kernel, order),
        out_shape=jax.ShapeDtypeStruct((8, BLOCK, BLOCK), jnp.float32),
        in_specs=[pl.BlockSpec(memory_space=pl.ANY)], out_specs=pl.BlockSpec(memory_space=pltpu.VMEM),
        scratch_shapes=[pltpu.VMEM((8, 16, BLOCK, BLOCK), bf), pltpu.VMEM((8, 16, BLOCK, BLOCK), bf), pltpu.VMEM((8, 8, BLOCK, BLOCK), bf),
            pltpu.VMEM((8, 4, BLOCK, BLOCK), bf), pltpu.VMEM((8, 2, BLOCK, BLOCK), bf), pltpu.VMEM((8, 1, BLOCK, BLOCK), bf),
            pltpu.SemaphoreType.DMA((8,)), pltpu.SemaphoreType.DMA((8, 5)), pltpu.SemaphoreType.DMA((8, 5))],
        compiler_params=pltpu.CompilerParams(collective_id=cid, has_side_effects=True, vmem_limit_bytes=VLIM))(grads)

def positions(slot):
    owner = slot // 8; j = slot % 8
    z = owner // 8; x = owner // 4 % 2; c = owner // 2 % 2; y = owner % 2
    lo = z % 2; hi = z // 2
    a = ((x * 2 + lo) * 2 + y) * 2 + hi
    b = ((y * 2 + lo) * 2 + x) * 2 + hi
    return (c * 8 + j) * 16 + jnp.where(j % 2 == 0, a, b)


highest = lax.Precision.HIGHEST
moment_decay = 0.5
LOW = jnp.bfloat16
WIDE = jnp.float32

WAVE_OUT = sorted(
    [(j, k) for k in range(1, 5) for j in range(8)], key=lambda t: (t[0] // 2 + t[1], t[1], t[0])
)
WAVE_IN = sorted(
    [(j, k) for k in range(1, 6) for j in range(8)], key=lambda t: (t[0] // 2 + t[1], t[1], t[0])
)


def shapes_list():
    return [(D, D), (DIMG, D), (DIMG, D), (D, D), (D, D), (D, D), (D, D), (D, D), (D, FF), (FF, D)]


Q_CROSS, K_CROSS, V_CROSS, O_CROSS, Q_SELF, K_SELF, V_SELF, O_SELF, W_UP, W_DOWN = (
    int(v) for v in np.cumsum([0] + [a * b // BLOCK**2 for a, b in shapes_list()])[:10]
)


def weight_scales():
    self_root = (2.0 * TOK_DEV) ** 0.5
    cross_root = (IMG_MAX / 2.0) ** 0.5
    return [
        D ** (-0.5),
        DIMG ** (-0.5),
        DIMG ** (-0.5),
        0.5 * cross_root * D ** (-0.5),
        D ** (-0.5),
        D ** (-0.5),
        D ** (-0.5),
        0.5 * self_root * D ** (-0.5),
        D ** (-0.5),
        2.0 * FF ** (-0.5),
    ]


def block_table(scales):
    pieces = []
    for shape_pair, scale_value in zip(shapes_list(), scales):
        amount = shape_pair[0] * shape_pair[1] // (BLOCK * BLOCK)
        pieces.append(np.full((amount,), scale_value, np.float32))
    return np.concatenate(pieces)


def low(v):
    return v.astype(LOW)


def dot(a, b):
    return jnp.dot(a, b, preferred_element_type=WIDE)


def dot_nt(a, b):
    return lax.dot_general(a, b, (((1,), (1,)), ((), ())), preferred_element_type=WIDE)


def part(k):
    return slice(k * BLOCK, (k + 1) * BLOCK)


def norm_parts(values):
    centered = values - jnp.mean(values, axis=-1, keepdims=True)
    variance = jnp.mean(centered * centered, axis=-1, keepdims=True)
    return centered, lax.rsqrt(variance + 1e-06)


def modulated_norm(values, shift, scale):
    centered, inverse = norm_parts(values)
    return centered * inverse * (1.0 + scale) + shift


def norm_back(values, scale, grad_normed):
    centered, inverse = norm_parts(values)
    unit = centered * inverse
    grad_unit = grad_normed * (1.0 + scale)
    return inverse * (
        grad_unit
        - jnp.mean(grad_unit, axis=-1, keepdims=True)
        - unit * jnp.mean(grad_unit * unit, axis=-1, keepdims=True)
    )


def halves(pair):
    lane = lax.broadcasted_iota(jnp.int32, pair.shape, 1)
    zero = jnp.zeros_like(pair)
    return jnp.where(lane < HEAD, pair, zero), jnp.where(lane < HEAD, zero, pair)


def masked(scores, valid):
    if valid is None:
        return scores
    wide = jnp.concatenate([valid] * (scores.shape[1] // valid.shape[1]), axis=1)
    return jnp.where(wide > 0.0, scores, -1e30)


def columns(base, tall, wide):
    return [
        pl.BlockSpec((1, BLOCK, BLOCK), lambda n, where, i=i: (where[base + i * wide + n], 0, 0))
        for i in range(tall)
    ]


def rows(base, wide):
    return [
        pl.BlockSpec((1, BLOCK, BLOCK), lambda n, where, k=k: (where[base + n * wide + k], 0, 0))
        for k in range(wide)
    ]


def whole(shape):
    return pl.BlockSpec(shape, lambda n, where: (0,) * len(shape))


def stripe(height):
    return pl.BlockSpec((height, BLOCK), lambda n, where: (0, n))


def by_columns(left, blocks):
    total = dot(left[:, part(0)], blocks[0][0])
    for i in range(1, len(blocks)):
        total = total + dot(left[:, part(i)], blocks[i][0])
    return total


def by_rows(left, blocks):
    total = dot_nt(left[:, part(0)], blocks[0][0])
    for i in range(1, len(blocks)):
        total = total + dot_nt(left[:, part(i)], blocks[i][0])
    return total


def attend(queries, keys, values_turned, weights, valid, count):
    outs, logs = [], []
    for pair in range(2):
        lanes = slice(pair * 2 * HEAD, (pair + 1) * 2 * HEAD)
        key_pair = keys[:count, lanes]
        for which, query in enumerate(halves(queries[:, lanes])):
            head = pair * 2 + which
            scores = masked(dot_nt(key_pair, query), valid)
            top = jnp.max(scores, axis=0, keepdims=True)
            exponent = jnp.exp(scores - top)
            total = jnp.sum(exponent, axis=0, keepdims=True)
            weights[:count] = low(exponent)
            mixed = dot(values_turned[head * HEAD : (head + 1) * HEAD], weights[...])
            outs.append(mixed / total)
            logs.append(top + jnp.log(total))
    turned = jnp.concatenate(outs, axis=0)
    return low(turned.T), jnp.concatenate(logs + logs, axis=0)


def attend_back(queries, keys, values, keys_turned, mixed, grad_mixed, logs, probs, grads, valid, count):
    tokens = queries.shape[0]
    inner = (mixed.astype(WIDE) * grad_mixed.astype(WIDE)).T
    grad_query, grad_key, grad_value = [], [], []
    for pair in range(2):
        lanes = slice(pair * 2 * HEAD, (pair + 1) * 2 * HEAD)
        key_pair, value_pair = keys[:count, lanes], values[:count, lanes]
        query_halves = halves(queries[:, lanes])
        mixed_halves = halves(grad_mixed[:, lanes])
        for which in range(2):
            head = pair * 2 + which
            own = slice(head * HEAD, (head + 1) * HEAD)
            side = slice(which * tokens, (which + 1) * tokens)
            scores = masked(dot_nt(key_pair, query_halves[which]), valid)
            full = jnp.exp(scores - logs[head : head + 1])
            grad_full = dot_nt(value_pair, mixed_halves[which])
            back = low(full * (grad_full - jnp.sum(inner[own], axis=0, keepdims=True)))
            probs[:count, side] = low(full)
            grads[:count, side] = back
            grad_query.append(dot(keys_turned[own], grads[:, side]))
        grad_key.append(dot(grads[:count], jnp.concatenate(query_halves, axis=0)))
        grad_value.append(dot(probs[:count], jnp.concatenate(mixed_halves, axis=0)))
    grad_query = jnp.concatenate(grad_query, axis=0).T * HEAD ** (-0.5)
    return grad_query, jnp.concatenate(grad_key, axis=1), jnp.concatenate(grad_value, axis=1)


def send_blocks(stage, sems, store, where, numbers):
    return [
        pltpu.make_async_copy(stage.at[i], store.at[where[number]], sems.at[i])
        for i, number in enumerate(numbers)
    ]


def cross_forward_kernel(count, where, x, tokens, shifts, valid, *rest):
    q, k, v, o = rest[:4], rest[4:7], rest[7:10], rest[10:14]
    normed_turned, cq, ck, cv, co, logs, x1, n2, normed, total, turned, weights = rest[14:]
    n = pl.program_id(0)

    @pl.when(n == 0)
    def first():
        one = low(modulated_norm(x[...].astype(WIDE), shifts[0:1], shifts[1:2]))
        normed[...] = one
        normed_turned[...] = one.T
        total[...] = x[...].astype(WIDE)
        turned[...] = jnp.zeros_like(turned)
        weights[...] = jnp.zeros_like(weights)

    queries = low(by_columns(normed, q)) * HEAD ** (-0.5)
    cq[...] = queries
    ck[...] = low(by_columns(tokens, k))
    cv[...] = low(by_columns(tokens, v))
    turned[:count] = cv[...]
    mixed, log_total = attend(queries, ck, turned[...].T, weights, valid[...], count)
    co[...] = mixed
    logs[0] = log_total
    for i in range(4):
        total[:, part(i)] += dot(mixed, o[i][0])

    @pl.when(n == 3)
    def last():
        after = total[...]
        x1[...] = after
        n2[...] = low(modulated_norm(after, shifts[2:3], shifts[3:4]))


def self_forward_kernel(x1, mine, other, shifts, *rest):
    q, k, v, o = rest[:4], rest[4:8], rest[8:12], rest[12:16]
    normed_turned, sq, sk, sv, so, logs, x2, n3, total, weights = rest[16:]
    n = pl.program_id(0)
    rows_here = x1.shape[0]

    @pl.when(n == 0)
    def first():
        normed_turned[:, :rows_here] = mine[...].T
        normed_turned[:, rows_here:] = other[...].T
        total[...] = x1[...]

    queries = low(by_columns(mine, q)) * HEAD ** (-0.5)
    sq[...] = queries
    sk[:rows_here] = low(by_columns(mine, k))
    sk[rows_here:] = low(by_columns(other, k))
    sv[:rows_here] = low(by_columns(mine, v))
    sv[rows_here:] = low(by_columns(other, v))
    mixed, log_total = attend(queries, sk, sv[...].T, weights, None, 2 * rows_here)
    so[...] = mixed
    logs[0] = log_total
    for i in range(4):
        total[:, part(i)] += dot(mixed, o[i][0])

    @pl.when(n == 3)
    def last():
        after = total[...]
        x2[...] = after
        n3[...] = low(modulated_norm(after, shifts[4:5], shifts[5:6]))


def feed_kernel(where, x2, n3, cotangent, shifts, *rest):
    up, down = rest[:4], rest[4:8]
    layer_out, g2, store, total, back, turned, stage, sems = rest[8:]
    f = pl.program_id(0)
    steps = FF // BLOCK

    @pl.when(f == 0)
    def first():
        total[...] = x2[...]
        back[...] = jnp.zeros_like(back)
        turned[...] = n3[...].T

    hidden = by_columns(n3, up)
    grad_act = by_rows(cotangent, down)
    square = hidden * hidden
    root = (2.0 / np.pi) ** 0.5
    bent = jnp.tanh(root * (hidden + 0.044715 * (square * hidden)))
    act = low(0.5 * hidden * (1.0 + bent))
    slope = 0.5 * (1.0 + bent) + 0.5 * hidden * (1.0 - bent * bent) * (
        root * (1.0 + 3.0 * 0.044715 * square)
    )
    eh = low(grad_act * slope)
    act_turned = act.T
    for i in range(4):
        total[:, part(i)] += dot(act, down[i][0])
        back[:, part(i)] += dot_nt(eh, up[i][0])

    numbers = [W_UP + i * steps + f for i in range(4)] + [W_DOWN + f * 4 + i for i in range(4)]

    @pl.when(f > 0)
    def drain():
        for copy in send_blocks(stage, sems, store, where, [W_UP] * 8):
            copy.wait()

    for i in range(4):
        stage[i] = low(dot(turned[part(i)], eh))
        stage[4 + i] = low(dot(act_turned, cotangent[:, part(i)]))
    for copy in send_blocks(stage, sems, store, where, numbers):
        copy.start()

    @pl.when(f == steps - 1)
    def last():
        layer_out[...] = low(total[...])
        g2[...] = cotangent[...].astype(WIDE) + norm_back(x2[...], shifts[5:6], back[...])
        for copy in send_blocks(stage, sems, store, where, numbers):
            copy.wait()


def self_backward_kernel(where, g2, normed_turned, sq, sk, sv, so, logs, *rest):
    q, k, v, o = rest[:4], rest[4:8], rest[8:12], rest[12:16]
    own_back, other_back, store, es, probs, grads, own_total, other_total, stage, sems = rest[17:]
    n = pl.program_id(0)
    here = g2.shape[0]
    both = 2 * here

    @pl.when(n == 0)
    def first():
        es[...] = low(g2[...])
        own_total[...] = jnp.zeros_like(own_total)
        other_total[...] = jnp.zeros_like(other_total)

    grad_mixed = low(by_rows(es, o))
    dq, dk, dv = attend_back(
        sq, sk, sv, sk[...].T, so[...], grad_mixed, logs[0], probs, grads, None, both
    )
    dq, dk, dv = low(dq), low(dk), low(dv)
    mixed_turned = so[...].T
    for i in range(4):
        own_total[:, part(i)] += (
            dot_nt(dq, q[i][0]) + dot_nt(dk[:here], k[i][0]) + dot_nt(dv[:here], v[i][0])
        )
        other_total[:, part(i)] += dot_nt(dk[here:], k[i][0]) + dot_nt(dv[here:], v[i][0])

    @pl.when(n > 0)
    def drain():
        for copy in send_blocks(stage, sems, store, where, [Q_SELF] * 16):
            copy.wait()

    for i in range(4):
        stage[i] = low(dot(normed_turned[part(i), :here], dq))
        stage[4 + i] = low(dot(normed_turned[part(i)], dk))
        stage[8 + i] = low(dot(normed_turned[part(i)], dv))
        stage[12 + i] = low(dot(mixed_turned, es[:, part(i)]))
    numbers = [base + i * 4 + n for base in (Q_SELF, K_SELF, V_SELF) for i in range(4)]
    numbers += [O_SELF + n * 4 + i for i in range(4)]
    for copy in send_blocks(stage, sems, store, where, numbers):
        copy.start()

    @pl.when(n == 3)
    def last():
        own_back[...] = own_total[...]
        other_back[...] = low(other_total[...])
        for copy in send_blocks(stage, sems, store, where, numbers):
            copy.wait()


def cross_backward_kernel(
    count, where, x, g2, x1, own_back, got_back, tokens, shifts, valid, normed_turned, cq, ck, cv, co, logs, *rest
):
    q, k, v, o = rest[:4], rest[4:7], rest[7:10], rest[10:14]
    grad_x, grad_tokens, store, ec, g1, probs, grads, x_total, turned, keys_padded, rows_padded, stage, sems = rest[15:]
    n = pl.program_id(0)

    @pl.when(n == 0)
    def first():
        value = g2[...] + norm_back(
            x1[...], shifts[3:4], own_back[...] + got_back[...].astype(WIDE)
        )
        g1[...] = value
        ec[...] = low(value)
        x_total[...] = jnp.zeros_like(x_total)
        grad_tokens[...] = jnp.zeros_like(grad_tokens)
        probs[...] = jnp.zeros_like(probs)
        grads[...] = jnp.zeros_like(grads)
        keys_padded[...] = jnp.zeros_like(keys_padded)
        rows_padded[...] = jnp.zeros_like(rows_padded)
        rows_padded[0, :count] = tokens[:, :BLOCK]
        rows_padded[1, :count] = tokens[:, BLOCK : 2 * BLOCK]
        rows_padded[2, :count] = tokens[:, 2 * BLOCK :]
        for i in range(3):
            turned[part(i)] = rows_padded[i].T

    grad_mixed = low(by_rows(ec, o))
    keys_padded[:count] = ck[...]
    dq, dk, dv = attend_back(
        cq, ck, cv, keys_padded[...].T, co[...], grad_mixed, logs[0], probs, grads, valid[...], count
    )
    dq = low(dq)
    rows_padded[0, :count] = low(dk)
    rows_padded[1, :count] = low(dv)
    mixed_turned = co[...].T
    for i in range(4):
        x_total[:, part(i)] += dot_nt(dq, q[i][0])
    for i in range(3):
        grad_tokens[:, part(i)] += dot_nt(rows_padded[0, :count], k[i][0]) + dot_nt(
            rows_padded[1, :count], v[i][0]
        )

    @pl.when(n > 0)
    def drain():
        for copy in send_blocks(stage, sems, store, where, [Q_CROSS] * 14):
            copy.wait()

    for i in range(4):
        stage[i] = low(dot(normed_turned[part(i)], dq))
        stage[10 + i] = low(dot(mixed_turned, ec[:, part(i)]))
    for i in range(3):
        stage[4 + i] = low(dot(turned[part(i)], rows_padded[0]))
        stage[7 + i] = low(dot(turned[part(i)], rows_padded[1]))
    numbers = [Q_CROSS + i * 4 + n for i in range(4)]
    numbers += [base + i * 4 + n for base in (K_CROSS, V_CROSS) for i in range(3)]
    numbers += [O_CROSS + n * 4 + i for i in range(4)]
    for copy in send_blocks(stage, sems, store, where, numbers):
        copy.start()

    @pl.when(n == 3)
    def last():
        grad_x[...] = g1[...] + norm_back(x[...].astype(WIDE), shifts[1:2], x_total[...])
        for copy in send_blocks(stage, sems, store, where, numbers):
            copy.wait()


def shape(*dims, kind=LOW):
    return jax.ShapeDtypeStruct(dims, kind)


def call(kernel, grid, where, ins, outs, scratch, aliases=None):
    return pl.pallas_call(
        kernel,
        grid_spec=pltpu.PrefetchScalarGridSpec(
            num_scalar_prefetch=1,
            grid=(grid,),
            in_specs=[spec for _, spec in ins],
            out_specs=[spec for _, spec in outs],
            scratch_shapes=scratch,
        ),
        out_shape=[struct for struct, _ in outs],
        input_output_aliases=aliases or {},
        compiler_params=pltpu.CompilerParams(vmem_limit_bytes=VLIM),
    )(where, *[array for array, _ in ins])


def full(array):
    return (array, whole(array.shape))


def made(*dims, kind=LOW):
    return (shape(*dims, kind=kind), whole(dims))


def striped(height):
    return (shape(height, D), stripe(height))


LOG_SPEC = pl.BlockSpec((1, 8, TOK_DEV), lambda n, where: (n, 0, 0))
ANYWHERE = pl.BlockSpec(memory_space=pl.ANY)


def cross_forward(where, store, x, tokens, shifts, valid):
    here, count = x.shape[0], tokens.shape[0]
    padded = -(-count // 128) * 128
    specs = columns(Q_CROSS, 4, 4) + columns(K_CROSS, 3, 4) + columns(V_CROSS, 3, 4) + rows(O_CROSS, 4)
    return call(
        functools.partial(cross_forward_kernel, count),
        4,
        where,
        [full(x), full(tokens), full(shifts), full(valid)] + [(store, spec) for spec in specs],
        [
            made(D, here),
            striped(here),
            striped(count),
            striped(count),
            striped(here),
            (shape(4, 8, here, kind=WIDE), LOG_SPEC),
            made(here, D, kind=WIDE),
            made(here, D),
        ],
        [
            pltpu.VMEM((here, D), LOW),
            pltpu.VMEM((here, D), WIDE),
            pltpu.VMEM((padded, BLOCK), LOW),
            pltpu.VMEM((padded, here), LOW),
        ],
    )


def self_forward(where, store, x1, mine, other, shifts):
    here = x1.shape[0]
    specs = columns(Q_SELF, 4, 4) + columns(K_SELF, 4, 4) + columns(V_SELF, 4, 4) + rows(O_SELF, 4)
    return call(
        lambda where, *refs: self_forward_kernel(*refs),
        4,
        where,
        [full(x1), full(mine), full(other), full(shifts)] + [(store, spec) for spec in specs],
        [
            made(D, 2 * here),
            striped(here),
            striped(2 * here),
            striped(2 * here),
            striped(here),
            (shape(4, 8, here, kind=WIDE), LOG_SPEC),
            made(here, D, kind=WIDE),
            made(here, D),
        ],
        [pltpu.VMEM((here, D), WIDE), pltpu.VMEM((2 * here, here), LOW)],
    )


def feed(where, store, x2, n3, cotangent, shifts, slots):
    here = x2.shape[0]
    specs = columns(W_UP, 4, FF // BLOCK) + rows(W_DOWN, 4)
    return call(
        feed_kernel,
        FF // BLOCK,
        where,
        [full(x2), full(n3), full(cotangent), full(shifts)] + [(store, spec) for spec in specs],
        [made(here, D), made(here, D, kind=WIDE), (shape(slots, BLOCK, BLOCK), ANYWHERE)],
        [
            pltpu.VMEM((here, D), WIDE),
            pltpu.VMEM((here, D), WIDE),
            pltpu.VMEM((D, here), LOW),
            pltpu.VMEM((8, BLOCK, BLOCK), LOW),
            pltpu.SemaphoreType.DMA((8,)),
        ],
    )


def self_backward(where, store, grads, g2, normed_turned, sq, sk, sv, so, logs):
    here = g2.shape[0]
    specs = columns(Q_SELF, 4, 4) + columns(K_SELF, 4, 4) + columns(V_SELF, 4, 4) + rows(O_SELF, 4)
    stripes = [(a, stripe(a.shape[0])) for a in (sq, sk, sv, so)]
    ins = [full(g2), full(normed_turned)] + stripes + [(logs, LOG_SPEC)]
    ins += [(store, spec) for spec in specs] + [(grads, ANYWHERE)]
    return call(
        self_backward_kernel,
        4,
        where,
        ins,
        [made(here, D, kind=WIDE), made(here, D), (shape(*grads.shape), ANYWHERE)],
        [
            pltpu.VMEM((here, D), LOW),
            pltpu.VMEM((2 * here, 2 * here), LOW),
            pltpu.VMEM((2 * here, 2 * here), LOW),
            pltpu.VMEM((here, D), WIDE),
            pltpu.VMEM((here, D), WIDE),
            pltpu.VMEM((16, BLOCK, BLOCK), LOW),
            pltpu.SemaphoreType.DMA((16,)),
        ],
        {len(ins): 2},
    )


def cross_backward(
    where, store, grads, x, g2, x1, own_back, got_back, tokens, shifts, valid, normed_turned, cq, ck, cv, co, logs
):
    here, count = x.shape[0], tokens.shape[0]
    padded = -(-count // 128) * 128
    specs = columns(Q_CROSS, 4, 4) + columns(K_CROSS, 3, 4) + columns(V_CROSS, 3, 4) + rows(O_CROSS, 4)
    ins = [full(a) for a in (x, g2, x1, own_back, got_back, tokens, shifts, valid, normed_turned)]
    ins += [(a, stripe(a.shape[0])) for a in (cq, ck, cv, co)] + [(logs, LOG_SPEC)]
    ins += [(store, spec) for spec in specs] + [(grads, ANYWHERE)]
    return call(
        functools.partial(cross_backward_kernel, count),
        4,
        where,
        ins,
        [made(here, D, kind=WIDE), made(count, DIMG, kind=WIDE), (shape(*grads.shape), ANYWHERE)],
        [
            pltpu.VMEM((here, D), LOW),
            pltpu.VMEM((here, D), WIDE),
            pltpu.VMEM((padded, 2 * here), LOW),
            pltpu.VMEM((padded, 2 * here), LOW),
            pltpu.VMEM((here, D), WIDE),
            pltpu.VMEM((DIMG, padded), LOW),
            pltpu.VMEM((padded, BLOCK), LOW),
            pltpu.VMEM((3, padded, BLOCK), LOW),
            pltpu.VMEM((14, BLOCK, BLOCK), LOW),
            pltpu.SemaphoreType.DMA((14,)),
        ],
        {len(ins): 2},
    )


def partner(block, axis):
    size = lax.axis_size(axis)
    return lax.ppermute(block, axis, [(i, i ^ 1) for i in range(size)])


def soap_update(
    slot_grads,
    first_moment,
    second_moment,
    left_basis,
    right_basis,
    master_weights,
    slot_rates,
    slot_used,
):
    keep_mask = slot_used[:, None, None] > 0.0
    slot_grads = jnp.where(keep_mask, slot_grads, 0.0)
    rotated = jnp.matmul(
        jnp.matmul(jnp.swapaxes(left_basis, 1, 2), slot_grads, precision=highest),
        right_basis,
        precision=highest,
    )
    first_new = moment_decay * first_moment + (1.0 - moment_decay) * rotated
    second_new = moment_decay * second_moment + (1.0 - moment_decay) * rotated * rotated
    correction = 1.0 - moment_decay**STEP
    normalized = first_new / correction / (jnp.sqrt(second_new / correction) + 1e-08)
    rotated_back = jnp.matmul(
        jnp.matmul(left_basis, normalized, precision=highest),
        jnp.swapaxes(right_basis, 1, 2),
        precision=highest,
    )
    fresh_master = master_weights - slot_rates[:, None, None] * (
        rotated_back + 0.01 * master_weights
    )
    fresh_master = jnp.where(keep_mask, fresh_master, 0.0)
    return (
        slot_grads,
        jnp.where(keep_mask, first_new, 0.0),
        jnp.where(keep_mask, second_new, 0.0),
        fresh_master,
        fresh_master.astype(jnp.bfloat16),
    )


def shards(
    triplane,
    cotangent,
    image_tokens,
    modulation,
    image_counts,
    owner_slots,
    master_weights,
    first_moment,
    second_moment,
    left_basis,
    right_basis,
):
    img_size = lax.axis_size("img")
    rows_size = lax.axis_size("rows")
    img_index = lax.axis_index("img")
    flat_index = lax.axis_index("rows") * img_size + img_index
    object_index = flat_index // 2
    pair_index = img_index // 2
    groups = img_size // 2
    slot_cap = image_tokens.shape[0] // groups
    own_count = master_weights.shape[0]
    slot_total = rows_size * img_size * own_count
    fits = rows_size == 16 and img_size == 2 and own_count == 8
    if fits:
        store = gather(master_weights, WAVE_OUT).reshape(-1, BLOCK, BLOCK)
        where = positions(owner_slots)
    else:
        store = lax.all_gather(master_weights.astype(LOW), ("rows", "img"), axis=0, tiled=True)
        where = owner_slots
    where = where.astype(jnp.int32)
    shifts = lax.dynamic_index_in_dim(modulation, object_index, 0, keepdims=False)
    count_here = lax.dynamic_index_in_dim(image_counts, object_index, 0, keepdims=False)
    slot = jnp.arange(slot_cap, dtype=jnp.int32)
    if img_size == 2:
        tokens = jnp.concatenate([image_tokens, partner(image_tokens, "img")], 0)
        sources = jnp.stack([img_index, 1 - img_index])
    else:
        gathered = lax.all_gather(image_tokens, "img", axis=0, tiled=True)
        gathered = gathered.reshape(img_size, groups, slot_cap, DIMG)
        tokens = lax.dynamic_index_in_dim(gathered, pair_index, 1, keepdims=False)
        tokens = tokens.reshape(img_size * slot_cap, DIMG)
        sources = jnp.arange(img_size, dtype=jnp.int32)
    token_index = (slot[None, :] * img_size + sources[:, None]).reshape(-1)
    valid = jnp.broadcast_to((token_index < count_here).astype(WIDE)[:, None], (token_index.shape[0], 128))

    n1_turned, cq, ck, cv, co, cross_logs, x1, n2 = cross_forward(
        where, store, triplane, tokens, shifts, valid
    )
    n2_turned, sq, sk, sv, so, self_logs, x2, n3 = self_forward(
        where, store, x1, n2, partner(n2, "img"), shifts
    )
    layer_out, g2, grads = feed(where, store, x2, n3, cotangent, shifts, slot_total)
    own_back, other_back, grads = self_backward(
        where, store, grads, g2, n2_turned, sq, sk, sv, so, self_logs
    )
    grad_triplane, grad_tokens, grads = cross_backward(
        where,
        store,
        grads,
        triplane,
        g2,
        x1,
        own_back,
        partner(other_back, "img"),
        tokens,
        shifts,
        valid,
        n1_turned,
        cq,
        ck,
        cv,
        co,
        cross_logs,
    )
    if img_size == 2:
        grad_image = grad_tokens[:slot_cap] + partner(grad_tokens[slot_cap:].astype(LOW), "img").astype(WIDE)
    else:
        pick = (jnp.arange(groups, dtype=jnp.int32) == pair_index).astype(WIDE)
        spread = grad_tokens.reshape(img_size, 1, slot_cap, DIMG) * pick[None, :, None, None]
        grad_image = lax.psum_scatter(
            spread.reshape(img_size * groups * slot_cap, DIMG).astype(LOW),
            "img",
            scatter_dimension=0,
            tiled=True,
        ).astype(WIDE)
    if fits:
        slot_grads = scatter(grads.reshape(2, 8, 16, BLOCK, BLOCK), WAVE_IN)
    else:
        used = jnp.zeros((slot_total,), jnp.bool_).at[owner_slots].set(True)
        grads = jnp.where(used[:, None, None], grads, jnp.zeros_like(grads))
        slot_grads = lax.psum_scatter(
            grads, ("rows", "img"), scatter_dimension=0, tiled=True
        ).astype(WIDE)
    my_slots = flat_index * own_count + jnp.arange(own_count, dtype=jnp.int32)
    matched = (owner_slots[:, None] == my_slots[None, :]).astype(WIDE)
    slot_used = jnp.sum(matched, axis=0)
    slot_rates = jnp.sum(matched * jnp.asarray(block_table(weight_scales()))[:, None], axis=0)
    updated = soap_update(
        slot_grads,
        first_moment,
        second_moment,
        left_basis,
        right_basis,
        master_weights,
        slot_rates,
        slot_used,
    )
    return (layer_out, grad_triplane, grad_image) + tuple(updated)


def solution(mesh):
    flat = P(("rows", "img"), None)
    blocks = P(("rows", "img"), None, None)
    in_specs = (flat, flat, flat, P(), P(), P()) + (blocks,) * 5
    out_specs = (flat, flat, flat) + (blocks,) * 5
    return jax.shard_map(shards, mesh=mesh, in_specs=in_specs, out_specs=out_specs, check_vma=False)
```

```python
import functools

import jax
import jax.numpy as jnp
import numpy as np
from jax import lax
from jax.experimental import pallas as pl
from jax.experimental.pallas import tpu as pltpu
from jax.sharding import PartitionSpec as P

D = 1024
HEADS = 16
FF = 4096
DIMG = 768
TOK_DEV = 384
IMG_MAX = 1025
BLOCK = 256
STEP = 5
HEAD = D // HEADS

MESH = pl.DeviceIdType.MESH
VLIM = 60 * 1024 * 1024
WAYS_OUT = (
    ('hi', 'x', 'y', 'lo'),
    ('lo', 'y', 'hi', 'x'),
    ('y', 'hi', 'lo', 'x'),
    ('hi', 'y', 'lo', 'x'),
    ('lo', 'x', 'hi', 'y'),
    ('x', 'hi', 'lo', 'y'),
    ('hi', 'lo', 'x', 'y'),
    ('hi', 'lo', 'y', 'x'),
)
WAYS_IN = (
    ('hi', 'y', 'lo', 'x'),
    ('hi', 'x', 'lo', 'y'),
    ('hi', 'y', 'lo', 'x'),
    ('hi', 'x', 'lo', 'y'),
    ('hi', 'y', 'lo', 'x'),
    ('hi', 'x', 'lo', 'y'),
    ('hi', 'y', 'lo', 'x'),
    ('hi', 'x', 'lo', 'y'),
)
FRONT = 17
ORDER_OUT = (
    (-1, 0), (0, 0), (1, 0), (2, 0), (3, 0), (4, 0), (5, 0), (6, 0),
    (7, 0), (6, 1), (7, 1), (4, 1), (1, 1), (0, 1), (4, 2), (3, 1),
    (6, 2), (7, 2), (7, 3), (6, 3), (3, 2), (5, 1), (2, 1), (0, 2),
    (5, 2), (1, 2), (3, 3), (4, 3), (1, 3), (2, 2), (6, 4), (2, 3),
    (4, 4), (5, 3), (0, 3), (3, 4), (7, 4), (1, 4), (5, 4), (0, 4),
    (2, 4),
)
ORDER_IN = (
    (0, 0), (1, 0), (2, 0), (3, 0), (4, 0), (5, 0), (6, 0), (7, 0),
    (0, 1), (1, 1), (2, 1), (3, 1), (0, 2), (1, 2), (4, 1), (5, 1),
    (2, 2), (3, 2), (0, 3), (1, 3), (6, 1), (7, 1), (4, 2), (5, 2),
    (2, 3), (3, 3), (0, 4), (1, 4), (6, 2), (7, 2), (4, 3), (5, 3),
    (2, 4), (3, 4), (0, 5), (1, 5), (6, 3), (7, 3), (4, 4), (5, 4),
    (2, 5), (3, 5), (6, 4), (7, 4), (4, 5), (5, 5), (6, 5), (7, 5),
)


def coords():
    row = lax.axis_index("rows")
    rest = lax.rem(row, 4)
    return lax.div(row, 4), lax.div(rest, 2), lax.rem(rest, 2), lax.axis_index("img")


def neighbour(kind):
    z, x, c, y = coords()
    if kind == "c":
        c = 1 - c
    if kind == "x":
        x = 1 - x
    if kind == "y":
        y = 1 - y
    if kind == "lo":
        z = z + 1 - 2 * lax.rem(z, 2)
    if kind == "hi":
        z = lax.rem(z + 2, 4)
    return (z * 4 + x * 2 + c, y)


def place(way):
    z, x, c, y = coords()
    bits = {"x": x, "y": y, "lo": lax.rem(z, 2), "hi": lax.div(z, 2)}
    return sum(bits[kind] * 2**k for k, kind in enumerate(way))


def positions(slot, ways):
    owner, j = slot // 8, slot % 8
    z, x, c, y = owner // 8, owner // 4 % 2, owner // 2 % 2, owner % 2
    bits = {"x": x, "y": y, "lo": z % 2, "hi": z // 2}
    total = (c * 8 + j) * 16
    for kind, bit in bits.items():
        total = total + bit * jnp.asarray([2 ** way.index(kind) for way in ways], jnp.int32)[j]
    return total


def greet():
    barrier = pltpu.get_barrier_semaphore()
    for kind in ("c", "x", "y", "lo", "hi"):
        pl.semaphore_signal(barrier, inc=1, device_id=neighbour(kind), device_id_type=MESH)
    pl.semaphore_wait(barrier, 5)


def gather_kernel(
    master, tokens, triplane, modulation, out, both, turned, n1, n1_turned,
    own, wide, mine, x, shifts, others, spread, upright, lsem, csem, ssem, rsem, tsem,
):
    c = coords()[2]
    early = [
        pltpu.make_async_copy(source, target, lsem.at[i])
        for i, (source, target) in enumerate(
            ((master, wide), (tokens, mine), (triplane, x), (modulation, shifts))
        )
    ]
    for copy in early:
        copy.start()
    greet()
    cross = pltpu.make_async_remote_copy(
        tokens, others, tsem.at[0], tsem.at[1], device_id=neighbour("y"), device_id_type=MESH
    )
    early[0].wait()
    copies, keeps = {}, {}

    def start(j, k):
        base = place(WAYS_OUT[j])
        count = 2**k
        first = lax.div(base, count) * count if k < 4 else 0
        here = pl.ds(first, count)
        source = own.at[pl.ds(j, 1)] if k == 0 else out.at[c, j, here]
        copy = pltpu.make_async_remote_copy(
            source,
            out.at[c, j, here],
            ssem.at[j, k],
            rsem.at[j, k],
            device_id=neighbour((WAYS_OUT[j] + ("c",))[k]),
            device_id_type=MESH,
        )
        copy.start()
        copies[j, k] = copy

    for j, k in ORDER_OUT:
        if j < 0:
            cross.start()
        elif k == 0:
            own[j] = wide[j].astype(jnp.bfloat16)
            start(j, 0)
            keep = pltpu.make_async_copy(
                own.at[pl.ds(j, 1)], out.at[c, j, pl.ds(place(WAYS_OUT[j]), 1)], csem.at[j]
            )
            keep.start()
            keeps[j] = keep
        else:
            if k == 1:
                keeps[j].wait()
            copies[j, k - 1].wait_recv()
            start(j, k)
        if (j, k) == ORDER_OUT[FRONT]:
            row = pl.ds(lax.axis_index("rows"), 1)
            early[2].wait()
            early[3].wait()
            one = modulated_norm(
                x[...].astype(jnp.float32), shifts[0, row], shifts[1, row]
            )
            n1[...] = one.astype(jnp.bfloat16)
            n1_turned[...] = one.astype(jnp.bfloat16).T
        if (j, k) == ORDER_OUT[FRONT + 6]:
            half = tokens.shape[0]
            cross.wait()
            early[1].wait()
            spread[:half] = mine[...].astype(jnp.float32)
            spread[half:] = others[...].astype(jnp.float32)
            both[...] = spread[...].astype(jnp.bfloat16)
            upright[2 * half :] = jnp.zeros_like(upright[2 * half :])
            for i in range(tokens.shape[1] // BLOCK):
                lanes = slice(i * BLOCK, (i + 1) * BLOCK)
                upright[: 2 * half] = both[:, lanes]
                turned[lanes] = upright[...].T
    for j in range(8):
        copies[j, 4].wait_recv()
    for copy in copies.values():
        copy.wait_send()


def gather(master, tokens, x, modulation):
    anywhere, inside = pl.BlockSpec(memory_space=pl.ANY), pl.BlockSpec(memory_space=pltpu.VMEM)
    half, width = tokens.shape
    padded = -(-2 * half // 128) * 128
    bf = jnp.bfloat16
    return pl.pallas_call(
        gather_kernel,
        out_shape=[
            jax.ShapeDtypeStruct((2, 8, 16, BLOCK, BLOCK), bf),
            jax.ShapeDtypeStruct((2 * half, width), bf),
            jax.ShapeDtypeStruct((width, padded), bf),
            jax.ShapeDtypeStruct(x.shape, bf),
            jax.ShapeDtypeStruct(x.shape[::-1], bf),
        ],
        in_specs=[anywhere] * 4,
        out_specs=[anywhere] + [inside] * 4,
        scratch_shapes=[
            pltpu.VMEM((8, BLOCK, BLOCK), bf),
            pltpu.VMEM((8, BLOCK, BLOCK), jnp.float32),
            pltpu.VMEM((half, width), bf),
            pltpu.VMEM(x.shape, bf),
            pltpu.VMEM(modulation.shape, jnp.float32),
            pltpu.VMEM((half, width), bf),
            pltpu.VMEM((2 * half, width), jnp.float32),
            pltpu.VMEM((padded, BLOCK), bf),
            pltpu.SemaphoreType.DMA((4,)),
            pltpu.SemaphoreType.DMA((8,)),
            pltpu.SemaphoreType.DMA((8, 5)),
            pltpu.SemaphoreType.DMA((8, 5)),
            pltpu.SemaphoreType.DMA((2,)),
        ],
        compiler_params=pltpu.CompilerParams(
            collective_id=11, has_side_effects=True, vmem_limit_bytes=VLIM
        ),
    )(master, tokens, x, modulation)


def times(a, b, left, right):
    return lax.dot_general(
        a,
        b,
        (((left,), (right,)), ((), ())),
        precision=lax.Precision.HIGHEST,
        preferred_element_type=jnp.float32,
    )


def scatter_kernel(grads, first, second, left, right, master, rates, *rest):
    outs = rest[:5]
    own, r0, r1, r2, r3, r4, held, made, made_low, lsem, ssem, rsem, hsem, osem = rest[5:]
    c = coords()[2]
    got = (r0, r1, r2, r3, r4)
    loads, copies, fetches, puts = [], {}, {}, {}
    for j in range(8):
        load = pltpu.make_async_copy(grads.at[c, j], own.at[j], lsem.at[j])
        load.start()
        loads.append(load)
    greet()

    def exchange(j, s, source, kind):
        copy = pltpu.make_async_remote_copy(
            source,
            got[s].at[j],
            ssem.at[j, s],
            rsem.at[j, s],
            device_id=neighbour(kind),
            device_id_type=MESH,
        )
        copy.start()
        copies[j, s] = copy

    def add(j, s):
        count = 16 >> s
        start = lax.div(place(WAYS_IN[j]), count) * count if s else 0

        def body(b, carry):
            own[j, start + b] = (
                own[j, start + b].astype(jnp.float32) + got[s][j, b].astype(jnp.float32)
            ).astype(jnp.bfloat16)
            return carry

        lax.fori_loop(0, count, body, 0)

    def send(j, s):
        count = 16 >> s
        half = lax.div(place(WAYS_IN[j]), count)
        other = (half + 1 - 2 * lax.rem(half, 2)) * count
        exchange(j, s, own.at[j, pl.ds(other, count)], WAYS_IN[j][4 - s])

    def fetch(turn, j):
        side = turn % 2
        fetches[turn] = [
            pltpu.make_async_copy(array.at[j], held.at[side, i], hsem.at[side, i])
            for i, array in enumerate((first, second, left, right, master))
        ]
        for copy in fetches[turn]:
            copy.start()

    def finish(turn, j):
        side = turn % 2
        for copy in fetches[turn]:
            copy.wait()
        if turn >= 2:
            for copy in puts[turn - 2]:
                copy.wait()
        base = place(WAYS_IN[j])
        used = rates[j, 1:2] > 0.0
        total = own[j, base].astype(jnp.float32) + r4[j, 0].astype(jnp.float32)
        total = jnp.where(used, total, 0.0)
        rotated = times(times(held[side, 2], total, 0, 0), held[side, 3], 1, 0)
        new_first = 0.5 * held[side, 0] + 0.5 * rotated
        new_second = 0.5 * held[side, 1] + 0.5 * rotated * rotated
        fix = 1.0 - 0.5**STEP
        unit = (new_first / fix) / (jnp.sqrt(new_second / fix) + 1e-08)
        update = times(times(held[side, 2], unit, 1, 0), held[side, 3], 1, 1)
        old = held[side, 4]
        new = jnp.where(used, old - rates[j, 0:1] * (update + 0.01 * old), 0.0)
        made[side, 0] = total
        made[side, 1] = jnp.where(used, new_first, 0.0)
        made[side, 2] = jnp.where(used, new_second, 0.0)
        made[side, 3] = new
        made_low[side] = new.astype(jnp.bfloat16)
        puts[turn] = [
            pltpu.make_async_copy(made.at[side, i], outs[i].at[j], osem.at[side, i])
            for i in range(4)
        ] + [pltpu.make_async_copy(made_low.at[side], outs[4].at[j], osem.at[side, 4])]
        for copy in puts[turn]:
            copy.start()

    ends = [j for j, s in ORDER_IN if s == 5]
    for turn in range(2):
        fetch(turn, ends[turn])
    turn = 0
    for j, s in ORDER_IN:
        if s == 0:
            exchange(j, 0, grads.at[1 - c, j], "c")
            continue
        if s == 1:
            loads[j].wait()
        copies[j, s - 1].wait_recv()
        if s < 5:
            add(j, s - 1)
            send(j, s)
        else:
            finish(turn, j)
            if turn < 6:
                fetch(turn + 2, ends[turn + 2])
            turn += 1
    for copy in puts[6] + puts[7]:
        copy.wait()
    for copy in copies.values():
        copy.wait_send()


def scatter(grads, first, second, left, right, master, rates):
    bf, wide, block = jnp.bfloat16, jnp.float32, (BLOCK, BLOCK)
    anywhere = pl.BlockSpec(memory_space=pl.ANY)
    return pl.pallas_call(
        scatter_kernel,
        out_shape=[jax.ShapeDtypeStruct((8,) + block, kind) for kind in (wide,) * 4 + (bf,)],
        in_specs=[anywhere] * 6 + [pl.BlockSpec(memory_space=pltpu.VMEM)],
        out_specs=[anywhere] * 5,
        scratch_shapes=[pltpu.VMEM((8, count) + block, bf) for count in (16, 16, 8, 4, 2, 1)]
        + [
            pltpu.VMEM((2, 5) + block, wide),
            pltpu.VMEM((2, 4) + block, wide),
            pltpu.VMEM((2,) + block, bf),
            pltpu.SemaphoreType.DMA((8,)),
            pltpu.SemaphoreType.DMA((8, 5)),
            pltpu.SemaphoreType.DMA((8, 5)),
            pltpu.SemaphoreType.DMA((2, 5)),
            pltpu.SemaphoreType.DMA((2, 5)),
        ],
        compiler_params=pltpu.CompilerParams(
            collective_id=12, has_side_effects=True, vmem_limit_bytes=VLIM
        ),
    )(grads, first, second, left, right, master, rates)


highest = lax.Precision.HIGHEST
moment_decay = 0.5
LOW = jnp.bfloat16
ROOM = 32 * 1024 * 1024
WIDE = jnp.float32

def shapes_list():
    return [(D, D), (DIMG, D), (DIMG, D), (D, D), (D, D), (D, D), (D, D), (D, D), (D, FF), (FF, D)]


Q_CROSS, K_CROSS, V_CROSS, O_CROSS, Q_SELF, K_SELF, V_SELF, O_SELF, W_UP, W_DOWN = (
    int(v) for v in np.cumsum([0] + [a * b // BLOCK**2 for a, b in shapes_list()])[:10]
)


NBLK = W_DOWN + FF * D // BLOCK**2


def weight_scales():
    self_root = (2.0 * TOK_DEV) ** 0.5
    cross_root = (IMG_MAX / 2.0) ** 0.5
    return [
        D ** (-0.5),
        DIMG ** (-0.5),
        DIMG ** (-0.5),
        0.5 * cross_root * D ** (-0.5),
        D ** (-0.5),
        D ** (-0.5),
        D ** (-0.5),
        0.5 * self_root * D ** (-0.5),
        D ** (-0.5),
        2.0 * FF ** (-0.5),
    ]


def block_table(scales):
    pieces = []
    for shape_pair, scale_value in zip(shapes_list(), scales):
        amount = shape_pair[0] * shape_pair[1] // (BLOCK * BLOCK)
        pieces.append(np.full((amount,), scale_value, np.float32))
    return np.concatenate(pieces)


def low(v):
    return v.astype(LOW)


def dot(a, b):
    return jnp.dot(a, b, preferred_element_type=WIDE)


def dot_nt(a, b):
    return lax.dot_general(a, b, (((1,), (1,)), ((), ())), preferred_element_type=WIDE)


def part(k):
    return slice(k * BLOCK, (k + 1) * BLOCK)


def norm_parts(values):
    centered = values - jnp.mean(values, axis=-1, keepdims=True)
    variance = jnp.mean(centered * centered, axis=-1, keepdims=True)
    return centered, lax.rsqrt(variance + 1e-06)


def modulated_norm(values, shift, scale):
    centered, inverse = norm_parts(values)
    return centered * inverse * (1.0 + scale) + shift


def norm_back(values, scale, grad_normed):
    centered, inverse = norm_parts(values)
    unit = centered * inverse
    grad_unit = grad_normed * (1.0 + scale)
    return inverse * (
        grad_unit
        - jnp.mean(grad_unit, axis=-1, keepdims=True)
        - unit * jnp.mean(grad_unit * unit, axis=-1, keepdims=True)
    )


def halves(pair):
    lane = lax.broadcasted_iota(jnp.int32, pair.shape, 1)
    zero = jnp.zeros_like(pair)
    return jnp.where(lane < HEAD, pair, zero), jnp.where(lane < HEAD, zero, pair)


def fill_valid(valid, where, parts):
    cap = valid.shape[0] // parts
    slot = lax.broadcasted_iota(jnp.int32, (cap, 128), 0)
    for i in range(parts):
        number = slot * parts + where[2 * NBLK + 2 + i]
        valid[i * cap : (i + 1) * cap] = (number < where[2 * NBLK + 1]).astype(WIDE)


def of_row(shifts, where, k):
    return shifts[k, pl.ds(where[2 * NBLK], 1)]


def masked(scores, valid):
    if valid is None:
        return scores
    wide = jnp.concatenate([valid] * (scores.shape[1] // valid.shape[1]), axis=1)
    return jnp.where(wide > 0.0, scores, -1e30)


def columns(base, tall, wide):
    return [
        pl.BlockSpec((1, BLOCK, BLOCK), lambda n, where, i=i: (where[base + i * wide + n], 0, 0))
        for i in range(tall)
    ]


def rows(base, wide):
    return [
        pl.BlockSpec((1, BLOCK, BLOCK), lambda n, where, k=k: (where[base + n * wide + k], 0, 0))
        for k in range(wide)
    ]


def whole(shape, mode=None):
    return pl.BlockSpec(shape, lambda n, where: (0,) * len(shape), pipeline_mode=mode)


def stripe(height):
    return pl.BlockSpec((height, BLOCK), lambda n, where: (0, n))


def stacked(blocks, axis):
    return jnp.concatenate([block[0] for block in blocks], axis=axis)


def by_columns(left, blocks):
    return dot(left[...], stacked(blocks, 0))


def by_rows(left, blocks):
    return dot_nt(left[...], stacked(blocks, 1))


def attend_part(queries, keys, values_turned, weights, valid, count):
    outs, tops, totals, scores = [], [], [], []
    for pair in range(2):
        lanes = slice(pair * 2 * HEAD, (pair + 1) * 2 * HEAD)
        key_pair = keys[:count, lanes]
        for query in halves(queries[:, lanes]):
            scores.append(masked(dot_nt(key_pair, query), valid))
    for head in range(4):
        top = jnp.max(scores[head], axis=0, keepdims=True)
        exponent = jnp.exp(scores[head] - top)
        weights[head, :count] = low(exponent)
        tops.append(top)
        totals.append(jnp.sum(exponent, axis=0, keepdims=True))
    for head in range(4):
        outs.append(dot(values_turned[head * HEAD : (head + 1) * HEAD], weights[head]))
    return outs, tops, totals


def attend_end(outs, tops, totals):
    turned = jnp.concatenate([out / total for out, total in zip(outs, totals)], axis=0)
    logs = [top + jnp.log(total) for top, total in zip(tops, totals)]
    return low(turned.T), jnp.concatenate(logs + logs, axis=0)


def attend_back(queries, keys, values, keys_turned, mixed, grad_mixed, logs, probs, grads, valid, count):
    tokens = queries.shape[0]
    inner = (mixed.astype(WIDE) * grad_mixed.astype(WIDE)).T
    grad_query, grad_key, grad_value = [], [], []
    for pair in range(2):
        lanes = slice(pair * 2 * HEAD, (pair + 1) * 2 * HEAD)
        key_pair, value_pair = keys[:count, lanes], values[:count, lanes]
        query_halves = halves(queries[:, lanes])
        mixed_halves = halves(grad_mixed[:, lanes])
        scores = [masked(dot_nt(key_pair, query), valid) for query in query_halves]
        grad_full = [dot_nt(value_pair, mix) for mix in mixed_halves]
        for which in range(2):
            head = pair * 2 + which
            own = slice(head * HEAD, (head + 1) * HEAD)
            side = slice(which * tokens, (which + 1) * tokens)
            full = jnp.exp(scores[which] - logs[head : head + 1])
            back = low(full * (grad_full[which] - jnp.sum(inner[own], axis=0, keepdims=True)))
            probs[pair, :count, side] = low(full)
            grads[pair, :count, side] = back
        for which in range(2):
            head = pair * 2 + which
            own = slice(head * HEAD, (head + 1) * HEAD)
            side = slice(which * tokens, (which + 1) * tokens)
            grad_query.append(dot(keys_turned[own], grads[pair, :, side]))
        grad_key.append(dot(grads[pair, :count], jnp.concatenate(query_halves, axis=0)))
        grad_value.append(dot(probs[pair, :count], jnp.concatenate(mixed_halves, axis=0)))
    grad_query = jnp.concatenate(grad_query, axis=0).T * HEAD ** (-0.5)
    return grad_query, jnp.concatenate(grad_key, axis=1), jnp.concatenate(grad_value, axis=1)


def send_blocks(stage, sems, side, store, where, numbers):
    return [
        pltpu.make_async_copy(stage.at[side, i], store.at[where[NBLK + number]], sems.at[side, i])
        for i, number in enumerate(numbers)
    ]


def keep_blocks(products, stage, sems, store, where, numbers):
    step, steps = pl.program_id(0), pl.num_programs(0)
    side = lax.rem(step, 2)

    @pl.when(step >= 2)
    def reuse():
        for copy in send_blocks(stage, sems, side, store, where, numbers):
            copy.wait()

    for i, product in enumerate(products()):
        stage[side, i] = product
    for copy in send_blocks(stage, sems, side, store, where, numbers):
        copy.start()

    @pl.when(step == steps - 1)
    def drain():
        for copy in send_blocks(stage, sems, 1 - side, store, where, numbers):
            copy.wait()
        for copy in send_blocks(stage, sems, side, store, where, numbers):
            copy.wait()


def cross_forward_kernel(parts, where, x, n1, tokens, shifts, *rest):
    q, k, v, o = rest[:4], rest[4:7], rest[7:10], rest[10:14]
    cq, ck, cv, co, logs, x1, n2, total, turned, weights, valid = rest[14:]
    n = pl.program_id(0)
    count = tokens.shape[0]

    @pl.when(n == 0)
    def first():
        total[...] = x[...].astype(WIDE)
        turned[count:] = jnp.zeros_like(turned[count:])
        for head in range(4):
            weights[head, count:] = jnp.zeros_like(weights[head, count:])
        fill_valid(valid, where, parts)

    queries = low(by_columns(n1, q)) * HEAD ** (-0.5)
    cq[...] = queries
    pair = low(dot(tokens[...], jnp.concatenate([stacked(k, 0), stacked(v, 0)], axis=1)))
    ck[...] = pair[:, :BLOCK]
    cv[...] = pair[:, BLOCK:]
    turned[:count] = pair[:, BLOCK:]
    mixed, log_total = attend_end(
        *attend_part(queries, ck, turned[...].T, weights, valid[...], count)
    )
    co[...] = mixed
    logs[0] = log_total
    total[...] += dot(mixed, stacked(o, 1))

    @pl.when(n == 3)
    def last():
        after = total[...]
        x1[...] = after
        n2[...] = low(modulated_norm(after, of_row(shifts, where, 2), of_row(shifts, where, 3)))


def self_own_kernel(where, mine, *rest):
    q, k, v = rest[:4], rest[4:8], rest[8:12]
    turned, sq, sk, sv, mix, stats, weights = rest[12:]
    n = pl.program_id(0)

    @pl.when(n == 0)
    def first():
        turned[...] = mine[...].T

    all_three = low(
        dot(mine[...], jnp.concatenate([stacked(q, 0), stacked(k, 0), stacked(v, 0)], axis=1))
    )
    queries = all_three[:, :BLOCK] * HEAD ** (-0.5)
    sq[...] = queries
    sk[...] = all_three[:, BLOCK : 2 * BLOCK]
    sv[...] = all_three[:, 2 * BLOCK :]
    outs, tops, totals = attend_part(queries, sk, sv[...].T, weights, None, mine.shape[0])
    mix[...] = jnp.concatenate(outs, axis=0)
    stats[0] = jnp.concatenate(tops + totals, axis=0)


def self_other_kernel(where, x1, other, shifts, sq, mix, stats, *rest):
    k, v, o = rest[:4], rest[4:8], rest[8:12]
    turned, sk, sv, so, logs, x2, n3, total, weights = rest[12:]
    n = pl.program_id(0)

    @pl.when(n == 0)
    def first():
        turned[...] = other[...].T
        total[...] = x1[...]

    pair = low(dot(other[...], jnp.concatenate([stacked(k, 0), stacked(v, 0)], axis=1)))
    sk[...] = pair[:, :BLOCK]
    sv[...] = pair[:, BLOCK:]
    parts = attend_part(sq[...], sk, sv[...].T, weights, None, other.shape[0])
    outs, tops, totals = [], [], []
    for head, (out, top, amount) in enumerate(zip(*parts)):
        old_top, old_amount = stats[0, head : head + 1], stats[0, 4 + head : 5 + head]
        new_top = jnp.maximum(top, old_top)
        grow, keep = jnp.exp(top - new_top), jnp.exp(old_top - new_top)
        outs.append(out * grow + mix[head * HEAD : (head + 1) * HEAD] * keep)
        tops.append(new_top)
        totals.append(amount * grow + old_amount * keep)
    mixed, logs[0] = attend_end(outs, tops, totals)
    so[...] = mixed
    total[...] += dot(mixed, stacked(o, 1))

    @pl.when(n == 3)
    def last():
        after = total[...]
        x2[...] = after
        n3[...] = low(modulated_norm(after, of_row(shifts, where, 4), of_row(shifts, where, 5)))


def grid_of(blocks, across):
    return jnp.concatenate(
        [stacked(blocks[i : i + across], 1) for i in range(0, len(blocks), across)], axis=0
    )


def feed_early_kernel(where, cotangent, *rest):
    down, grad_act = rest[:16], rest[16]
    grad_act[...] = dot_nt(cotangent[...], grid_of(down, 4))


def feed_kernel(where, x2, n3, cotangent, shifts, grad_act, *rest):
    up, down = rest[:8], rest[8:16]
    layer_out, g2, act, eh, total, back = rest[16:]
    f = pl.program_id(0)

    @pl.when(f == 0)
    def first():
        total[...] = x2[...]
        back[...] = jnp.zeros_like(back)

    up = grid_of(up, 2)
    hidden = dot(n3[...], up)
    square = hidden * hidden
    root = (2.0 / np.pi) ** 0.5
    bent = jnp.tanh(root * (hidden + 0.044715 * (square * hidden)))
    act[...] = low(0.5 * hidden * (1.0 + bent))
    slope = 0.5 * (1.0 + bent) + 0.5 * hidden * (1.0 - bent * bent) * (
        root * (1.0 + 3.0 * 0.044715 * square)
    )
    eh[...] = low(grad_act[...] * slope)
    total[...] += dot(act[...], grid_of(down, 4))
    back[...] += dot_nt(eh[...], up)

    @pl.when(f == FF // BLOCK // 2 - 1)
    def last():
        layer_out[...] = low(total[...])
        g2[...] = cotangent[...].astype(WIDE) + norm_back(x2[...], of_row(shifts, where, 5), back[...])


def feed_late_kernel(where, n3, cotangent, act, eh, store, turned, stage, sems):
    f = pl.program_id(0)
    wide = FF // BLOCK

    @pl.when(f == 0)
    def first():
        turned[...] = n3[...].T

    def products():
        up = low(dot(turned[...], eh[...]))
        down = low(dot(act[...].T, cotangent[...]))
        return [up[part(i), part(j)] for j in range(2) for i in range(4)] + [
            down[part(j), part(i)] for j in range(2) for i in range(4)
        ]

    numbers = [W_UP + i * wide + f * 2 + j for j in range(2) for i in range(4)]
    numbers += [W_DOWN + (f * 2 + j) * 4 + i for j in range(2) for i in range(4)]
    keep_blocks(products, stage, sems, store, where, numbers)


def self_backward_kernel(where, g2, sq, k_own, k_other, v_own, v_other, so, logs, *rest):
    q, k, v, o = rest[:4], rest[4:8], rest[8:12], rest[12:16]
    own_back, other_back, dq, dk, dv, es, probs, grads, sk, sv, own_total, other_total = rest[16:]
    n = pl.program_id(0)
    here = g2.shape[0]
    both = 2 * here

    @pl.when(n == 0)
    def first():
        es[...] = low(g2[...])
        own_total[...] = jnp.zeros_like(own_total)
        other_total[...] = jnp.zeros_like(other_total)

    grad_mixed = low(by_rows(es, o))
    sk[:here] = k_own[...]
    sk[here:] = k_other[...]
    sv[:here] = v_own[...]
    sv[here:] = v_other[...]
    wide_dq, wide_dk, wide_dv = attend_back(
        sq, sk, sv, sk[...].T, so[...], grad_mixed, logs[0], probs, grads, None, both
    )
    dq[...] = low(wide_dq)
    dk[...] = low(wide_dk)
    dv[...] = low(wide_dv)
    key_values = jnp.concatenate([stacked(k, 0), stacked(v, 0)], axis=1)
    both_grads = jnp.concatenate([dk[...], dv[...]], axis=1)
    own_total[...] += dot_nt(
        jnp.concatenate([dq[...], both_grads[:here]], axis=1),
        jnp.concatenate([stacked(q, 0), key_values], axis=1),
    )
    other_total[...] += dot_nt(both_grads[here:], key_values)

    @pl.when(n == 3)
    def last():
        own_back[...] = own_total[...]
        other_back[...] = low(other_total[...])


def self_late_kernel(where, g2, own_turned, other_turned, dq, dk, dv, so, old, store, es, turned, stage, sems):
    n = pl.program_id(0)
    here = g2.shape[0]

    @pl.when(n == 0)
    def first():
        es[...] = low(g2[...])
        turned[:, :here] = own_turned[...]
        turned[:, here:] = other_turned[...]

    def products():
        tall = [low(dot(own_turned[...], dq[...]))]
        tall += [low(dot(turned[...], grad[...])) for grad in (dk, dv)]
        flat = low(dot(so[...].T, es[...]))
        return [matrix[part(i)] for matrix in tall for i in range(4)] + [
            flat[:, part(i)] for i in range(4)
        ]

    numbers = [base + i * 4 + n for base in (Q_SELF, K_SELF, V_SELF) for i in range(4)]
    numbers += [O_SELF + n * 4 + i for i in range(4)]
    keep_blocks(products, stage, sems, store, where, numbers)


def cross_backward_kernel(
    parts, where, x, g2, x1, own_back, got_back, turned, shifts, normed_turned, cq, ck, cv, co, logs, *rest
):
    q, k, v, o = rest[:4], rest[4:7], rest[7:10], rest[10:14]
    grad_x, grad_tokens, store, ec, g1, probs, grads, x_total, keys_padded, rows_padded, valid, stage, sems = rest[15:]
    n = pl.program_id(0)
    count = ck.shape[0]

    @pl.when(n == 0)
    def first():
        value = g2[...] + norm_back(
            x1[...], of_row(shifts, where, 3), own_back[...] + got_back[...].astype(WIDE)
        )
        g1[...] = value
        ec[...] = low(value)
        x_total[...] = jnp.zeros_like(x_total)
        grad_tokens[...] = jnp.zeros_like(grad_tokens)
        keys_padded[count:] = jnp.zeros_like(keys_padded[count:])
        for i in range(2):
            grads[i, count:] = jnp.zeros_like(grads[i, count:])
            rows_padded[i, count:] = jnp.zeros_like(rows_padded[i, count:])
        fill_valid(valid, where, parts)

    grad_mixed = low(by_rows(ec, o))
    keys_padded[:count] = ck[...]
    dq, dk, dv = attend_back(
        cq, ck, cv, keys_padded[...].T, co[...], grad_mixed, logs[0], probs, grads, valid[...], count
    )
    dq = low(dq)
    rows_padded[0, :count] = low(dk)
    rows_padded[1, :count] = low(dv)
    x_total[...] += dot_nt(dq, stacked(q, 0))
    grad_tokens[...] += dot_nt(
        jnp.concatenate([rows_padded[0, :count], rows_padded[1, :count]], axis=1),
        jnp.concatenate([stacked(k, 0), stacked(v, 0)], axis=1),
    )

    def products():
        tall = [low(dot(normed_turned[...], dq))]
        tall += [low(dot(turned[...], rows_padded[side])) for side in range(2)]
        flat = low(dot(co[...].T, ec[...]))
        return [matrix[part(i)] for matrix in tall for i in range(matrix.shape[0] // BLOCK)] + [
            flat[:, part(i)] for i in range(4)
        ]

    numbers = [Q_CROSS + i * 4 + n for i in range(4)]
    numbers += [base + i * 4 + n for base in (K_CROSS, V_CROSS) for i in range(3)]
    numbers += [O_CROSS + n * 4 + i for i in range(4)]
    keep_blocks(products, stage, sems, store, where, numbers)

    @pl.when(n == 3)
    def last():
        grad_x[...] = g1[...] + norm_back(x[...].astype(WIDE), of_row(shifts, where, 1), x_total[...])


def shape(*dims, kind=LOW):
    return jax.ShapeDtypeStruct(dims, kind)


def call(kernel, grid, where, ins, outs, scratch, products, aliases=None, room=ROOM):
    moved = BLOCK * BLOCK * 2 * grid * 16
    return pl.pallas_call(
        kernel,
        grid_spec=pltpu.PrefetchScalarGridSpec(
            num_scalar_prefetch=1,
            grid=(grid,),
            in_specs=[spec for _, spec in ins],
            out_specs=[spec for _, spec in outs],
            scratch_shapes=scratch,
        ),
        out_shape=[struct for struct, _ in outs],
        input_output_aliases=aliases or {},
        compiler_params=pltpu.CompilerParams(vmem_limit_bytes=room),
        cost_estimate=pl.CostEstimate(
            flops=int(2 * products), bytes_accessed=moved, transcendentals=0
        ),
    )(where, *[array for array, _ in ins])


def full(array):
    return (array, whole(array.shape, pl.Buffered(1)))


def of_object(modulation):
    return full(modulation)


def made(*dims, kind=LOW):
    return (shape(*dims, kind=kind), whole(dims))


def striped(height):
    return (shape(height, D), stripe(height))


LOG_SPEC = pl.BlockSpec((1, 8, TOK_DEV), lambda n, where: (n, 0, 0))
ANYWHERE = pl.BlockSpec(memory_space=pl.ANY)


def padded_to(count):
    return -(-count // 128) * 128


def cross_forward(where, store, x, n1, tokens, shifts, parts):
    here, count = x.shape[0], tokens.shape[0]
    padded = padded_to(count)
    specs = columns(Q_CROSS, 4, 4) + columns(K_CROSS, 3, 4) + columns(V_CROSS, 3, 4) + rows(O_CROSS, 4)
    return call(
        functools.partial(cross_forward_kernel, parts),
        4,
        where,
        [full(x), full(n1), full(tokens), of_object(shifts)] + [(store, spec) for spec in specs],
        [
            striped(here),
            striped(count),
            striped(count),
            striped(here),
            (shape(4, 8, here, kind=WIDE), LOG_SPEC),
            made(here, D, kind=WIDE),
            made(here, D),
        ],
        [
            pltpu.VMEM((here, D), WIDE),
            pltpu.VMEM((padded, BLOCK), LOW),
            pltpu.VMEM((4, padded, here), LOW),
            pltpu.VMEM((count, 128), WIDE),
        ],
        here * D * D * 12,
    )


def tall(here):
    return pl.BlockSpec((BLOCK, here), lambda n, where: (n, 0))


def self_own(where, store, mine):
    here = mine.shape[0]
    specs = columns(Q_SELF, 4, 4) + columns(K_SELF, 4, 4) + columns(V_SELF, 4, 4)
    return call(
        self_own_kernel,
        4,
        where,
        [full(mine)] + [(store, spec) for spec in specs],
        [
            made(D, here),
            striped(here),
            striped(here),
            striped(here),
            (shape(D, here, kind=WIDE), tall(here)),
            (shape(4, 8, here, kind=WIDE), LOG_SPEC),
        ],
        [pltpu.VMEM((4, here, here), LOW)],
        here * D * D * 6,
    )


def self_other(where, store, x1, other, shifts, sq, mix, stats):
    here = x1.shape[0]
    specs = columns(K_SELF, 4, 4) + columns(V_SELF, 4, 4) + rows(O_SELF, 4)
    return call(
        self_other_kernel,
        4,
        where,
        [full(x1), full(other), of_object(shifts), (sq, stripe(here)), (mix, tall(here)), (stats, LOG_SPEC)]
        + [(store, spec) for spec in specs],
        [
            made(D, here),
            striped(here),
            striped(here),
            striped(here),
            (shape(4, 8, here, kind=WIDE), LOG_SPEC),
            made(here, D, kind=WIDE),
            made(here, D),
        ],
        [pltpu.VMEM((here, D), WIDE), pltpu.VMEM((4, here, here), LOW)],
        here * D * D * 6,
    )


def feed_specs(height):
    wide = FF // BLOCK
    up = [
        pl.BlockSpec(
            (1, BLOCK, BLOCK),
            lambda n, where, i=i, j=j: (where[W_UP + i * wide + n * height + j], 0, 0),
        )
        for i in range(4)
        for j in range(height)
    ]
    down = [
        pl.BlockSpec(
            (1, BLOCK, BLOCK), lambda n, where, i=i: (where[W_DOWN + n * height * 4 + i], 0, 0)
        )
        for i in range(4 * height)
    ]
    return up, down


def broad(here, height):
    return pl.BlockSpec((here, height * BLOCK), lambda n, where: (0, n))


def feed_early(where, store, cotangent):
    here = cotangent.shape[0]
    return call(
        feed_early_kernel,
        FF // BLOCK // 4,
        where,
        [full(cotangent)] + [(store, spec) for spec in feed_specs(4)[1]],
        [(shape(here, FF, kind=WIDE), broad(here, 4))],
        [],
        here * D * FF,
    )[0]


def feed(where, store, x2, n3, cotangent, shifts, grad_act):
    here = x2.shape[0]
    up, down = feed_specs(2)
    return call(
        feed_kernel,
        FF // BLOCK // 2,
        where,
        [full(x2), full(n3), full(cotangent), of_object(shifts), (grad_act, broad(here, 2))]
        + [(store, spec) for spec in up + down],
        [
            made(here, D),
            made(here, D, kind=WIDE),
            (shape(here, FF), broad(here, 2)),
            (shape(here, FF), broad(here, 2)),
        ],
        [pltpu.VMEM((here, D), WIDE), pltpu.VMEM((here, D), WIDE)],
        here * D * FF * 3,
    )


def feed_late(where, n3, cotangent, act, eh, slots):
    here = n3.shape[0]
    return call(
        feed_late_kernel,
        FF // BLOCK // 2,
        where,
        [full(n3), full(cotangent), (act, broad(here, 2)), (eh, broad(here, 2))],
        [(shape(slots, BLOCK, BLOCK), ANYWHERE)],
        [
            pltpu.VMEM((D, here), LOW),
            pltpu.VMEM((2, 16, BLOCK, BLOCK), LOW),
            pltpu.SemaphoreType.DMA((2, 16)),
        ],
        here * D * FF * 2,
    )[0]


def self_backward(where, store, g2, sq, k_own, k_other, v_own, v_other, so, logs):
    here = g2.shape[0]
    specs = columns(Q_SELF, 4, 4) + columns(K_SELF, 4, 4) + columns(V_SELF, 4, 4) + rows(O_SELF, 4)
    ins = [full(g2)] + [(a, stripe(here)) for a in (sq, k_own, k_other, v_own, v_other, so)]
    ins += [(logs, LOG_SPEC)] + [(store, spec) for spec in specs]
    return call(
        self_backward_kernel,
        4,
        where,
        ins,
        [made(here, D, kind=WIDE), made(here, D), striped(here), striped(2 * here), striped(2 * here)],
        [
            pltpu.VMEM((here, D), LOW),
            pltpu.VMEM((2, 2 * here, 2 * here), LOW),
            pltpu.VMEM((2, 2 * here, 2 * here), LOW),
            pltpu.VMEM((2 * here, BLOCK), LOW),
            pltpu.VMEM((2 * here, BLOCK), LOW),
            pltpu.VMEM((here, D), WIDE),
            pltpu.VMEM((here, D), WIDE),
        ],
        here * D * D * 16,
    )


def self_late(where, grads, g2, own_turned, other_turned, dq, dk, dv, so):
    here = g2.shape[0]
    ins = [full(a) for a in (g2, own_turned, other_turned)]
    ins += [(a, stripe(a.shape[0])) for a in (dq, dk, dv, so)] + [(grads, ANYWHERE)]
    return call(
        self_late_kernel,
        4,
        where,
        ins,
        [(shape(*grads.shape), ANYWHERE)],
        [
            pltpu.VMEM((here, D), LOW),
            pltpu.VMEM((D, 2 * here), LOW),
            pltpu.VMEM((2, 16, BLOCK, BLOCK), LOW),
            pltpu.SemaphoreType.DMA((2, 16)),
        ],
        here * D * D * 6,
        {len(ins): 0},
    )[0]


def cross_backward(
    where, store, grads, x, g2, x1, own_back, got_back, turned, shifts, normed_turned, cq, ck, cv, co, logs, parts
):
    here, count = x.shape[0], ck.shape[0]
    padded = padded_to(count)
    specs = columns(Q_CROSS, 4, 4) + columns(K_CROSS, 3, 4) + columns(V_CROSS, 3, 4) + rows(O_CROSS, 4)
    ins = [full(a) for a in (x, g2, x1, own_back, got_back, turned)]
    ins += [of_object(shifts), full(normed_turned)]
    ins += [(a, stripe(a.shape[0])) for a in (cq, ck, cv, co)] + [(logs, LOG_SPEC)]
    ins += [(store, spec) for spec in specs] + [(grads, ANYWHERE)]
    return call(
        functools.partial(cross_backward_kernel, parts),
        4,
        where,
        ins,
        [made(here, D, kind=WIDE), made(count, DIMG, kind=WIDE), (shape(*grads.shape), ANYWHERE)],
        [
            pltpu.VMEM((here, D), LOW),
            pltpu.VMEM((here, D), WIDE),
            pltpu.VMEM((2, padded, 2 * here), LOW),
            pltpu.VMEM((2, padded, 2 * here), LOW),
            pltpu.VMEM((here, D), WIDE),
            pltpu.VMEM((padded, BLOCK), LOW),
            pltpu.VMEM((2, padded, BLOCK), LOW),
            pltpu.VMEM((count, 128), WIDE),
            pltpu.VMEM((2, 14, BLOCK, BLOCK), LOW),
            pltpu.SemaphoreType.DMA((2, 14)),
        ],
        here * D * D * 24,
        {len(ins): 2},
        room=40 * 1024 * 1024,
    )


def partner(block, axis):
    size = lax.axis_size(axis)
    return lax.ppermute(block, axis, [(i, i ^ 1) for i in range(size)])


def soap_update(
    slot_grads,
    first_moment,
    second_moment,
    left_basis,
    right_basis,
    master_weights,
    slot_rates,
    slot_used,
):
    keep_mask = slot_used[:, None, None] > 0.0
    slot_grads = jnp.where(keep_mask, slot_grads, 0.0)
    rotated = jnp.matmul(
        jnp.matmul(jnp.swapaxes(left_basis, 1, 2), slot_grads, precision=highest),
        right_basis,
        precision=highest,
    )
    first_new = moment_decay * first_moment + (1.0 - moment_decay) * rotated
    second_new = moment_decay * second_moment + (1.0 - moment_decay) * rotated * rotated
    correction = 1.0 - moment_decay**STEP
    normalized = first_new / correction / (jnp.sqrt(second_new / correction) + 1e-08)
    rotated_back = jnp.matmul(
        jnp.matmul(left_basis, normalized, precision=highest),
        jnp.swapaxes(right_basis, 1, 2),
        precision=highest,
    )
    fresh_master = master_weights - slot_rates[:, None, None] * (
        rotated_back + 0.01 * master_weights
    )
    fresh_master = jnp.where(keep_mask, fresh_master, 0.0)
    return (
        slot_grads,
        jnp.where(keep_mask, first_new, 0.0),
        jnp.where(keep_mask, second_new, 0.0),
        fresh_master,
        fresh_master.astype(jnp.bfloat16),
    )


def shards(
    triplane,
    cotangent,
    image_tokens,
    modulation,
    image_counts,
    owner_slots,
    master_weights,
    first_moment,
    second_moment,
    left_basis,
    right_basis,
):
    img_size = lax.axis_size("img")
    rows_size = lax.axis_size("rows")
    img_index = lax.axis_index("img")
    flat_index = lax.axis_index("rows") * img_size + img_index
    object_index = flat_index // 2
    pair_index = img_index // 2
    groups = img_size // 2
    slot_cap = image_tokens.shape[0] // groups
    own_count = master_weights.shape[0]
    slot_total = rows_size * img_size * own_count
    fits = rows_size == 16 and img_size == 2 and own_count == 8
    modulation = jnp.swapaxes(modulation, 0, 1)
    info = [object_index[None], image_counts[object_index][None]]
    if img_size == 2:
        info += [img_index[None], 1 - img_index[None]]
    else:
        info += [jnp.arange(img_size, dtype=jnp.int32)]
    if fits:
        store, tokens, tokens_turned, n1, n1_turned = gather(
            master_weights, image_tokens, triplane, modulation
        )
        store = store.reshape(-1, BLOCK, BLOCK)
        where = [positions(owner_slots, WAYS_OUT), positions(owner_slots, WAYS_IN)]
    else:
        store = lax.all_gather(master_weights.astype(LOW), ("rows", "img"), axis=0, tiled=True)
        where = [owner_slots, owner_slots]
        if img_size == 2:
            tokens = jnp.concatenate([image_tokens, partner(image_tokens, "img")], 0)
        else:
            tokens = lax.all_gather(image_tokens, "img", axis=0, tiled=True)
            tokens = tokens.reshape(img_size, groups, slot_cap, DIMG)
            tokens = lax.dynamic_index_in_dim(tokens, pair_index, 1, keepdims=False)
            tokens = tokens.reshape(img_size * slot_cap, DIMG)
        count = tokens.shape[0]
        tokens_turned = jnp.pad(tokens.T, ((0, 0), (0, padded_to(count) - count)))
        shifts = lax.dynamic_index_in_dim(modulation, object_index, 1, keepdims=False)
        n1 = low(modulated_norm(triplane.astype(WIDE), shifts[0], shifts[1]))
        n1_turned = n1.T
    where = jnp.concatenate([piece.astype(jnp.int32) for piece in where + info])

    cq, ck, cv, co, cross_logs, x1, n2 = cross_forward(
        where, store, triplane, n1, tokens, modulation, img_size
    )
    n2_other = partner(n2, "img")
    own_turned, sq, k_own, v_own, mix, stats = self_own(where, store, n2)
    grad_act = feed_early(where, store, cotangent)
    other_turned, k_other, v_other, so, self_logs, x2, n3 = self_other(
        where, store, x1, n2_other, modulation, sq, mix, stats
    )
    layer_out, g2, act, eh = feed(where, store, x2, n3, cotangent, modulation, grad_act)
    own_back, other_back, dq, dk, dv = self_backward(
        where, store, g2, sq, k_own, k_other, v_own, v_other, so, self_logs
    )
    got_back = partner(other_back, "img")
    grads = feed_late(where, n3, cotangent, act, eh, slot_total)
    grads = self_late(where, grads, g2, own_turned, other_turned, dq, dk, dv, so)
    grad_triplane, grad_tokens, grads = cross_backward(
        where,
        store,
        grads,
        triplane,
        g2,
        x1,
        own_back,
        got_back,
        tokens_turned,
        modulation,
        n1_turned,
        cq,
        ck,
        cv,
        co,
        cross_logs,
        img_size,
    )
    if img_size == 2:
        grad_image = grad_tokens[:slot_cap] + partner(grad_tokens[slot_cap:].astype(LOW), "img").astype(WIDE)
    else:
        pick = (jnp.arange(groups, dtype=jnp.int32) == pair_index).astype(WIDE)
        spread = grad_tokens.reshape(img_size, 1, slot_cap, DIMG) * pick[None, :, None, None]
        grad_image = lax.psum_scatter(
            spread.reshape(img_size * groups * slot_cap, DIMG).astype(LOW),
            "img",
            scatter_dimension=0,
            tiled=True,
        ).astype(WIDE)
    my_slots = flat_index * own_count + jnp.arange(own_count, dtype=jnp.int32)
    matched = (owner_slots[:, None] == my_slots[None, :]).astype(WIDE)
    slot_used = jnp.sum(matched, axis=0)
    slot_rates = jnp.sum(matched * jnp.asarray(block_table(weight_scales()))[:, None], axis=0)
    state = (first_moment, second_moment, left_basis, right_basis, master_weights)
    if fits:
        rates = jnp.broadcast_to(
            jnp.stack([slot_rates, slot_used], 1)[:, :, None], (own_count, 2, BLOCK)
        )
        updated = scatter(grads.reshape(2, 8, 16, BLOCK, BLOCK), *state, rates)
    else:
        used = jnp.zeros((slot_total,), jnp.bool_).at[owner_slots].set(True)
        grads = jnp.where(used[:, None, None], grads, jnp.zeros_like(grads))
        slot_grads = lax.psum_scatter(
            grads, ("rows", "img"), scatter_dimension=0, tiled=True
        ).astype(WIDE)
        updated = soap_update(slot_grads, *state, slot_rates, slot_used)
    return (layer_out, grad_triplane, grad_image) + tuple(updated)


def solution(mesh):
    flat = P(("rows", "img"), None)
    blocks = P(("rows", "img"), None, None)
    in_specs = (flat, flat, flat, P(), P(), P()) + (blocks,) * 5
    out_specs = (flat, flat, flat) + (blocks,) * 5
    return jax.shard_map(shards, mesh=mesh, in_specs=in_specs, out_specs=out_specs, check_vma=False)
```

```python
import functools

import jax
import jax.numpy as jnp
import numpy as np
from jax import lax
from jax.experimental import pallas as pl
from jax.experimental.pallas import tpu as pltpu
from jax.sharding import PartitionSpec as P

D = 1024
HEADS = 16
FF = 4096
DIMG = 768
TOK_DEV = 384
IMG_MAX = 1025
BLOCK = 256
STEP = 5
HEAD = D // HEADS

MESH = pl.DeviceIdType.MESH
VLIM = 60 * 1024 * 1024
WAYS_OUT = (
    ('hi', 'x', 'y', 'lo'),
    ('lo', 'y', 'hi', 'x'),
    ('y', 'hi', 'lo', 'x'),
    ('hi', 'y', 'lo', 'x'),
    ('lo', 'x', 'hi', 'y'),
    ('x', 'hi', 'lo', 'y'),
    ('hi', 'lo', 'x', 'y'),
    ('hi', 'lo', 'y', 'x'),
)
WAYS_IN = (
    ('lo', 'y', 'hi', 'x'),
    ('hi', 'x', 'y', 'lo'),
    ('hi', 'y', 'x', 'lo'),
    ('hi', 'lo', 'x', 'y'),
    ('hi', 'x', 'lo', 'y'),
    ('hi', 'y', 'lo', 'x'),
    ('hi', 'lo', 'x', 'y'),
    ('lo', 'hi', 'y', 'x'),
)
FRONT = 17
ORDER_OUT = (
    (-1, 0), (0, 0), (1, 0), (2, 0), (3, 0), (4, 0), (5, 0), (6, 0),
    (7, 0), (6, 1), (7, 1), (4, 1), (1, 1), (0, 1), (4, 2), (3, 1),
    (6, 2), (7, 2), (7, 3), (6, 3), (3, 2), (5, 1), (2, 1), (0, 2),
    (5, 2), (1, 2), (3, 3), (4, 3), (1, 3), (2, 2), (6, 4), (2, 3),
    (4, 4), (5, 3), (0, 3), (3, 4), (7, 4), (1, 4), (5, 4), (0, 4),
    (2, 4),
)
ORDER_IN = (
    (0, 0), (1, 0), (2, 0), (3, 0), (4, 0), (5, 0), (6, 0), (7, 0),
    (1, 1), (0, 1), (4, 1), (0, 2), (7, 1), (4, 2), (6, 1), (2, 1),
    (7, 2), (5, 1), (5, 2), (6, 2), (1, 2), (0, 3), (7, 3), (6, 3),
    (1, 3), (3, 1), (1, 4), (4, 3), (7, 4), (2, 2), (4, 4), (2, 3),
    (6, 4), (3, 2), (0, 4), (5, 3), (4, 5), (6, 5), (2, 4), (7, 5),
    (3, 3), (2, 5), (5, 4), (1, 5), (0, 5), (5, 5), (3, 4), (3, 5),
)


def coords():
    row = lax.axis_index("rows")
    rest = lax.rem(row, 4)
    return lax.div(row, 4), lax.div(rest, 2), lax.rem(rest, 2), lax.axis_index("img")


def neighbour(kind):
    z, x, c, y = coords()
    if kind == "c":
        c = 1 - c
    if kind == "x":
        x = 1 - x
    if kind == "y":
        y = 1 - y
    if kind == "lo":
        z = z + 1 - 2 * lax.rem(z, 2)
    if kind == "hi":
        z = lax.rem(z + 2, 4)
    return (z * 4 + x * 2 + c, y)


def place(way):
    z, x, c, y = coords()
    bits = {"x": x, "y": y, "lo": lax.rem(z, 2), "hi": lax.div(z, 2)}
    return sum(bits[kind] * 2**k for k, kind in enumerate(way))


def positions(slot, ways):
    owner, j = slot // 8, slot % 8
    z, x, c, y = owner // 8, owner // 4 % 2, owner // 2 % 2, owner % 2
    bits = {"x": x, "y": y, "lo": z % 2, "hi": z // 2}
    total = (c * 8 + j) * 16
    for kind, bit in bits.items():
        total = total + bit * jnp.asarray([2 ** way.index(kind) for way in ways], jnp.int32)[j]
    return total


def greet():
    barrier = pltpu.get_barrier_semaphore()
    for kind in ("c", "x", "y", "lo", "hi"):
        pl.semaphore_signal(barrier, inc=1, device_id=neighbour(kind), device_id_type=MESH)
    pl.semaphore_wait(barrier, 5)


def gather_kernel(
    master, tokens, triplane, modulation, out, both, turned, n1, n1_turned,
    own, wide, mine, x, shifts, others, spread, upright, lsem, csem, ssem, rsem, tsem,
):
    c = coords()[2]
    early = [
        pltpu.make_async_copy(source, target, lsem.at[i])
        for i, (source, target) in enumerate(
            ((master, wide), (tokens, mine), (triplane, x), (modulation, shifts))
        )
    ]
    for copy in early:
        copy.start()
    greet()
    cross = pltpu.make_async_remote_copy(
        tokens, others, tsem.at[0], tsem.at[1], device_id=neighbour("y"), device_id_type=MESH
    )
    early[0].wait()
    copies, keeps = {}, {}

    def start(j, k):
        base = place(WAYS_OUT[j])
        count = 2**k
        first = lax.div(base, count) * count if k < 4 else 0
        here = pl.ds(first, count)
        source = own.at[pl.ds(j, 1)] if k == 0 else out.at[c, j, here]
        copy = pltpu.make_async_remote_copy(
            source,
            out.at[c, j, here],
            ssem.at[j, k],
            rsem.at[j, k],
            device_id=neighbour((WAYS_OUT[j] + ("c",))[k]),
            device_id_type=MESH,
        )
        copy.start()
        copies[j, k] = copy

    for j, k in ORDER_OUT:
        if j < 0:
            cross.start()
        elif k == 0:
            own[j] = wide[j].astype(jnp.bfloat16)
            start(j, 0)
            keep = pltpu.make_async_copy(
                own.at[pl.ds(j, 1)], out.at[c, j, pl.ds(place(WAYS_OUT[j]), 1)], csem.at[j]
            )
            keep.start()
            keeps[j] = keep
        else:
            if k == 1:
                keeps[j].wait()
            copies[j, k - 1].wait_recv()
            start(j, k)
        if (j, k) == ORDER_OUT[FRONT]:
            row = pl.ds(lax.axis_index("rows"), 1)
            early[2].wait()
            early[3].wait()
            one = modulated_norm(
                x[...].astype(jnp.float32), shifts[0, row], shifts[1, row]
            )
            n1[...] = one.astype(jnp.bfloat16)
            n1_turned[...] = one.astype(jnp.bfloat16).T
        if (j, k) == ORDER_OUT[FRONT + 6]:
            half = tokens.shape[0]
            cross.wait()
            early[1].wait()
            spread[:half] = mine[...].astype(jnp.float32)
            spread[half:] = others[...].astype(jnp.float32)
            both[...] = spread[...].astype(jnp.bfloat16)
            upright[2 * half :] = jnp.zeros_like(upright[2 * half :])
            for i in range(tokens.shape[1] // BLOCK):
                lanes = slice(i * BLOCK, (i + 1) * BLOCK)
                upright[: 2 * half] = both[:, lanes]
                turned[lanes] = upright[...].T
    for j in range(8):
        copies[j, 4].wait_recv()
    for copy in copies.values():
        copy.wait_send()


def gather(master, tokens, x, modulation):
    anywhere, inside = pl.BlockSpec(memory_space=pl.ANY), pl.BlockSpec(memory_space=pltpu.VMEM)
    half, width = tokens.shape
    padded = -(-2 * half // 128) * 128
    bf = jnp.bfloat16
    return pl.pallas_call(
        gather_kernel,
        out_shape=[
            jax.ShapeDtypeStruct((2, 8, 16, BLOCK, BLOCK), bf),
            jax.ShapeDtypeStruct((2 * half, width), bf),
            jax.ShapeDtypeStruct((width, padded), bf),
            jax.ShapeDtypeStruct(x.shape, bf),
            jax.ShapeDtypeStruct(x.shape[::-1], bf),
        ],
        in_specs=[anywhere] * 4,
        out_specs=[anywhere] + [inside] * 4,
        scratch_shapes=[
            pltpu.VMEM((8, BLOCK, BLOCK), bf),
            pltpu.VMEM((8, BLOCK, BLOCK), jnp.float32),
            pltpu.VMEM((half, width), bf),
            pltpu.VMEM(x.shape, bf),
            pltpu.VMEM(modulation.shape, jnp.float32),
            pltpu.VMEM((half, width), bf),
            pltpu.VMEM((2 * half, width), jnp.float32),
            pltpu.VMEM((padded, BLOCK), bf),
            pltpu.SemaphoreType.DMA((4,)),
            pltpu.SemaphoreType.DMA((8,)),
            pltpu.SemaphoreType.DMA((8, 5)),
            pltpu.SemaphoreType.DMA((8, 5)),
            pltpu.SemaphoreType.DMA((2,)),
        ],
        compiler_params=pltpu.CompilerParams(
            collective_id=11, has_side_effects=True, vmem_limit_bytes=VLIM
        ),
    )(master, tokens, x, modulation)


def times(a, b, left, right):
    return lax.dot_general(
        a,
        b,
        (((left,), (right,)), ((), ())),
        precision=lax.Precision.HIGHEST,
        preferred_element_type=jnp.float32,
    )


def scatter_kernel(grads, first, second, left, right, master, rates, *rest):
    outs = rest[:5]
    own, r0, r1, r2, r3, r4, held, made, made_low, lsem, ssem, rsem, hsem, osem = rest[5:]
    c = coords()[2]
    got = (r0, r1, r2, r3, r4)
    loads, copies, fetches, puts = [], {}, {}, {}
    for j in range(8):
        load = pltpu.make_async_copy(grads.at[c, j], own.at[j], lsem.at[j])
        load.start()
        loads.append(load)
    greet()

    def exchange(j, s, source, kind):
        copy = pltpu.make_async_remote_copy(
            source,
            got[s].at[j],
            ssem.at[j, s],
            rsem.at[j, s],
            device_id=neighbour(kind),
            device_id_type=MESH,
        )
        copy.start()
        copies[j, s] = copy

    def add(j, s):
        count = 16 >> s
        start = lax.div(place(WAYS_IN[j]), count) * count if s else 0

        def body(b, carry):
            own[j, start + b] = own[j, start + b] + got[s][j, b]
            return carry

        lax.fori_loop(0, count, body, 0)

    def send(j, s):
        count = 16 >> s
        half = lax.div(place(WAYS_IN[j]), count)
        other = (half + 1 - 2 * lax.rem(half, 2)) * count
        exchange(j, s, own.at[j, pl.ds(other, count)], WAYS_IN[j][4 - s])

    def fetch(turn, j):
        side = turn % 2
        fetches[turn] = [
            pltpu.make_async_copy(array.at[j], held.at[side, i], hsem.at[side, i])
            for i, array in enumerate((first, second, left, right, master))
        ]
        for copy in fetches[turn]:
            copy.start()

    def finish(turn, j):
        side = turn % 2
        for copy in fetches[turn]:
            copy.wait()
        if turn >= 2:
            for copy in puts[turn - 2]:
                copy.wait()
        base = place(WAYS_IN[j])
        used = rates[j, 1:2] > 0.0
        total = own[j, base].astype(jnp.float32) + r4[j, 0].astype(jnp.float32)
        total = jnp.where(used, total, 0.0)
        rotated = times(times(held[side, 2], total, 0, 0), held[side, 3], 1, 0)
        new_first = 0.5 * held[side, 0] + 0.5 * rotated
        new_second = 0.5 * held[side, 1] + 0.5 * rotated * rotated
        fix = 1.0 - 0.5**STEP
        unit = (new_first / fix) / (jnp.sqrt(new_second / fix) + 1e-08)
        update = times(times(held[side, 2], unit, 1, 0), held[side, 3], 1, 1)
        old = held[side, 4]
        new = jnp.where(used, old - rates[j, 0:1] * (update + 0.01 * old), 0.0)
        made[side, 0] = total
        made[side, 1] = jnp.where(used, new_first, 0.0)
        made[side, 2] = jnp.where(used, new_second, 0.0)
        made[side, 3] = new
        made_low[side] = new.astype(jnp.bfloat16)
        puts[turn] = [
            pltpu.make_async_copy(made.at[side, i], outs[i].at[j], osem.at[side, i])
            for i in range(4)
        ] + [pltpu.make_async_copy(made_low.at[side], outs[4].at[j], osem.at[side, 4])]
        for copy in puts[turn]:
            copy.start()

    ends = [j for j, s in ORDER_IN if s == 5]
    for turn in range(2):
        fetch(turn, ends[turn])
    turn = 0
    for j, s in ORDER_IN:
        if s == 0:
            exchange(j, 0, grads.at[1 - c, j], "c")
            continue
        if s == 1:
            loads[j].wait()
        copies[j, s - 1].wait_recv()
        if s < 5:
            add(j, s - 1)
            send(j, s)
        else:
            finish(turn, j)
            if turn < 6:
                fetch(turn + 2, ends[turn + 2])
            turn += 1
    for copy in puts[6] + puts[7]:
        copy.wait()
    for copy in copies.values():
        copy.wait_send()


def scatter(grads, first, second, left, right, master, rates):
    bf, wide, block = jnp.bfloat16, jnp.float32, (BLOCK, BLOCK)
    anywhere = pl.BlockSpec(memory_space=pl.ANY)
    return pl.pallas_call(
        scatter_kernel,
        out_shape=[jax.ShapeDtypeStruct((8,) + block, kind) for kind in (wide,) * 4 + (bf,)],
        in_specs=[anywhere] * 6 + [pl.BlockSpec(memory_space=pltpu.VMEM)],
        out_specs=[anywhere] * 5,
        scratch_shapes=[pltpu.VMEM((8, count) + block, bf) for count in (16, 16, 8, 4, 2, 1)]
        + [
            pltpu.VMEM((2, 5) + block, wide),
            pltpu.VMEM((2, 4) + block, wide),
            pltpu.VMEM((2,) + block, bf),
            pltpu.SemaphoreType.DMA((8,)),
            pltpu.SemaphoreType.DMA((8, 5)),
            pltpu.SemaphoreType.DMA((8, 5)),
            pltpu.SemaphoreType.DMA((2, 5)),
            pltpu.SemaphoreType.DMA((2, 5)),
        ],
        compiler_params=pltpu.CompilerParams(
            collective_id=12, has_side_effects=True, vmem_limit_bytes=54 * 1024 * 1024
        ),
    )(grads, first, second, left, right, master, rates)


highest = lax.Precision.HIGHEST
moment_decay = 0.5
LOW = jnp.bfloat16
ROOM = 32 * 1024 * 1024
WIDE = jnp.float32

def shapes_list():
    return [(D, D), (DIMG, D), (DIMG, D), (D, D), (D, D), (D, D), (D, D), (D, D), (D, FF), (FF, D)]


Q_CROSS, K_CROSS, V_CROSS, O_CROSS, Q_SELF, K_SELF, V_SELF, O_SELF, W_UP, W_DOWN = (
    int(v) for v in np.cumsum([0] + [a * b // BLOCK**2 for a, b in shapes_list()])[:10]
)


NBLK = W_DOWN + FF * D // BLOCK**2


def weight_scales():
    self_root = (2.0 * TOK_DEV) ** 0.5
    cross_root = (IMG_MAX / 2.0) ** 0.5
    return [
        D ** (-0.5),
        DIMG ** (-0.5),
        DIMG ** (-0.5),
        0.5 * cross_root * D ** (-0.5),
        D ** (-0.5),
        D ** (-0.5),
        D ** (-0.5),
        0.5 * self_root * D ** (-0.5),
        D ** (-0.5),
        2.0 * FF ** (-0.5),
    ]


def block_table(scales):
    pieces = []
    for shape_pair, scale_value in zip(shapes_list(), scales):
        amount = shape_pair[0] * shape_pair[1] // (BLOCK * BLOCK)
        pieces.append(np.full((amount,), scale_value, np.float32))
    return np.concatenate(pieces)


def low(v):
    return v.astype(LOW)


def dot(a, b):
    return jnp.dot(a, b, preferred_element_type=WIDE)


def dot_nt(a, b):
    return lax.dot_general(a, b, (((1,), (1,)), ((), ())), preferred_element_type=WIDE)


def part(k):
    return slice(k * BLOCK, (k + 1) * BLOCK)


def norm_parts(values):
    centered = values - jnp.mean(values, axis=-1, keepdims=True)
    variance = jnp.mean(centered * centered, axis=-1, keepdims=True)
    return centered, lax.rsqrt(variance + 1e-06)


def modulated_norm(values, shift, scale):
    centered, inverse = norm_parts(values)
    return centered * inverse * (1.0 + scale) + shift


def norm_back(values, scale, grad_normed):
    centered, inverse = norm_parts(values)
    unit = centered * inverse
    grad_unit = grad_normed * (1.0 + scale)
    return inverse * (
        grad_unit
        - jnp.mean(grad_unit, axis=-1, keepdims=True)
        - unit * jnp.mean(grad_unit * unit, axis=-1, keepdims=True)
    )


def halves(pair):
    lane = lax.broadcasted_iota(jnp.int32, pair.shape, 1)
    zero = jnp.zeros_like(pair)
    return jnp.where(lane < HEAD, pair, zero), jnp.where(lane < HEAD, zero, pair)


def fill_valid(valid, where, parts):
    cap = valid.shape[0] // parts
    slot = lax.broadcasted_iota(jnp.int32, (cap, 128), 0)
    for i in range(parts):
        number = slot * parts + where[2 * NBLK + 2 + i]
        valid[i * cap : (i + 1) * cap] = (number < where[2 * NBLK + 1]).astype(WIDE)


def of_row(shifts, where, k):
    return shifts[k, pl.ds(where[2 * NBLK], 1)]


def masked(scores, valid):
    if valid is None:
        return scores
    wide = jnp.concatenate([valid] * (scores.shape[1] // valid.shape[1]), axis=1)
    return jnp.where(wide > 0.0, scores, -1e30)


def columns(base, tall, wide):
    return [
        pl.BlockSpec((1, BLOCK, BLOCK), lambda n, where, i=i: (where[base + i * wide + n], 0, 0))
        for i in range(tall)
    ]


def rows(base, wide):
    return [
        pl.BlockSpec((1, BLOCK, BLOCK), lambda n, where, k=k: (where[base + n * wide + k], 0, 0))
        for k in range(wide)
    ]


def whole(shape, mode=None):
    return pl.BlockSpec(shape, lambda n, where: (0,) * len(shape), pipeline_mode=mode)


def stripe(height):
    return pl.BlockSpec((height, BLOCK), lambda n, where: (0, n))


def stacked(blocks, axis):
    return jnp.concatenate([block[0] for block in blocks], axis=axis)


def by_columns(left, blocks):
    return dot(left[...], stacked(blocks, 0))


def by_rows(left, blocks):
    return dot_nt(left[...], stacked(blocks, 1))


def attend_part(queries, keys, values_turned, weights, valid, count):
    outs, tops, totals, scores = [], [], [], []
    for pair in range(2):
        lanes = slice(pair * 2 * HEAD, (pair + 1) * 2 * HEAD)
        key_pair = keys[:count, lanes]
        for query in halves(queries[:, lanes]):
            scores.append(masked(dot_nt(key_pair, query), valid))
    for head in range(4):
        top = jnp.max(scores[head], axis=0, keepdims=True)
        exponent = jnp.exp(scores[head] - top)
        weights[head, :count] = low(exponent)
        tops.append(top)
        totals.append(jnp.sum(exponent, axis=0, keepdims=True))
    for head in range(4):
        outs.append(dot(values_turned[head * HEAD : (head + 1) * HEAD], weights[head]))
    return outs, tops, totals


def attend_end(outs, tops, totals):
    turned = jnp.concatenate([out / total for out, total in zip(outs, totals)], axis=0)
    logs = [top + jnp.log(total) for top, total in zip(tops, totals)]
    return low(turned.T), jnp.concatenate(logs + logs, axis=0)


def attend_back(queries, keys, values, keys_turned, mixed, grad_mixed, logs, probs, grads, valid, count):
    tokens = queries.shape[0]
    inner = (mixed.astype(WIDE) * grad_mixed.astype(WIDE)).T
    grad_query, grad_key, grad_value = [], [], []
    for pair in range(2):
        lanes = slice(pair * 2 * HEAD, (pair + 1) * 2 * HEAD)
        key_pair, value_pair = keys[:count, lanes], values[:count, lanes]
        query_halves = halves(queries[:, lanes])
        mixed_halves = halves(grad_mixed[:, lanes])
        scores = [masked(dot_nt(key_pair, query), valid) for query in query_halves]
        grad_full = [dot_nt(value_pair, mix) for mix in mixed_halves]
        for which in range(2):
            head = pair * 2 + which
            own = slice(head * HEAD, (head + 1) * HEAD)
            side = slice(which * tokens, (which + 1) * tokens)
            full = jnp.exp(scores[which] - logs[head : head + 1])
            back = low(full * (grad_full[which] - jnp.sum(inner[own], axis=0, keepdims=True)))
            probs[pair, :count, side] = low(full)
            grads[pair, :count, side] = back
        for which in range(2):
            head = pair * 2 + which
            own = slice(head * HEAD, (head + 1) * HEAD)
            side = slice(which * tokens, (which + 1) * tokens)
            grad_query.append(dot(keys_turned[own], grads[pair, :, side]))
        grad_key.append(dot(grads[pair, :count], jnp.concatenate(query_halves, axis=0)))
        grad_value.append(dot(probs[pair, :count], jnp.concatenate(mixed_halves, axis=0)))
    grad_query = jnp.concatenate(grad_query, axis=0).T * HEAD ** (-0.5)
    return grad_query, jnp.concatenate(grad_key, axis=1), jnp.concatenate(grad_value, axis=1)


def send_blocks(stage, sems, side, store, where, numbers):
    return [
        pltpu.make_async_copy(stage.at[side, i], store.at[where[NBLK + number]], sems.at[side, i])
        for i, number in enumerate(numbers)
    ]


def keep_blocks(products, stage, sems, store, where, numbers):
    step, steps = pl.program_id(0), pl.num_programs(0)
    side = lax.rem(step, 2)

    @pl.when(step >= 2)
    def reuse():
        for copy in send_blocks(stage, sems, side, store, where, numbers):
            copy.wait()

    for i, product in enumerate(products()):
        stage[side, i] = product
    for copy in send_blocks(stage, sems, side, store, where, numbers):
        copy.start()

    @pl.when(step == steps - 1)
    def drain():
        for copy in send_blocks(stage, sems, 1 - side, store, where, numbers):
            copy.wait()
        for copy in send_blocks(stage, sems, side, store, where, numbers):
            copy.wait()


def cross_forward_kernel(parts, where, x, n1, tokens, shifts, *rest):
    q, k, v, o = rest[:4], rest[4:7], rest[7:10], rest[10:14]
    cq, ck, cv, co, logs, x1, n2, total, turned, weights, valid = rest[14:]
    n = pl.program_id(0)
    count = tokens.shape[0]

    @pl.when(n == 0)
    def first():
        total[...] = x[...].astype(WIDE)
        turned[count:] = jnp.zeros_like(turned[count:])
        for head in range(4):
            weights[head, count:] = jnp.zeros_like(weights[head, count:])
        fill_valid(valid, where, parts)

    queries = low(by_columns(n1, q)) * HEAD ** (-0.5)
    cq[...] = queries
    pair = low(dot(tokens[...], jnp.concatenate([stacked(k, 0), stacked(v, 0)], axis=1)))
    ck[...] = pair[:, :BLOCK]
    cv[...] = pair[:, BLOCK:]
    turned[:count] = pair[:, BLOCK:]
    mixed, log_total = attend_end(
        *attend_part(queries, ck, turned[...].T, weights, valid[...], count)
    )
    co[...] = mixed
    logs[0] = log_total
    total[...] += dot(mixed, stacked(o, 1))

    @pl.when(n == 3)
    def last():
        after = total[...]
        x1[...] = after
        n2[...] = low(modulated_norm(after, of_row(shifts, where, 2), of_row(shifts, where, 3)))


def self_own_kernel(where, mine, *rest):
    q, k, v = rest[:4], rest[4:8], rest[8:12]
    turned, sq, sk, sv, mix, stats, weights = rest[12:]
    n = pl.program_id(0)

    @pl.when(n == 0)
    def first():
        turned[...] = mine[...].T

    all_three = low(
        dot(mine[...], jnp.concatenate([stacked(q, 0), stacked(k, 0), stacked(v, 0)], axis=1))
    )
    queries = all_three[:, :BLOCK] * HEAD ** (-0.5)
    sq[...] = queries
    sk[...] = all_three[:, BLOCK : 2 * BLOCK]
    sv[...] = all_three[:, 2 * BLOCK :]
    outs, tops, totals = attend_part(queries, sk, sv[...].T, weights, None, mine.shape[0])
    mix[...] = jnp.concatenate(outs, axis=0)
    stats[0] = jnp.concatenate(tops + totals, axis=0)


def self_other_kernel(where, x1, other, shifts, sq, mix, stats, *rest):
    k, v, o = rest[:4], rest[4:8], rest[8:12]
    turned, sk, sv, so, logs, x2, n3, total, weights = rest[12:]
    n = pl.program_id(0)

    @pl.when(n == 0)
    def first():
        turned[...] = other[...].T
        total[...] = x1[...]

    pair = low(dot(other[...], jnp.concatenate([stacked(k, 0), stacked(v, 0)], axis=1)))
    sk[...] = pair[:, :BLOCK]
    sv[...] = pair[:, BLOCK:]
    parts = attend_part(sq[...], sk, sv[...].T, weights, None, other.shape[0])
    outs, tops, totals = [], [], []
    for head, (out, top, amount) in enumerate(zip(*parts)):
        old_top, old_amount = stats[0, head : head + 1], stats[0, 4 + head : 5 + head]
        new_top = jnp.maximum(top, old_top)
        grow, keep = jnp.exp(top - new_top), jnp.exp(old_top - new_top)
        outs.append(out * grow + mix[head * HEAD : (head + 1) * HEAD] * keep)
        tops.append(new_top)
        totals.append(amount * grow + old_amount * keep)
    mixed, logs[0] = attend_end(outs, tops, totals)
    so[...] = mixed
    total[...] += dot(mixed, stacked(o, 1))

    @pl.when(n == 3)
    def last():
        after = total[...]
        x2[...] = after
        n3[...] = low(modulated_norm(after, of_row(shifts, where, 4), of_row(shifts, where, 5)))


def grid_of(blocks, across):
    return jnp.concatenate(
        [stacked(blocks[i : i + across], 1) for i in range(0, len(blocks), across)], axis=0
    )


def feed_early_kernel(where, cotangent, *rest):
    down, grad_act = rest[:16], rest[16]
    grad_act[...] = dot_nt(cotangent[...], grid_of(down, 4))


def feed_kernel(where, x2, n3, cotangent, shifts, grad_act, *rest):
    up, down = rest[:16], rest[16:32]
    layer_out, g2, act, eh, total, back = rest[32:]
    f = pl.program_id(0)

    @pl.when(f == 0)
    def first():
        total[...] = x2[...]
        back[...] = jnp.zeros_like(back)

    root = (2.0 / np.pi) ** 0.5
    ups = [stacked(up[j::4], 0) for j in range(4)]
    hiddens = [dot(n3[...], ups[j]) for j in range(4)]
    for j, hidden in enumerate(hiddens):
        square = hidden * hidden
        bent = jnp.tanh(hidden * (root + (0.044715 * root) * square))
        gate = 0.5 * bent + 0.5
        value = hidden * gate
        act[:, part(j)] = low(value)
        slope = gate + value * (1.0 - gate) * (2.0 * root + (6.0 * 0.044715 * root) * square)
        eh[:, part(j)] = low(grad_act[:, part(j)] * slope)
    total[...] += dot(act[...], grid_of(down, 4))
    back[...] += dot_nt(eh[...], jnp.concatenate(ups, axis=1))

    @pl.when(f == FF // BLOCK // 4 - 1)
    def last():
        layer_out[...] = low(total[...])
        g2[...] = cotangent[...].astype(WIDE) + norm_back(x2[...], of_row(shifts, where, 5), back[...])


def feed_late_kernel(where, n3, cotangent, act, eh, store, turned, stage, sems):
    f = pl.program_id(0)
    wide = FF // BLOCK

    @pl.when(f == 0)
    def first():
        turned[...] = n3[...].T

    def products():
        up = low(dot(turned[...], eh[...]))
        down = low(dot(act[...].T, cotangent[...]))
        return [up[part(i), part(j)] for j in range(2) for i in range(4)] + [
            down[part(j), part(i)] for j in range(2) for i in range(4)
        ]

    numbers = [W_UP + i * wide + f * 2 + j for j in range(2) for i in range(4)]
    numbers += [W_DOWN + (f * 2 + j) * 4 + i for j in range(2) for i in range(4)]
    keep_blocks(products, stage, sems, store, where, numbers)


def self_backward_kernel(where, g2, sq, k_own, k_other, v_own, v_other, so, logs, *rest):
    q, k, v, o = rest[:4], rest[4:8], rest[8:12], rest[12:16]
    own_back, other_back, dq, dk, dv, es, probs, grads, sk, sv, own_total, other_total = rest[16:]
    n = pl.program_id(0)
    here = g2.shape[0]
    both = 2 * here

    @pl.when(n == 0)
    def first():
        es[...] = low(g2[...])
        own_total[...] = jnp.zeros_like(own_total)
        other_total[...] = jnp.zeros_like(other_total)

    grad_mixed = low(by_rows(es, o))
    sk[:here] = k_own[...]
    sk[here:] = k_other[...]
    sv[:here] = v_own[...]
    sv[here:] = v_other[...]
    wide_dq, wide_dk, wide_dv = attend_back(
        sq, sk, sv, sk[...].T, so[...], grad_mixed, logs[0], probs, grads, None, both
    )
    dq[...] = low(wide_dq)
    dk[...] = low(wide_dk)
    dv[...] = low(wide_dv)
    key_values = jnp.concatenate([stacked(k, 0), stacked(v, 0)], axis=1)
    both_grads = jnp.concatenate([dk[...], dv[...]], axis=1)
    own_total[...] += dot_nt(
        jnp.concatenate([dq[...], both_grads[:here]], axis=1),
        jnp.concatenate([stacked(q, 0), key_values], axis=1),
    )
    other_total[...] += dot_nt(both_grads[here:], key_values)

    @pl.when(n == 3)
    def last():
        own_back[...] = own_total[...]
        other_back[...] = low(other_total[...])


def self_late_kernel(where, g2, own_turned, other_turned, dq, dk, dv, so, old, store, es, turned, stage, sems):
    n = pl.program_id(0)
    here = g2.shape[0]

    @pl.when(n == 0)
    def first():
        es[...] = low(g2[...])
        turned[:, :here] = own_turned[...]
        turned[:, here:] = other_turned[...]

    def products():
        query = low(dot(own_turned[...], dq[...]))
        pair = low(dot(turned[...], jnp.concatenate([dk[...], dv[...]], axis=1)))
        flat = low(dot(so[...].T, es[...]))
        blocks = [query[part(i)] for i in range(4)]
        blocks += [pair[part(i), part(j)] for j in range(2) for i in range(4)]
        return blocks + [flat[:, part(i)] for i in range(4)]

    numbers = [base + i * 4 + n for base in (Q_SELF, K_SELF, V_SELF) for i in range(4)]
    numbers += [O_SELF + n * 4 + i for i in range(4)]
    keep_blocks(products, stage, sems, store, where, numbers)


def cross_backward_kernel(
    parts, where, x, g2, x1, own_back, got_back, turned, shifts, normed_turned, cq, ck, cv, co, logs, *rest
):
    q, k, v, o = rest[:4], rest[4:7], rest[7:10], rest[10:14]
    grad_x, grad_own, grad_others, store, grad_tokens, ec, g1, probs, grads, x_total, keys_padded, rows_padded, valid, stage, sems = rest[15:]
    n = pl.program_id(0)
    count = ck.shape[0]

    @pl.when(n == 0)
    def first():
        value = g2[...] + norm_back(
            x1[...], of_row(shifts, where, 3), own_back[...] + got_back[...].astype(WIDE)
        )
        g1[...] = value
        ec[...] = low(value)
        x_total[...] = jnp.zeros_like(x_total)
        grad_tokens[...] = jnp.zeros_like(grad_tokens)
        keys_padded[count:] = jnp.zeros_like(keys_padded[count:])
        for i in range(2):
            grads[i, count:] = jnp.zeros_like(grads[i, count:])
        rows_padded[count:] = jnp.zeros_like(rows_padded[count:])
        fill_valid(valid, where, parts)

    grad_mixed = low(by_rows(ec, o))
    keys_padded[:count] = ck[...]
    dq, dk, dv = attend_back(
        cq, ck, cv, keys_padded[...].T, co[...], grad_mixed, logs[0], probs, grads, valid[...], count
    )
    dq = low(dq)
    rows_padded[:count, :BLOCK] = low(dk)
    rows_padded[:count, BLOCK:] = low(dv)
    x_total[...] += dot_nt(dq, stacked(q, 0))
    grad_tokens[...] += dot_nt(
        rows_padded[:count],
        jnp.concatenate([stacked(k, 0), stacked(v, 0)], axis=1),
    )

    def products():
        query = low(dot(normed_turned[...], dq))
        pair = low(dot(turned[...], rows_padded[...]))
        flat = low(dot(co[...].T, ec[...]))
        blocks = [query[part(i)] for i in range(4)]
        blocks += [pair[part(i), part(j)] for j in range(2) for i in range(3)]
        return blocks + [flat[:, part(i)] for i in range(4)]

    numbers = [Q_CROSS + i * 4 + n for i in range(4)]
    numbers += [base + i * 4 + n for base in (K_CROSS, V_CROSS) for i in range(3)]
    numbers += [O_CROSS + n * 4 + i for i in range(4)]
    keep_blocks(products, stage, sems, store, where, numbers)

    @pl.when(n == 3)
    def last():
        half = grad_own.shape[0]
        grad_own[...] = grad_tokens[:half]
        grad_others[...] = low(grad_tokens[half:])
        grad_x[...] = g1[...] + norm_back(x[...].astype(WIDE), of_row(shifts, where, 1), x_total[...])


def shape(*dims, kind=LOW):
    return jax.ShapeDtypeStruct(dims, kind)


def call(kernel, grid, where, ins, outs, scratch, products, aliases=None, room=ROOM):
    moved = BLOCK * BLOCK * 2 * grid * 16
    return pl.pallas_call(
        kernel,
        grid_spec=pltpu.PrefetchScalarGridSpec(
            num_scalar_prefetch=1,
            grid=(grid,),
            in_specs=[spec for _, spec in ins],
            out_specs=[spec for _, spec in outs],
            scratch_shapes=scratch,
        ),
        out_shape=[struct for struct, _ in outs],
        input_output_aliases=aliases or {},
        compiler_params=pltpu.CompilerParams(vmem_limit_bytes=room),
        cost_estimate=pl.CostEstimate(
            flops=int(2 * products), bytes_accessed=moved, transcendentals=0
        ),
    )(where, *[array for array, _ in ins])


def full(array):
    return (array, whole(array.shape, pl.Buffered(1)))


def of_object(modulation):
    return full(modulation)


def made(*dims, kind=LOW):
    return (shape(*dims, kind=kind), whole(dims))


def striped(height):
    return (shape(height, D), stripe(height))


LOG_SPEC = pl.BlockSpec((1, 8, TOK_DEV), lambda n, where: (n, 0, 0))
ANYWHERE = pl.BlockSpec(memory_space=pl.ANY)


def padded_to(count):
    return -(-count // 128) * 128


def cross_forward(where, store, x, n1, tokens, shifts, parts):
    here, count = x.shape[0], tokens.shape[0]
    padded = padded_to(count)
    specs = columns(Q_CROSS, 4, 4) + columns(K_CROSS, 3, 4) + columns(V_CROSS, 3, 4) + rows(O_CROSS, 4)
    return call(
        functools.partial(cross_forward_kernel, parts),
        4,
        where,
        [full(x), full(n1), full(tokens), of_object(shifts)] + [(store, spec) for spec in specs],
        [
            striped(here),
            striped(count),
            striped(count),
            striped(here),
            (shape(4, 8, here, kind=WIDE), LOG_SPEC),
            made(here, D, kind=WIDE),
            made(here, D),
        ],
        [
            pltpu.VMEM((here, D), WIDE),
            pltpu.VMEM((padded, BLOCK), LOW),
            pltpu.VMEM((4, padded, here), LOW),
            pltpu.VMEM((count, 128), WIDE),
        ],
        here * D * D * 12,
    )


def tall(here):
    return pl.BlockSpec((BLOCK, here), lambda n, where: (n, 0))


def self_own(where, store, mine):
    here = mine.shape[0]
    specs = columns(Q_SELF, 4, 4) + columns(K_SELF, 4, 4) + columns(V_SELF, 4, 4)
    return call(
        self_own_kernel,
        4,
        where,
        [full(mine)] + [(store, spec) for spec in specs],
        [
            made(D, here),
            striped(here),
            striped(here),
            striped(here),
            (shape(D, here, kind=WIDE), tall(here)),
            (shape(4, 8, here, kind=WIDE), LOG_SPEC),
        ],
        [pltpu.VMEM((4, here, here), LOW)],
        here * D * D * 6,
    )


def self_other(where, store, x1, other, shifts, sq, mix, stats):
    here = x1.shape[0]
    specs = columns(K_SELF, 4, 4) + columns(V_SELF, 4, 4) + rows(O_SELF, 4)
    return call(
        self_other_kernel,
        4,
        where,
        [full(x1), full(other), of_object(shifts), (sq, stripe(here)), (mix, tall(here)), (stats, LOG_SPEC)]
        + [(store, spec) for spec in specs],
        [
            made(D, here),
            striped(here),
            striped(here),
            striped(here),
            (shape(4, 8, here, kind=WIDE), LOG_SPEC),
            made(here, D, kind=WIDE),
            made(here, D),
        ],
        [pltpu.VMEM((here, D), WIDE), pltpu.VMEM((4, here, here), LOW)],
        here * D * D * 6,
    )


def feed_specs(height):
    wide = FF // BLOCK
    up = [
        pl.BlockSpec(
            (1, BLOCK, BLOCK),
            lambda n, where, i=i, j=j: (where[W_UP + i * wide + n * height + j], 0, 0),
        )
        for i in range(4)
        for j in range(height)
    ]
    down = [
        pl.BlockSpec(
            (1, BLOCK, BLOCK), lambda n, where, i=i: (where[W_DOWN + n * height * 4 + i], 0, 0)
        )
        for i in range(4 * height)
    ]
    return up, down


def broad(here, height):
    return pl.BlockSpec((here, height * BLOCK), lambda n, where: (0, n))


def feed_early(where, store, cotangent):
    here = cotangent.shape[0]
    return call(
        feed_early_kernel,
        FF // BLOCK // 4,
        where,
        [full(cotangent)] + [(store, spec) for spec in feed_specs(4)[1]],
        [(shape(here, FF, kind=WIDE), broad(here, 4))],
        [],
        here * D * FF,
    )[0]


def feed(where, store, x2, n3, cotangent, shifts, grad_act):
    here = x2.shape[0]
    up, down = feed_specs(4)
    return call(
        feed_kernel,
        FF // BLOCK // 4,
        where,
        [full(x2), full(n3), full(cotangent), of_object(shifts), (grad_act, broad(here, 4))]
        + [(store, spec) for spec in up + down],
        [
            made(here, D),
            made(here, D, kind=WIDE),
            (shape(here, FF), broad(here, 4)),
            (shape(here, FF), broad(here, 4)),
        ],
        [pltpu.VMEM((here, D), WIDE), pltpu.VMEM((here, D), WIDE)],
        here * D * FF * 3,
    )


def feed_late(where, n3, cotangent, act, eh, slots):
    here = n3.shape[0]
    return call(
        feed_late_kernel,
        FF // BLOCK // 2,
        where,
        [full(n3), full(cotangent), (act, broad(here, 2)), (eh, broad(here, 2))],
        [(shape(slots, BLOCK, BLOCK), ANYWHERE)],
        [
            pltpu.VMEM((D, here), LOW),
            pltpu.VMEM((2, 16, BLOCK, BLOCK), LOW),
            pltpu.SemaphoreType.DMA((2, 16)),
        ],
        here * D * FF * 2,
    )[0]


def self_backward(where, store, g2, sq, k_own, k_other, v_own, v_other, so, logs):
    here = g2.shape[0]
    specs = columns(Q_SELF, 4, 4) + columns(K_SELF, 4, 4) + columns(V_SELF, 4, 4) + rows(O_SELF, 4)
    ins = [full(g2)] + [(a, stripe(here)) for a in (sq, k_own, k_other, v_own, v_other, so)]
    ins += [(logs, LOG_SPEC)] + [(store, spec) for spec in specs]
    return call(
        self_backward_kernel,
        4,
        where,
        ins,
        [made(here, D, kind=WIDE), made(here, D), striped(here), striped(2 * here), striped(2 * here)],
        [
            pltpu.VMEM((here, D), LOW),
            pltpu.VMEM((2, 2 * here, 2 * here), LOW),
            pltpu.VMEM((2, 2 * here, 2 * here), LOW),
            pltpu.VMEM((2 * here, BLOCK), LOW),
            pltpu.VMEM((2 * here, BLOCK), LOW),
            pltpu.VMEM((here, D), WIDE),
            pltpu.VMEM((here, D), WIDE),
        ],
        here * D * D * 16,
    )


def self_late(where, grads, g2, own_turned, other_turned, dq, dk, dv, so):
    here = g2.shape[0]
    ins = [full(a) for a in (g2, own_turned, other_turned)]
    ins += [(a, stripe(a.shape[0])) for a in (dq, dk, dv, so)] + [(grads, ANYWHERE)]
    return call(
        self_late_kernel,
        4,
        where,
        ins,
        [(shape(*grads.shape), ANYWHERE)],
        [
            pltpu.VMEM((here, D), LOW),
            pltpu.VMEM((D, 2 * here), LOW),
            pltpu.VMEM((2, 16, BLOCK, BLOCK), LOW),
            pltpu.SemaphoreType.DMA((2, 16)),
        ],
        here * D * D * 6,
        {len(ins): 0},
    )[0]


def cross_backward(
    where, store, grads, x, g2, x1, own_back, got_back, turned, shifts, normed_turned, cq, ck, cv, co, logs, parts
):
    here, count = x.shape[0], ck.shape[0]
    padded = padded_to(count)
    specs = columns(Q_CROSS, 4, 4) + columns(K_CROSS, 3, 4) + columns(V_CROSS, 3, 4) + rows(O_CROSS, 4)
    ins = [full(a) for a in (x, g2, x1, own_back, got_back, turned)]
    ins += [of_object(shifts), full(normed_turned)]
    ins += [(a, stripe(a.shape[0])) for a in (cq, ck, cv, co)] + [(logs, LOG_SPEC)]
    ins += [(store, spec) for spec in specs] + [(grads, ANYWHERE)]
    return call(
        functools.partial(cross_backward_kernel, parts),
        4,
        where,
        ins,
        [
            made(here, D, kind=WIDE),
            made(count // parts, DIMG, kind=WIDE),
            made(count - count // parts, DIMG),
            (shape(*grads.shape), ANYWHERE),
        ],
        [
            pltpu.VMEM((count, DIMG), WIDE),
            pltpu.VMEM((here, D), LOW),
            pltpu.VMEM((here, D), WIDE),
            pltpu.VMEM((2, padded, 2 * here), LOW),
            pltpu.VMEM((2, padded, 2 * here), LOW),
            pltpu.VMEM((here, D), WIDE),
            pltpu.VMEM((padded, BLOCK), LOW),
            pltpu.VMEM((padded, 2 * BLOCK), LOW),
            pltpu.VMEM((count, 128), WIDE),
            pltpu.VMEM((2, 14, BLOCK, BLOCK), LOW),
            pltpu.SemaphoreType.DMA((2, 14)),
        ],
        here * D * D * 24,
        {len(ins): 3},
        room=40 * 1024 * 1024,
    )


def hand_on_kernel(*refs):
    count = len(refs) // 2
    for source, target in zip(refs[:count], refs[count:]):
        target[...] = source[...]


def hand_on(arrays):
    specs = [
        pl.BlockSpec((a.shape[0] // 4,) + a.shape[1:], lambda i: (i, 0, 0)) for a in arrays
    ]
    return pl.pallas_call(
        hand_on_kernel,
        grid=(4,),
        out_shape=[jax.ShapeDtypeStruct(a.shape, a.dtype) for a in arrays],
        in_specs=specs,
        out_specs=specs,
        compiler_params=pltpu.CompilerParams(vmem_limit_bytes=VLIM),
    )(*arrays)


def partner(block, axis):
    size = lax.axis_size(axis)
    return lax.ppermute(block, axis, [(i, i ^ 1) for i in range(size)])


def soap_update(
    slot_grads,
    first_moment,
    second_moment,
    left_basis,
    right_basis,
    master_weights,
    slot_rates,
    slot_used,
):
    keep_mask = slot_used[:, None, None] > 0.0
    slot_grads = jnp.where(keep_mask, slot_grads, 0.0)
    rotated = jnp.matmul(
        jnp.matmul(jnp.swapaxes(left_basis, 1, 2), slot_grads, precision=highest),
        right_basis,
        precision=highest,
    )
    first_new = moment_decay * first_moment + (1.0 - moment_decay) * rotated
    second_new = moment_decay * second_moment + (1.0 - moment_decay) * rotated * rotated
    correction = 1.0 - moment_decay**STEP
    normalized = first_new / correction / (jnp.sqrt(second_new / correction) + 1e-08)
    rotated_back = jnp.matmul(
        jnp.matmul(left_basis, normalized, precision=highest),
        jnp.swapaxes(right_basis, 1, 2),
        precision=highest,
    )
    fresh_master = master_weights - slot_rates[:, None, None] * (
        rotated_back + 0.01 * master_weights
    )
    fresh_master = jnp.where(keep_mask, fresh_master, 0.0)
    return (
        slot_grads,
        jnp.where(keep_mask, first_new, 0.0),
        jnp.where(keep_mask, second_new, 0.0),
        fresh_master,
        fresh_master.astype(jnp.bfloat16),
    )


def shards(
    triplane,
    cotangent,
    image_tokens,
    modulation,
    image_counts,
    owner_slots,
    master_weights,
    first_moment,
    second_moment,
    left_basis,
    right_basis,
):
    img_size = lax.axis_size("img")
    rows_size = lax.axis_size("rows")
    img_index = lax.axis_index("img")
    flat_index = lax.axis_index("rows") * img_size + img_index
    object_index = flat_index // 2
    pair_index = img_index // 2
    groups = img_size // 2
    slot_cap = image_tokens.shape[0] // groups
    own_count = master_weights.shape[0]
    slot_total = rows_size * img_size * own_count
    fits = rows_size == 16 and img_size == 2 and own_count == 8
    modulation = jnp.swapaxes(modulation, 0, 1)
    info = [object_index[None], image_counts[object_index][None]]
    if img_size == 2:
        info += [img_index[None], 1 - img_index[None]]
    else:
        info += [jnp.arange(img_size, dtype=jnp.int32)]
    if fits:
        store, tokens, tokens_turned, n1, n1_turned = gather(
            master_weights, image_tokens, triplane, modulation
        )
        store = store.reshape(-1, BLOCK, BLOCK)
        where = [positions(owner_slots, WAYS_OUT), positions(owner_slots, WAYS_IN)]
    else:
        store = lax.all_gather(master_weights.astype(LOW), ("rows", "img"), axis=0, tiled=True)
        where = [owner_slots, owner_slots]
        if img_size == 2:
            tokens = jnp.concatenate([image_tokens, partner(image_tokens, "img")], 0)
        else:
            tokens = lax.all_gather(image_tokens, "img", axis=0, tiled=True)
            tokens = tokens.reshape(img_size, groups, slot_cap, DIMG)
            tokens = lax.dynamic_index_in_dim(tokens, pair_index, 1, keepdims=False)
            tokens = tokens.reshape(img_size * slot_cap, DIMG)
        count = tokens.shape[0]
        tokens_turned = jnp.pad(tokens.T, ((0, 0), (0, padded_to(count) - count)))
        shifts = lax.dynamic_index_in_dim(modulation, object_index, 1, keepdims=False)
        n1 = low(modulated_norm(triplane.astype(WIDE), shifts[0], shifts[1]))
        n1_turned = n1.T
    where = jnp.concatenate([piece.astype(jnp.int32) for piece in where + info])

    cq, ck, cv, co, cross_logs, x1, n2 = cross_forward(
        where, store, triplane, n1, tokens, modulation, img_size
    )
    n2_other = partner(n2, "img")
    own_turned, sq, k_own, v_own, mix, stats = self_own(where, store, n2)
    grad_act = feed_early(where, store, cotangent)
    other_turned, k_other, v_other, so, self_logs, x2, n3 = self_other(
        where, store, x1, n2_other, modulation, sq, mix, stats
    )
    layer_out, g2, act, eh = feed(where, store, x2, n3, cotangent, modulation, grad_act)
    own_back, other_back, dq, dk, dv = self_backward(
        where, store, g2, sq, k_own, k_other, v_own, v_other, so, self_logs
    )
    got_back = partner(other_back, "img")
    grads = feed_late(where, n3, cotangent, act, eh, slot_total)
    grads = self_late(where, grads, g2, own_turned, other_turned, dq, dk, dv, so)
    grad_triplane, grad_own, grad_others, grads = cross_backward(
        where,
        store,
        grads,
        triplane,
        g2,
        x1,
        own_back,
        got_back,
        tokens_turned,
        modulation,
        n1_turned,
        cq,
        ck,
        cv,
        co,
        cross_logs,
        img_size,
    )
    if img_size == 2:
        grad_image = grad_own + partner(grad_others, "img").astype(WIDE)
    else:
        pick = (jnp.arange(groups, dtype=jnp.int32) == pair_index).astype(WIDE)
        grad_tokens = jnp.concatenate([grad_own, grad_others.astype(WIDE)], 0)
        spread = grad_tokens.reshape(img_size, 1, slot_cap, DIMG) * pick[None, :, None, None]
        grad_image = lax.psum_scatter(
            spread.reshape(img_size * groups * slot_cap, DIMG).astype(LOW),
            "img",
            scatter_dimension=0,
            tiled=True,
        ).astype(WIDE)
    my_slots = flat_index * own_count + jnp.arange(own_count, dtype=jnp.int32)
    matched = (owner_slots[:, None] == my_slots[None, :]).astype(WIDE)
    slot_used = jnp.sum(matched, axis=0)
    slot_rates = jnp.sum(matched * jnp.asarray(block_table(weight_scales()))[:, None], axis=0)
    state = (first_moment, second_moment, left_basis, right_basis, master_weights)
    if fits:
        rates = jnp.broadcast_to(
            jnp.stack([slot_rates, slot_used], 1)[:, :, None], (own_count, 2, BLOCK)
        )
        updated = hand_on(scatter(grads.reshape(2, 8, 16, BLOCK, BLOCK), *state, rates))
    else:
        used = jnp.zeros((slot_total,), jnp.bool_).at[owner_slots].set(True)
        grads = jnp.where(used[:, None, None], grads, jnp.zeros_like(grads))
        slot_grads = lax.psum_scatter(
            grads, ("rows", "img"), scatter_dimension=0, tiled=True
        ).astype(WIDE)
        updated = soap_update(slot_grads, *state, slot_rates, slot_used)
    return (layer_out, grad_triplane, grad_image) + tuple(updated)


def solution(mesh):
    flat = P(("rows", "img"), None)
    blocks = P(("rows", "img"), None, None)
    in_specs = (flat, flat, flat, P(), P(), P()) + (blocks,) * 5
    out_specs = (flat, flat, flat) + (blocks,) * 5
    return jax.shard_map(shards, mesh=mesh, in_specs=in_specs, out_specs=out_specs, check_vma=False)
```

```python
import functools

import jax
import jax.numpy as jnp
import numpy as np
from jax import lax
from jax.experimental import pallas as pl
from jax.experimental.pallas import tpu as pltpu
from jax.sharding import PartitionSpec as P

D = 1024
HEADS = 16
FF = 4096
DIMG = 768
TOK_DEV = 384
IMG_MAX = 1025
BLOCK = 256
STEP = 5
HEAD = D // HEADS

MESH = pl.DeviceIdType.MESH
VLIM = 60 * 1024 * 1024
WAYS_OUT = (
    ('lo', 'hi', 'y', 'x'),
    ('hi', 'lo', 'x', 'y'),
    ('y', 'x', 'hi', 'lo'),
    ('hi', 'lo', 'x', 'y'),
    ('hi', 'x', 'lo', 'y'),
    ('lo', 'y', 'hi', 'x'),
    ('hi', 'y', 'lo', 'x'),
    ('hi', 'x', 'y', 'lo'),
)
WAYS_IN = (
    ('lo', 'y', 'hi', 'x'),
    ('hi', 'x', 'y', 'lo'),
    ('hi', 'y', 'x', 'lo'),
    ('hi', 'lo', 'x', 'y'),
    ('hi', 'x', 'lo', 'y'),
    ('hi', 'y', 'lo', 'x'),
    ('hi', 'lo', 'x', 'y'),
    ('lo', 'hi', 'y', 'x'),
)
FRONT = 17
ORDER_OUT = (
    (6, 0), (2, 0), (2, 1), (0, 0), (5, 0), (3, 0), (6, 1), (-1, 0),
    (3, 1), (1, 0), (5, 1), (4, 0), (1, 1), (3, 2), (4, 1), (0, 1),
    (0, 2), (6, 2), (7, 0), (7, 1), (4, 2), (3, 3), (5, 2), (0, 3),
    (7, 2), (3, 4), (1, 2), (7, 3), (6, 3), (5, 3), (2, 2), (4, 3),
    (0, 4), (7, 4), (2, 3), (4, 4), (1, 3), (6, 4), (1, 4), (5, 4),
    (2, 4),
)
ORDER_IN = (
    (0, 0), (1, 0), (2, 0), (3, 0), (4, 0), (5, 0), (6, 0), (7, 0),
    (1, 1), (0, 1), (4, 1), (0, 2), (7, 1), (4, 2), (6, 1), (2, 1),
    (7, 2), (5, 1), (5, 2), (6, 2), (1, 2), (0, 3), (7, 3), (6, 3),
    (1, 3), (3, 1), (1, 4), (4, 3), (7, 4), (2, 2), (4, 4), (2, 3),
    (6, 4), (3, 2), (0, 4), (5, 3), (4, 5), (6, 5), (2, 4), (7, 5),
    (3, 3), (2, 5), (5, 4), (1, 5), (0, 5), (5, 5), (3, 4), (3, 5),
)


def coords():
    row = lax.axis_index("rows")
    rest = lax.rem(row, 4)
    return lax.div(row, 4), lax.div(rest, 2), lax.rem(rest, 2), lax.axis_index("img")


def neighbour(kind):
    z, x, c, y = coords()
    if kind == "c":
        c = 1 - c
    if kind == "x":
        x = 1 - x
    if kind == "y":
        y = 1 - y
    if kind == "lo":
        z = z + 1 - 2 * lax.rem(z, 2)
    if kind == "hi":
        z = lax.rem(z + 2, 4)
    return (z * 4 + x * 2 + c, y)


def place(way):
    z, x, c, y = coords()
    bits = {"x": x, "y": y, "lo": lax.rem(z, 2), "hi": lax.div(z, 2)}
    return sum(bits[kind] * 2**k for k, kind in enumerate(way))


def positions(slot, ways):
    owner, j = slot // 8, slot % 8
    z, x, c, y = owner // 8, owner // 4 % 2, owner // 2 % 2, owner % 2
    bits = {"x": x, "y": y, "lo": z % 2, "hi": z // 2}
    total = (c * 8 + j) * 16
    for kind, bit in bits.items():
        total = total + bit * jnp.asarray([2 ** way.index(kind) for way in ways], jnp.int32)[j]
    return total


def greet():
    barrier = pltpu.get_barrier_semaphore()
    for kind in ("c", "x", "y", "lo", "hi"):
        pl.semaphore_signal(barrier, inc=1, device_id=neighbour(kind), device_id_type=MESH)
    pl.semaphore_wait(barrier, 5)


def gather_kernel(
    master, tokens, triplane, modulation, out, both, turned, n1, n1_turned,
    own, wide, mine, x, shifts, others, spread, upright, lsem, csem, ssem, rsem, tsem,
):
    c = coords()[2]
    early = [
        pltpu.make_async_copy(source, target, lsem.at[i])
        for i, (source, target) in enumerate(
            ((master, wide), (tokens, mine), (triplane, x), (modulation, shifts))
        )
    ]
    for copy in early:
        copy.start()
    greet()
    cross = pltpu.make_async_remote_copy(
        tokens, others, tsem.at[0], tsem.at[1], device_id=neighbour("y"), device_id_type=MESH
    )
    early[0].wait()
    copies, keeps = {}, {}

    def start(j, k):
        base = place(WAYS_OUT[j])
        count = 2**k
        first = lax.div(base, count) * count if k < 4 else 0
        here = pl.ds(first, count)
        source = own.at[pl.ds(j, 1)] if k == 0 else out.at[c, j, here]
        copy = pltpu.make_async_remote_copy(
            source,
            out.at[c, j, here],
            ssem.at[j, k],
            rsem.at[j, k],
            device_id=neighbour((WAYS_OUT[j] + ("c",))[k]),
            device_id_type=MESH,
        )
        copy.start()
        copies[j, k] = copy

    for j, k in ORDER_OUT:
        if j < 0:
            cross.start()
        elif k == 0:
            own[j] = wide[j].astype(jnp.bfloat16)
            start(j, 0)
            keep = pltpu.make_async_copy(
                own.at[pl.ds(j, 1)], out.at[c, j, pl.ds(place(WAYS_OUT[j]), 1)], csem.at[j]
            )
            keep.start()
            keeps[j] = keep
        else:
            if k == 1:
                keeps[j].wait()
            copies[j, k - 1].wait_recv()
            start(j, k)
        if (j, k) == ORDER_OUT[FRONT]:
            row = pl.ds(lax.axis_index("rows"), 1)
            early[2].wait()
            early[3].wait()
            one = modulated_norm(
                x[...].astype(jnp.float32), shifts[0, row], shifts[1, row]
            )
            n1[...] = one.astype(jnp.bfloat16)
            n1_turned[...] = one.astype(jnp.bfloat16).T
        if (j, k) == ORDER_OUT[min(max(FRONT + 6, ORDER_OUT.index((-1, 0)) + 9), len(ORDER_OUT) - 1)]:
            half = tokens.shape[0]
            cross.wait()
            early[1].wait()
            spread[:half] = mine[...].astype(jnp.float32)
            spread[half:] = others[...].astype(jnp.float32)
            both[...] = spread[...].astype(jnp.bfloat16)
            upright[2 * half :] = jnp.zeros_like(upright[2 * half :])
            for i in range(tokens.shape[1] // BLOCK):
                lanes = slice(i * BLOCK, (i + 1) * BLOCK)
                upright[: 2 * half] = both[:, lanes]
                turned[lanes] = upright[...].T
    for j in range(8):
        copies[j, 4].wait_recv()
    for copy in copies.values():
        copy.wait_send()


def gather(master, tokens, x, modulation):
    anywhere, inside = pl.BlockSpec(memory_space=pl.ANY), pl.BlockSpec(memory_space=pltpu.VMEM)
    half, width = tokens.shape
    padded = -(-2 * half // 128) * 128
    bf = jnp.bfloat16
    return pl.pallas_call(
        gather_kernel,
        out_shape=[
            jax.ShapeDtypeStruct((2, 8, 16, BLOCK, BLOCK), bf),
            jax.ShapeDtypeStruct((2 * half, width), bf),
            jax.ShapeDtypeStruct((width, padded), bf),
            jax.ShapeDtypeStruct(x.shape, bf),
            jax.ShapeDtypeStruct(x.shape[::-1], bf),
        ],
        in_specs=[anywhere] * 4,
        out_specs=[anywhere] + [inside] * 4,
        scratch_shapes=[
            pltpu.VMEM((8, BLOCK, BLOCK), bf),
            pltpu.VMEM((8, BLOCK, BLOCK), jnp.float32),
            pltpu.VMEM((half, width), bf),
            pltpu.VMEM(x.shape, bf),
            pltpu.VMEM(modulation.shape, jnp.float32),
            pltpu.VMEM((half, width), bf),
            pltpu.VMEM((2 * half, width), jnp.float32),
            pltpu.VMEM((padded, BLOCK), bf),
            pltpu.SemaphoreType.DMA((4,)),
            pltpu.SemaphoreType.DMA((8,)),
            pltpu.SemaphoreType.DMA((8, 5)),
            pltpu.SemaphoreType.DMA((8, 5)),
            pltpu.SemaphoreType.DMA((2,)),
        ],
        compiler_params=pltpu.CompilerParams(
            collective_id=11, has_side_effects=True, vmem_limit_bytes=VLIM
        ),
    )(master, tokens, x, modulation)


def times(a, b, left, right):
    return lax.dot_general(
        a,
        b,
        (((left,), (right,)), ((), ())),
        precision=lax.Precision.HIGHEST,
        preferred_element_type=jnp.float32,
    )


def scatter_kernel(grads, first, second, left, right, master, rates, *rest):
    outs = rest[:5]
    own, r0, r1, r2, r3, r4, held, made, made_low, lsem, ssem, rsem, hsem, osem = rest[5:]
    c = coords()[2]
    got = (r0, r1, r2, r3, r4)
    loads, copies, fetches, puts = [], {}, {}, {}
    for j in range(8):
        load = pltpu.make_async_copy(grads.at[c, j], own.at[j], lsem.at[j])
        load.start()
        loads.append(load)
    greet()

    def exchange(j, s, source, kind):
        copy = pltpu.make_async_remote_copy(
            source,
            got[s].at[j],
            ssem.at[j, s],
            rsem.at[j, s],
            device_id=neighbour(kind),
            device_id_type=MESH,
        )
        copy.start()
        copies[j, s] = copy

    def add(j, s):
        count = 16 >> s
        start = lax.div(place(WAYS_IN[j]), count) * count if s else 0

        def body(b, carry):
            own[j, start + b] = own[j, start + b] + got[s][j, b]
            return carry

        lax.fori_loop(0, count, body, 0)

    def send(j, s):
        count = 16 >> s
        half = lax.div(place(WAYS_IN[j]), count)
        other = (half + 1 - 2 * lax.rem(half, 2)) * count
        exchange(j, s, own.at[j, pl.ds(other, count)], WAYS_IN[j][4 - s])

    def fetch(turn, j):
        side = turn % 2
        fetches[turn] = [
            pltpu.make_async_copy(array.at[j], held.at[side, i], hsem.at[side, i])
            for i, array in enumerate((first, second, left, right, master))
        ]
        for copy in fetches[turn]:
            copy.start()

    def finish(turn, j):
        side = turn % 2
        for copy in fetches[turn]:
            copy.wait()
        if turn >= 2:
            for copy in puts[turn - 2]:
                copy.wait()
        base = place(WAYS_IN[j])
        used = rates[j, 1:2] > 0.0
        total = own[j, base].astype(jnp.float32) + r4[j, 0].astype(jnp.float32)
        total = jnp.where(used, total, 0.0)
        rotated = times(times(held[side, 2], total, 0, 0), held[side, 3], 1, 0)
        new_first = 0.5 * held[side, 0] + 0.5 * rotated
        new_second = 0.5 * held[side, 1] + 0.5 * rotated * rotated
        fix = 1.0 - 0.5**STEP
        unit = (new_first / fix) / (jnp.sqrt(new_second / fix) + 1e-08)
        update = times(times(held[side, 2], unit, 1, 0), held[side, 3], 1, 1)
        old = held[side, 4]
        new = jnp.where(used, old - rates[j, 0:1] * (update + 0.01 * old), 0.0)
        made[side, 0] = total
        made[side, 1] = jnp.where(used, new_first, 0.0)
        made[side, 2] = jnp.where(used, new_second, 0.0)
        made[side, 3] = new
        made_low[side] = new.astype(jnp.bfloat16)
        puts[turn] = [
            pltpu.make_async_copy(made.at[side, i], outs[i].at[j], osem.at[side, i])
            for i in range(4)
        ] + [pltpu.make_async_copy(made_low.at[side], outs[4].at[j], osem.at[side, 4])]
        for copy in puts[turn]:
            copy.start()

    ends = [j for j, s in ORDER_IN if s == 5]
    for turn in range(2):
        fetch(turn, ends[turn])
    turn = 0
    for j, s in ORDER_IN:
        if s == 0:
            exchange(j, 0, grads.at[1 - c, j], "c")
            continue
        if s == 1:
            loads[j].wait()
        copies[j, s - 1].wait_recv()
        if s < 5:
            add(j, s - 1)
            send(j, s)
        else:
            finish(turn, j)
            if turn < 6:
                fetch(turn + 2, ends[turn + 2])
            turn += 1
    for copy in puts[6] + puts[7]:
        copy.wait()
    for copy in copies.values():
        copy.wait_send()


def scatter(grads, first, second, left, right, master, rates):
    bf, wide, block = jnp.bfloat16, jnp.float32, (BLOCK, BLOCK)
    anywhere = pl.BlockSpec(memory_space=pl.ANY)
    return pl.pallas_call(
        scatter_kernel,
        out_shape=[jax.ShapeDtypeStruct((8,) + block, kind) for kind in (wide,) * 4 + (bf,)],
        in_specs=[anywhere] * 6 + [pl.BlockSpec(memory_space=pltpu.VMEM)],
        out_specs=[anywhere] * 5,
        scratch_shapes=[pltpu.VMEM((8, count) + block, bf) for count in (16, 16, 8, 4, 2, 1)]
        + [
            pltpu.VMEM((2, 5) + block, wide),
            pltpu.VMEM((2, 4) + block, wide),
            pltpu.VMEM((2,) + block, bf),
            pltpu.SemaphoreType.DMA((8,)),
            pltpu.SemaphoreType.DMA((8, 5)),
            pltpu.SemaphoreType.DMA((8, 5)),
            pltpu.SemaphoreType.DMA((2, 5)),
            pltpu.SemaphoreType.DMA((2, 5)),
        ],
        compiler_params=pltpu.CompilerParams(
            collective_id=12, has_side_effects=True, vmem_limit_bytes=54 * 1024 * 1024
        ),
    )(grads, first, second, left, right, master, rates)


highest = lax.Precision.HIGHEST
moment_decay = 0.5
LOW = jnp.bfloat16
WIDE = jnp.float32

def shapes_list():
    return [(D, D), (DIMG, D), (DIMG, D), (D, D), (D, D), (D, D), (D, D), (D, D), (D, FF), (FF, D)]


Q_CROSS, K_CROSS, V_CROSS, O_CROSS, Q_SELF, K_SELF, V_SELF, O_SELF, W_UP, W_DOWN = (
    int(v) for v in np.cumsum([0] + [a * b // BLOCK**2 for a, b in shapes_list()])[:10]
)


NBLK = W_DOWN + FF * D // BLOCK**2


def weight_scales():
    self_root = (2.0 * TOK_DEV) ** 0.5
    cross_root = (IMG_MAX / 2.0) ** 0.5
    return [
        D ** (-0.5),
        DIMG ** (-0.5),
        DIMG ** (-0.5),
        0.5 * cross_root * D ** (-0.5),
        D ** (-0.5),
        D ** (-0.5),
        D ** (-0.5),
        0.5 * self_root * D ** (-0.5),
        D ** (-0.5),
        2.0 * FF ** (-0.5),
    ]


def block_table(scales):
    pieces = []
    for shape_pair, scale_value in zip(shapes_list(), scales):
        amount = shape_pair[0] * shape_pair[1] // (BLOCK * BLOCK)
        pieces.append(np.full((amount,), scale_value, np.float32))
    return np.concatenate(pieces)


def low(v):
    return v.astype(LOW)


def dot(a, b):
    return jnp.dot(a, b, preferred_element_type=WIDE)


def dot_nt(a, b):
    return lax.dot_general(a, b, (((1,), (1,)), ((), ())), preferred_element_type=WIDE)


def part(k):
    return slice(k * BLOCK, (k + 1) * BLOCK)


def norm_parts(values):
    centered = values - jnp.mean(values, axis=-1, keepdims=True)
    variance = jnp.mean(centered * centered, axis=-1, keepdims=True)
    return centered, lax.rsqrt(variance + 1e-06)


def modulated_norm(values, shift, scale):
    centered, inverse = norm_parts(values)
    return centered * inverse * (1.0 + scale) + shift


def norm_back(values, scale, grad_normed):
    centered, inverse = norm_parts(values)
    unit = centered * inverse
    grad_unit = grad_normed * (1.0 + scale)
    return inverse * (
        grad_unit
        - jnp.mean(grad_unit, axis=-1, keepdims=True)
        - unit * jnp.mean(grad_unit * unit, axis=-1, keepdims=True)
    )


def halves(pair):
    lane = lax.broadcasted_iota(jnp.int32, pair.shape, 1)
    zero = jnp.zeros_like(pair)
    return jnp.where(lane < HEAD, pair, zero), jnp.where(lane < HEAD, zero, pair)


def fill_valid(valid, where, parts):
    cap = valid.shape[0] // parts
    slot = lax.broadcasted_iota(jnp.int32, (cap, 128), 0)
    for i in range(parts):
        number = slot * parts + where[2 * NBLK + 1 + i]
        limit = where[2 * NBLK + 1 + parts + where[2 * NBLK]]
        valid[i * cap : (i + 1) * cap] = (number < limit).astype(WIDE)


def group(n, width):
    return pl.ds(pl.multiple_of(n * width, width), width)


def of_row(shifts, where, k):
    return shifts[k, pl.ds(where[2 * NBLK], 1)]


def masked(scores, valid):
    if valid is None:
        return scores
    wide = jnp.concatenate([valid] * (scores.shape[1] // valid.shape[1]), axis=1)
    return jnp.where(wide > 0.0, scores, -1e30)


def columns(base, tall, wide):
    return [
        pl.BlockSpec((1, BLOCK, BLOCK), lambda n, where, i=i: (where[base + i * wide + n], 0, 0))
        for i in range(tall)
    ]


def rows(base, wide):
    return [
        pl.BlockSpec((1, BLOCK, BLOCK), lambda n, where, k=k: (where[base + n * wide + k], 0, 0))
        for k in range(wide)
    ]


def whole(shape, mode=None):
    return pl.BlockSpec(shape, lambda n, where: (0,) * len(shape), pipeline_mode=mode)


def stripe(height):
    return pl.BlockSpec((height, BLOCK), lambda n, where: (0, n))


def stacked(blocks, axis):
    return jnp.concatenate([block[0] for block in blocks], axis=axis)


def by_columns(left, blocks):
    return dot(left[...], stacked(blocks, 0))


def by_rows(left, blocks):
    return dot_nt(left[...], stacked(blocks, 1))


def attend_part(queries, keys, values_turned, weights, valid, count):
    outs, tops, totals = [], [], []
    tokens = queries.shape[0]
    scores = []
    for pair in range(2):
        lanes = slice(pair * 2 * HEAD, (pair + 1) * 2 * HEAD)
        both = jnp.concatenate(halves(queries[:, lanes]), axis=0)
        scores.append(masked(dot_nt(keys[:count, lanes], both), valid))
    for pair in range(2):
        top = jnp.max(scores[pair], axis=0, keepdims=True)
        exponent = jnp.exp(scores[pair] - top)
        total = jnp.sum(exponent, axis=0, keepdims=True)
        weights[pair, :count] = low(exponent)
        tops += [top[:, :tokens], top[:, tokens:]]
        totals += [total[:, :tokens], total[:, tokens:]]
    for pair in range(2):
        lanes = slice(pair * 2 * HEAD, (pair + 1) * 2 * HEAD)
        mixed = dot(values_turned[lanes], weights[pair])
        outs += [mixed[:HEAD, :tokens], mixed[HEAD:, tokens:]]
    return outs, tops, totals


def attend_end(outs, tops, totals):
    turned = jnp.concatenate([out / total for out, total in zip(outs, totals)], axis=0)
    logs = [top + jnp.log(total) for top, total in zip(tops, totals)]
    return low(turned.T), jnp.concatenate(logs + logs, axis=0)


def attend_back(queries, keys, values, keys_turned, mixed, grad_mixed, logs, probs, grads, valid, count):
    tokens = queries.shape[0]
    inner = (mixed.astype(WIDE) * grad_mixed.astype(WIDE)).T
    inner = jnp.concatenate(
        [jnp.sum(inner[head * HEAD : (head + 1) * HEAD], axis=0, keepdims=True) for head in range(4)],
        axis=1,
    )
    logs = jnp.concatenate([logs[head : head + 1] for head in range(4)], axis=1)
    grad_query, grad_key, grad_value = [], [], []
    for pair in range(2):
        kept = pair % grads.shape[0]
        lanes = slice(pair * 2 * HEAD, (pair + 1) * 2 * HEAD)
        side = slice(pair * 2 * tokens, (pair + 1) * 2 * tokens)
        both_queries = jnp.concatenate(halves(queries[:, lanes]), axis=0)
        both_mixed = jnp.concatenate(halves(grad_mixed[:, lanes]), axis=0)
        scores = masked(dot_nt(keys[:count, lanes], both_queries), valid)
        grad_full = dot_nt(values[:count, lanes], both_mixed)
        full = jnp.exp(scores - logs[:, side])
        grads[kept, :count] = low(full * (grad_full - inner[:, side]))
        probs[kept, :count] = low(full)
        turned = dot(keys_turned[lanes], grads[kept])
        grad_query += [turned[:HEAD, :tokens], turned[HEAD:, tokens:]]
        grad_key.append(dot(grads[kept, :count], both_queries))
        grad_value.append(dot(probs[kept, :count], both_mixed))
    grad_query = jnp.concatenate(grad_query, axis=0).T * HEAD ** (-0.5)
    return grad_query, jnp.concatenate(grad_key, axis=1), jnp.concatenate(grad_value, axis=1)


def send_blocks(stage, sems, side, store, where, numbers):
    return [
        pltpu.make_async_copy(stage.at[side, i], store.at[where[NBLK + number]], sems.at[side, i])
        for i, number in enumerate(numbers)
    ]


def keep_blocks(products, stage, sems, store, where, numbers):
    step, steps = pl.program_id(0), pl.num_programs(0)
    side = lax.rem(step, 2)

    @pl.when(step >= 2)
    def reuse():
        for copy in send_blocks(stage, sems, side, store, where, numbers):
            copy.wait()

    for i, product in enumerate(products()):
        stage[side, i] = product
    for copy in send_blocks(stage, sems, side, store, where, numbers):
        copy.start()

    @pl.when(step == steps - 1)
    def drain():
        for copy in send_blocks(stage, sems, 1 - side, store, where, numbers):
            copy.wait()
        for copy in send_blocks(stage, sems, side, store, where, numbers):
            copy.wait()


def cross_forward_kernel(parts, where, x, n1, tokens, shifts, *rest):
    q, k, v, o = rest[:4], rest[4:7], rest[7:10], rest[10:14]
    cq, ck, cv, co, logs, x1, n2, all_mixed, all_out, turned, weights, valid = rest[14:]
    n = pl.program_id(0)
    count = tokens.shape[0]

    @pl.when(n == 0)
    def first():
        turned[count:] = jnp.zeros_like(turned[count:])
        for pair in range(2):
            weights[pair, count:] = jnp.zeros_like(weights[pair, count:])
        fill_valid(valid, where, parts)

    queries = low(by_columns(n1, q)) * HEAD ** (-0.5)
    cq[...] = queries
    pair = low(dot(tokens[...], jnp.concatenate([stacked(k, 0), stacked(v, 0)], axis=1)))
    ck[...] = pair[:, :BLOCK]
    cv[...] = pair[:, BLOCK:]
    turned[:count] = pair[:, BLOCK:]
    mixed, log_total = attend_end(
        *attend_part(queries, ck, turned[...].T, weights, valid[...], count)
    )
    co[...] = mixed
    logs[0] = log_total
    all_mixed[:, group(n, BLOCK)] = mixed
    all_out[group(n, BLOCK)] = stacked(o, 1)

    @pl.when(n == 3)
    def last():
        after = x[...].astype(WIDE) + dot(all_mixed[...], all_out[...])
        x1[...] = after
        n2[...] = low(modulated_norm(after, of_row(shifts, where, 2), of_row(shifts, where, 3)))


def self_own_kernel(where, mine, *rest):
    q, k, v = rest[:4], rest[4:8], rest[8:12]
    turned, sq, sk, sv, mix, stats, weights = rest[12:]
    n = pl.program_id(0)

    @pl.when(n == 0)
    def first():
        turned[...] = mine[...].T

    all_three = low(
        dot(mine[...], jnp.concatenate([stacked(q, 0), stacked(k, 0), stacked(v, 0)], axis=1))
    )
    queries = all_three[:, :BLOCK] * HEAD ** (-0.5)
    sq[...] = queries
    sk[...] = all_three[:, BLOCK : 2 * BLOCK]
    sv[...] = all_three[:, 2 * BLOCK :]
    outs, tops, totals = attend_part(queries, sk, sv[...].T, weights, None, mine.shape[0])
    mix[...] = jnp.concatenate(outs, axis=0)
    stats[0] = jnp.concatenate(tops + totals, axis=0)


def self_other_kernel(where, x1, other, shifts, sq, mix, stats, *rest):
    k, v, o = rest[:4], rest[4:8], rest[8:12]
    turned, sk, sv, so, logs, x2, n3, all_mixed, all_out, weights = rest[12:]
    n = pl.program_id(0)

    @pl.when(n == 0)
    def first():
        turned[...] = other[...].T

    pair = low(dot(other[...], jnp.concatenate([stacked(k, 0), stacked(v, 0)], axis=1)))
    sk[...] = pair[:, :BLOCK]
    sv[...] = pair[:, BLOCK:]
    parts = attend_part(sq[...], sk, sv[...].T, weights, None, other.shape[0])
    outs, tops, totals = [], [], []
    for head, (out, top, amount) in enumerate(zip(*parts)):
        old_top, old_amount = stats[0, head : head + 1], stats[0, 4 + head : 5 + head]
        new_top = jnp.maximum(top, old_top)
        grow, keep = jnp.exp(top - new_top), jnp.exp(old_top - new_top)
        outs.append(out * grow + mix[head * HEAD : (head + 1) * HEAD] * keep)
        tops.append(new_top)
        totals.append(amount * grow + old_amount * keep)
    mixed, logs[0] = attend_end(outs, tops, totals)
    so[...] = mixed
    all_mixed[:, group(n, BLOCK)] = mixed
    all_out[group(n, BLOCK)] = stacked(o, 1)

    @pl.when(n == 3)
    def last():
        after = x1[...] + dot(all_mixed[...], all_out[...])
        x2[...] = after
        n3[...] = low(modulated_norm(after, of_row(shifts, where, 4), of_row(shifts, where, 5)))


def grid_of(blocks, across):
    return jnp.concatenate(
        [stacked(blocks[i : i + across], 1) for i in range(0, len(blocks), across)], axis=0
    )


def feed_early_kernel(where, cotangent, *rest):
    down, grad_act = rest[:16], rest[16]
    grad_act[...] = dot_nt(cotangent[...], grid_of(down, 4))


def feed_kernel(where, x2, n3, cotangent, shifts, grad_act, *rest):
    up, down = rest[:16], rest[16:32]
    layer_out, g2, act, eh, total, back = rest[32:]
    f = pl.program_id(0)

    @pl.when(f == 0)
    def first():
        total[...] = x2[...]
        back[...] = jnp.zeros_like(back)

    root = (2.0 / np.pi) ** 0.5
    ups = [stacked(up[j::4], 0) for j in range(4)]
    hiddens = [dot(n3[...], ups[j]) for j in range(4)]
    for j, hidden in enumerate(hiddens):
        square = hidden * hidden
        bent = jnp.tanh(hidden * (root + (0.044715 * root) * square))
        gate = 0.5 * bent + 0.5
        value = hidden * gate
        act[:, part(j)] = low(value)
        slope = gate + value * (1.0 - gate) * (2.0 * root + (6.0 * 0.044715 * root) * square)
        eh[:, part(j)] = low(grad_act[:, part(j)] * slope)
    total[...] += dot(act[...], grid_of(down, 4))
    back[...] += dot_nt(eh[...], jnp.concatenate(ups, axis=1))

    @pl.when(f == FF // BLOCK // 4 - 1)
    def last():
        layer_out[...] = low(total[...])
        g2[...] = cotangent[...].astype(WIDE) + norm_back(x2[...], of_row(shifts, where, 5), back[...])


def feed_late_kernel(where, n3, cotangent, act, eh, store, turned, stage, sems):
    f = pl.program_id(0)
    wide = FF // BLOCK

    @pl.when(f == 0)
    def first():
        turned[...] = n3[...].T

    def products():
        up = low(dot(turned[...], eh[...]))
        down = low(dot(act[...].T, cotangent[...]))
        return [up[part(i), part(j)] for j in range(2) for i in range(4)] + [
            down[part(j), part(i)] for j in range(2) for i in range(4)
        ]

    numbers = [W_UP + i * wide + f * 2 + j for j in range(2) for i in range(4)]
    numbers += [W_DOWN + (f * 2 + j) * 4 + i for j in range(2) for i in range(4)]
    keep_blocks(products, stage, sems, store, where, numbers)


def self_backward_kernel(where, g2, sq, k_own, k_other, v_own, v_other, so, logs, *rest):
    q, k, v, o = rest[:4], rest[4:8], rest[8:12], rest[12:16]
    own_back, other_back, dq, dk, dv, es, probs, grads, sk, sv, own_total, other_total = rest[16:]
    n = pl.program_id(0)
    here = g2.shape[0]
    both = 2 * here

    @pl.when(n == 0)
    def first():
        es[...] = low(g2[...])
        own_total[...] = jnp.zeros_like(own_total)
        other_total[...] = jnp.zeros_like(other_total)

    grad_mixed = low(by_rows(es, o))
    sk[:here] = k_own[...]
    sk[here:] = k_other[...]
    sv[:here] = v_own[...]
    sv[here:] = v_other[...]
    wide_dq, wide_dk, wide_dv = attend_back(
        sq, sk, sv, sk[...].T, so[...], grad_mixed, logs[0], probs, grads, None, both
    )
    dq[...] = low(wide_dq)
    dk[...] = low(wide_dk)
    dv[...] = low(wide_dv)
    key_values = jnp.concatenate([stacked(k, 0), stacked(v, 0)], axis=1)
    both_grads = jnp.concatenate([dk[...], dv[...]], axis=1)
    own_total[...] += dot_nt(
        jnp.concatenate([dq[...], both_grads[:here]], axis=1),
        jnp.concatenate([stacked(q, 0), key_values], axis=1),
    )
    other_total[...] += dot_nt(both_grads[here:], key_values)

    @pl.when(n == 3)
    def last():
        own_back[...] = own_total[...]
        other_back[...] = low(other_total[...])


def self_late_kernel(where, g2, own_turned, other_turned, dq, dk, dv, so, old, store, es, turned, stage, sems):
    n = pl.program_id(0)
    here = g2.shape[0]

    @pl.when(n == 0)
    def first():
        es[...] = low(g2[...])
        turned[:, :here] = own_turned[...]
        turned[:, here:] = other_turned[...]

    def products():
        query = low(dot(own_turned[...], dq[...]))
        pair = low(dot(turned[...], jnp.concatenate([dk[...], dv[...]], axis=1)))
        flat = low(dot(so[...].T, es[...]))
        blocks = [query[part(i)] for i in range(4)]
        blocks += [pair[part(i), part(j)] for j in range(2) for i in range(4)]
        return blocks + [flat[:, part(i)] for i in range(4)]

    numbers = [base + i * 4 + n for base in (Q_SELF, K_SELF, V_SELF) for i in range(4)]
    numbers += [O_SELF + n * 4 + i for i in range(4)]
    keep_blocks(products, stage, sems, store, where, numbers)


def cross_backward_kernel(
    parts, where, x, g2, x1, own_back, got_back, turned, shifts, normed_turned, cq, ck, cv, co, logs, *rest
):
    q, k, v, o = rest[:4], rest[4:7], rest[7:10], rest[10:14]
    grad_x, grad_own, grad_others, store, grad_tokens, ec, g1, probs, grads, x_total, keys_padded, rows_padded, valid, stage, sems = rest[15:]
    n = pl.program_id(0)
    count = ck.shape[0]

    @pl.when(n == 0)
    def first():
        value = g2[...] + norm_back(
            x1[...], of_row(shifts, where, 3), own_back[...] + got_back[...].astype(WIDE)
        )
        g1[...] = value
        ec[...] = low(value)
        x_total[...] = jnp.zeros_like(x_total)
        grad_tokens[...] = jnp.zeros_like(grad_tokens)
        keys_padded[count:] = jnp.zeros_like(keys_padded[count:])
        for i in range(2):
            grads[i, count:] = jnp.zeros_like(grads[i, count:])
        rows_padded[count:] = jnp.zeros_like(rows_padded[count:])
        fill_valid(valid, where, parts)

    grad_mixed = low(by_rows(ec, o))
    keys_padded[:count] = ck[...]
    dq, dk, dv = attend_back(
        cq, ck, cv, keys_padded[...].T, co[...], grad_mixed, logs[0], probs, grads, valid[...], count
    )
    dq = low(dq)
    rows_padded[:count, :BLOCK] = low(dk)
    rows_padded[:count, BLOCK:] = low(dv)
    x_total[...] += dot_nt(dq, stacked(q, 0))
    grad_tokens[...] += dot_nt(
        rows_padded[:count],
        jnp.concatenate([stacked(k, 0), stacked(v, 0)], axis=1),
    )

    def products():
        query = low(dot(normed_turned[...], dq))
        pair = low(dot(turned[...], rows_padded[...]))
        flat = low(dot(co[...].T, ec[...]))
        blocks = [query[part(i)] for i in range(4)]
        blocks += [pair[part(i), part(j)] for j in range(2) for i in range(3)]
        return blocks + [flat[:, part(i)] for i in range(4)]

    numbers = [Q_CROSS + i * 4 + n for i in range(4)]
    numbers += [base + i * 4 + n for base in (K_CROSS, V_CROSS) for i in range(3)]
    numbers += [O_CROSS + n * 4 + i for i in range(4)]
    keep_blocks(products, stage, sems, store, where, numbers)

    @pl.when(n == 3)
    def last():
        half = grad_own.shape[0]
        grad_own[...] = grad_tokens[:half]
        grad_others[...] = low(grad_tokens[half:])
        grad_x[...] = g1[...] + norm_back(x[...].astype(WIDE), of_row(shifts, where, 1), x_total[...])


def shape(*dims, kind=LOW):
    return jax.ShapeDtypeStruct(dims, kind)


def call(kernel, grid, where, ins, outs, scratch, products, aliases=None, room=32):
    moved = BLOCK * BLOCK * 2 * grid * 16
    return pl.pallas_call(
        kernel,
        grid_spec=pltpu.PrefetchScalarGridSpec(
            num_scalar_prefetch=1,
            grid=(grid,),
            in_specs=[spec for _, spec in ins],
            out_specs=[spec for _, spec in outs],
            scratch_shapes=scratch,
        ),
        out_shape=[struct for struct, _ in outs],
        input_output_aliases=aliases or {},
        compiler_params=pltpu.CompilerParams(vmem_limit_bytes=room * 1024 * 1024),
        cost_estimate=pl.CostEstimate(
            flops=int(2 * products), bytes_accessed=moved, transcendentals=0
        ),
    )(where, *[array for array, _ in ins])


def full(array):
    return (array, whole(array.shape, pl.Buffered(1)))


def of_object(modulation):
    return full(modulation)


def made(*dims, kind=LOW):
    return (shape(*dims, kind=kind), whole(dims))


def striped(height):
    return (shape(height, D), stripe(height))


LOG_SPEC = pl.BlockSpec((1, 8, TOK_DEV), lambda n, where: (n, 0, 0))
ANYWHERE = pl.BlockSpec(memory_space=pl.ANY)


def padded_to(count):
    return -(-count // 128) * 128


def cross_forward(where, store, x, n1, tokens, shifts, parts):
    here, count = x.shape[0], tokens.shape[0]
    padded = padded_to(count)
    specs = columns(Q_CROSS, 4, 4) + columns(K_CROSS, 3, 4) + columns(V_CROSS, 3, 4) + rows(O_CROSS, 4)
    return call(
        functools.partial(cross_forward_kernel, parts),
        4,
        where,
        [full(x), full(n1), full(tokens), of_object(shifts)] + [(store, spec) for spec in specs],
        [
            striped(here),
            striped(count),
            striped(count),
            striped(here),
            (shape(4, 8, here, kind=WIDE), LOG_SPEC),
            made(here, D, kind=WIDE),
            made(here, D),
        ],
        [
            pltpu.VMEM((here, D), LOW),
            pltpu.VMEM((D, D), LOW),
            pltpu.VMEM((padded, BLOCK), LOW),
            pltpu.VMEM((2, padded, 2 * here), LOW),
            pltpu.VMEM((count, 128), WIDE),
        ],
        here * D * D * 12,
        room=34,
    )


def tall(here):
    return pl.BlockSpec((BLOCK, here), lambda n, where: (n, 0))


def self_own(where, store, mine):
    here = mine.shape[0]
    specs = columns(Q_SELF, 4, 4) + columns(K_SELF, 4, 4) + columns(V_SELF, 4, 4)
    return call(
        self_own_kernel,
        4,
        where,
        [full(mine)] + [(store, spec) for spec in specs],
        [
            made(D, here),
            striped(here),
            striped(here),
            striped(here),
            (shape(D, here, kind=WIDE), tall(here)),
            (shape(4, 8, here, kind=WIDE), LOG_SPEC),
        ],
        [pltpu.VMEM((2, here, 2 * here), LOW)],
        here * D * D * 6,
    )


def self_other(where, store, x1, other, shifts, sq, mix, stats):
    here = x1.shape[0]
    specs = columns(K_SELF, 4, 4) + columns(V_SELF, 4, 4) + rows(O_SELF, 4)
    return call(
        self_other_kernel,
        4,
        where,
        [full(x1), full(other), of_object(shifts), (sq, stripe(here)), (mix, tall(here)), (stats, LOG_SPEC)]
        + [(store, spec) for spec in specs],
        [
            made(D, here),
            striped(here),
            striped(here),
            striped(here),
            (shape(4, 8, here, kind=WIDE), LOG_SPEC),
            made(here, D, kind=WIDE),
            made(here, D),
        ],
        [pltpu.VMEM((here, D), LOW), pltpu.VMEM((D, D), LOW), pltpu.VMEM((2, here, 2 * here), LOW)],
        here * D * D * 6,
    )


def feed_specs(height):
    wide = FF // BLOCK
    up = [
        pl.BlockSpec(
            (1, BLOCK, BLOCK),
            lambda n, where, i=i, j=j: (where[W_UP + i * wide + n * height + j], 0, 0),
        )
        for i in range(4)
        for j in range(height)
    ]
    down = [
        pl.BlockSpec(
            (1, BLOCK, BLOCK), lambda n, where, i=i: (where[W_DOWN + n * height * 4 + i], 0, 0)
        )
        for i in range(4 * height)
    ]
    return up, down


def broad(here, height):
    return pl.BlockSpec((here, height * BLOCK), lambda n, where: (0, n))


def feed_early(where, store, cotangent):
    here = cotangent.shape[0]
    return call(
        feed_early_kernel,
        FF // BLOCK // 4,
        where,
        [full(cotangent)] + [(store, spec) for spec in feed_specs(4)[1]],
        [(shape(here, FF, kind=WIDE), broad(here, 4))],
        [],
        here * D * FF,
    )[0]


def feed(where, store, x2, n3, cotangent, shifts, grad_act):
    here = x2.shape[0]
    up, down = feed_specs(4)
    return call(
        feed_kernel,
        FF // BLOCK // 4,
        where,
        [full(x2), full(n3), full(cotangent), of_object(shifts), (grad_act, broad(here, 4))]
        + [(store, spec) for spec in up + down],
        [
            made(here, D),
            made(here, D, kind=WIDE),
            (shape(here, FF), broad(here, 4)),
            (shape(here, FF), broad(here, 4)),
        ],
        [pltpu.VMEM((here, D), WIDE), pltpu.VMEM((here, D), WIDE)],
        here * D * FF * 3,
        room=32,
    )


def feed_late(where, n3, cotangent, act, eh, slots):
    here = n3.shape[0]
    return call(
        feed_late_kernel,
        FF // BLOCK // 2,
        where,
        [full(n3), full(cotangent), (act, broad(here, 2)), (eh, broad(here, 2))],
        [(shape(slots, BLOCK, BLOCK), ANYWHERE)],
        [
            pltpu.VMEM((D, here), LOW),
            pltpu.VMEM((2, 16, BLOCK, BLOCK), LOW),
            pltpu.SemaphoreType.DMA((2, 16)),
        ],
        here * D * FF * 2,
        room=26,
    )[0]


def self_backward(where, store, g2, sq, k_own, k_other, v_own, v_other, so, logs):
    here = g2.shape[0]
    specs = columns(Q_SELF, 4, 4) + columns(K_SELF, 4, 4) + columns(V_SELF, 4, 4) + rows(O_SELF, 4)
    ins = [full(g2)] + [(a, stripe(here)) for a in (sq, k_own, k_other, v_own, v_other, so)]
    ins += [(logs, LOG_SPEC)] + [(store, spec) for spec in specs]
    return call(
        self_backward_kernel,
        4,
        where,
        ins,
        [made(here, D, kind=WIDE), made(here, D), striped(here), striped(2 * here), striped(2 * here)],
        [
            pltpu.VMEM((here, D), LOW),
            pltpu.VMEM((1, 2 * here, 2 * here), LOW),
            pltpu.VMEM((1, 2 * here, 2 * here), LOW),
            pltpu.VMEM((2 * here, BLOCK), LOW),
            pltpu.VMEM((2 * here, BLOCK), LOW),
            pltpu.VMEM((here, D), WIDE),
            pltpu.VMEM((here, D), WIDE),
        ],
        here * D * D * 16,
        room=28,
    )


def self_late(where, grads, g2, own_turned, other_turned, dq, dk, dv, so):
    here = g2.shape[0]
    ins = [full(a) for a in (g2, own_turned, other_turned)]
    ins += [(a, stripe(a.shape[0])) for a in (dq, dk, dv, so)] + [(grads, ANYWHERE)]
    return call(
        self_late_kernel,
        4,
        where,
        ins,
        [(shape(*grads.shape), ANYWHERE)],
        [
            pltpu.VMEM((here, D), LOW),
            pltpu.VMEM((D, 2 * here), LOW),
            pltpu.VMEM((2, 16, BLOCK, BLOCK), LOW),
            pltpu.SemaphoreType.DMA((2, 16)),
        ],
        here * D * D * 6,
        {len(ins): 0},
        room=30,
    )[0]


def cross_backward(
    where, store, grads, x, g2, x1, own_back, got_back, turned, shifts, normed_turned, cq, ck, cv, co, logs, parts
):
    here, count = x.shape[0], ck.shape[0]
    padded = padded_to(count)
    specs = columns(Q_CROSS, 4, 4) + columns(K_CROSS, 3, 4) + columns(V_CROSS, 3, 4) + rows(O_CROSS, 4)
    ins = [full(a) for a in (x, g2, x1, own_back, got_back, turned)]
    ins += [of_object(shifts), full(normed_turned)]
    ins += [(a, stripe(a.shape[0])) for a in (cq, ck, cv, co)] + [(logs, LOG_SPEC)]
    ins += [(store, spec) for spec in specs] + [(grads, ANYWHERE)]
    return call(
        functools.partial(cross_backward_kernel, parts),
        4,
        where,
        ins,
        [
            made(here, D, kind=WIDE),
            made(count // parts, DIMG, kind=WIDE),
            made(count - count // parts, DIMG),
            (shape(*grads.shape), ANYWHERE),
        ],
        [
            pltpu.VMEM((count, DIMG), WIDE),
            pltpu.VMEM((here, D), LOW),
            pltpu.VMEM((here, D), WIDE),
            pltpu.VMEM((2, padded, 2 * here), LOW),
            pltpu.VMEM((2, padded, 2 * here), LOW),
            pltpu.VMEM((here, D), WIDE),
            pltpu.VMEM((padded, BLOCK), LOW),
            pltpu.VMEM((padded, 2 * BLOCK), LOW),
            pltpu.VMEM((count, 128), WIDE),
            pltpu.VMEM((2, 14, BLOCK, BLOCK), LOW),
            pltpu.SemaphoreType.DMA((2, 14)),
        ],
        here * D * D * 24,
        {len(ins): 3},
        room=40,
    )


def hand_on_kernel(*refs):
    count = len(refs) // 2
    for source, target in zip(refs[:count], refs[count:]):
        target[...] = source[...]


def hand_on(arrays):
    specs = [
        pl.BlockSpec((a.shape[0] // 4,) + a.shape[1:], lambda i: (i, 0, 0)) for a in arrays
    ]
    return pl.pallas_call(
        hand_on_kernel,
        grid=(4,),
        out_shape=[jax.ShapeDtypeStruct(a.shape, a.dtype) for a in arrays],
        in_specs=specs,
        out_specs=specs,
        compiler_params=pltpu.CompilerParams(vmem_limit_bytes=VLIM),
    )(*arrays)


def partner(block, axis):
    size = lax.axis_size(axis)
    return lax.ppermute(block, axis, [(i, i ^ 1) for i in range(size)])


def soap_update(
    slot_grads,
    first_moment,
    second_moment,
    left_basis,
    right_basis,
    master_weights,
    slot_rates,
    slot_used,
):
    keep_mask = slot_used[:, None, None] > 0.0
    slot_grads = jnp.where(keep_mask, slot_grads, 0.0)
    rotated = jnp.matmul(
        jnp.matmul(jnp.swapaxes(left_basis, 1, 2), slot_grads, precision=highest),
        right_basis,
        precision=highest,
    )
    first_new = moment_decay * first_moment + (1.0 - moment_decay) * rotated
    second_new = moment_decay * second_moment + (1.0 - moment_decay) * rotated * rotated
    correction = 1.0 - moment_decay**STEP
    normalized = first_new / correction / (jnp.sqrt(second_new / correction) + 1e-08)
    rotated_back = jnp.matmul(
        jnp.matmul(left_basis, normalized, precision=highest),
        jnp.swapaxes(right_basis, 1, 2),
        precision=highest,
    )
    fresh_master = master_weights - slot_rates[:, None, None] * (
        rotated_back + 0.01 * master_weights
    )
    fresh_master = jnp.where(keep_mask, fresh_master, 0.0)
    return (
        slot_grads,
        jnp.where(keep_mask, first_new, 0.0),
        jnp.where(keep_mask, second_new, 0.0),
        fresh_master,
        fresh_master.astype(jnp.bfloat16),
    )


def shards(
    triplane,
    cotangent,
    image_tokens,
    modulation,
    image_counts,
    owner_slots,
    master_weights,
    first_moment,
    second_moment,
    left_basis,
    right_basis,
):
    img_size = lax.axis_size("img")
    rows_size = lax.axis_size("rows")
    img_index = lax.axis_index("img")
    flat_index = lax.axis_index("rows") * img_size + img_index
    object_index = flat_index // 2
    pair_index = img_index // 2
    groups = img_size // 2
    slot_cap = image_tokens.shape[0] // groups
    own_count = master_weights.shape[0]
    slot_total = rows_size * img_size * own_count
    fits = rows_size == 16 and img_size == 2 and own_count == 8
    modulation = jnp.swapaxes(modulation, 0, 1)
    info = [object_index[None]]
    if img_size == 2:
        info += [img_index[None], 1 - img_index[None]]
    else:
        info += [jnp.arange(img_size, dtype=jnp.int32)]
    info += [image_counts]
    if fits:
        store, tokens, tokens_turned, n1, n1_turned = gather(
            master_weights, image_tokens, triplane, modulation
        )
        store = store.reshape(-1, BLOCK, BLOCK)
        where = [positions(owner_slots, WAYS_OUT), positions(owner_slots, WAYS_IN)]
    else:
        store = lax.all_gather(master_weights.astype(LOW), ("rows", "img"), axis=0, tiled=True)
        where = [owner_slots, owner_slots]
        if img_size == 2:
            tokens = jnp.concatenate([image_tokens, partner(image_tokens, "img")], 0)
        else:
            tokens = lax.all_gather(image_tokens, "img", axis=0, tiled=True)
            tokens = tokens.reshape(img_size, groups, slot_cap, DIMG)
            tokens = lax.dynamic_index_in_dim(tokens, pair_index, 1, keepdims=False)
            tokens = tokens.reshape(img_size * slot_cap, DIMG)
        count = tokens.shape[0]
        tokens_turned = jnp.pad(tokens.T, ((0, 0), (0, padded_to(count) - count)))
        shifts = lax.dynamic_index_in_dim(modulation, object_index, 1, keepdims=False)
        n1 = low(modulated_norm(triplane.astype(WIDE), shifts[0], shifts[1]))
        n1_turned = n1.T
    where = jnp.concatenate([piece.astype(jnp.int32) for piece in where + info])

    cq, ck, cv, co, cross_logs, x1, n2 = cross_forward(
        where, store, triplane, n1, tokens, modulation, img_size
    )
    n2_other = partner(n2, "img")
    own_turned, sq, k_own, v_own, mix, stats = self_own(where, store, n2)
    grad_act = feed_early(where, store, cotangent)
    other_turned, k_other, v_other, so, self_logs, x2, n3 = self_other(
        where, store, x1, n2_other, modulation, sq, mix, stats
    )
    layer_out, g2, act, eh = feed(where, store, x2, n3, cotangent, modulation, grad_act)
    own_back, other_back, dq, dk, dv = self_backward(
        where, store, g2, sq, k_own, k_other, v_own, v_other, so, self_logs
    )
    got_back = partner(other_back, "img")
    grads = feed_late(where, n3, cotangent, act, eh, slot_total)
    grads = self_late(where, grads, g2, own_turned, other_turned, dq, dk, dv, so)
    grad_triplane, grad_own, grad_others, grads = cross_backward(
        where,
        store,
        grads,
        triplane,
        g2,
        x1,
        own_back,
        got_back,
        tokens_turned,
        modulation,
        n1_turned,
        cq,
        ck,
        cv,
        co,
        cross_logs,
        img_size,
    )
    if img_size == 2:
        grad_image = grad_own + partner(grad_others, "img").astype(WIDE)
    else:
        pick = (jnp.arange(groups, dtype=jnp.int32) == pair_index).astype(WIDE)
        grad_tokens = jnp.concatenate([grad_own, grad_others.astype(WIDE)], 0)
        spread = grad_tokens.reshape(img_size, 1, slot_cap, DIMG) * pick[None, :, None, None]
        grad_image = lax.psum_scatter(
            spread.reshape(img_size * groups * slot_cap, DIMG).astype(LOW),
            "img",
            scatter_dimension=0,
            tiled=True,
        ).astype(WIDE)
    my_slots = flat_index * own_count + jnp.arange(own_count, dtype=jnp.int32)
    matched = (owner_slots[:, None] == my_slots[None, :]).astype(WIDE)
    slot_used = jnp.sum(matched, axis=0)
    slot_rates = jnp.sum(matched * jnp.asarray(block_table(weight_scales()))[:, None], axis=0)
    state = (first_moment, second_moment, left_basis, right_basis, master_weights)
    if fits:
        rates = jnp.broadcast_to(
            jnp.stack([slot_rates, slot_used], 1)[:, :, None], (own_count, 2, BLOCK)
        )
        updated = hand_on(scatter(grads.reshape(2, 8, 16, BLOCK, BLOCK), *state, rates))
    else:
        used = jnp.zeros((slot_total,), jnp.bool_).at[owner_slots].set(True)
        grads = jnp.where(used[:, None, None], grads, jnp.zeros_like(grads))
        slot_grads = lax.psum_scatter(
            grads, ("rows", "img"), scatter_dimension=0, tiled=True
        ).astype(WIDE)
        updated = soap_update(slot_grads, *state, slot_rates, slot_used)
    return (layer_out, grad_triplane, grad_image) + tuple(updated)


def solution(mesh):
    flat = P(("rows", "img"), None)
    blocks = P(("rows", "img"), None, None)
    in_specs = (flat, flat, flat, P(), P(), P()) + (blocks,) * 5
    out_specs = (flat, flat, flat) + (blocks,) * 5
    return jax.shard_map(shards, mesh=mesh, in_specs=in_specs, out_specs=out_specs, check_vma=False)
```

```python
import functools

import jax
import jax.numpy as jnp
import numpy as np
from jax import lax
from jax.experimental import pallas as pl
from jax.experimental.pallas import tpu as pltpu
from jax.sharding import PartitionSpec as P

D = 1024
HEADS = 16
FF = 4096
DIMG = 768
TOK_DEV = 384
IMG_MAX = 1025
BLOCK = 256
STEP = 5
HEAD = D // HEADS

MESH = pl.DeviceIdType.MESH
VLIM = 60 * 1024 * 1024
WAYS_OUT = (
    ('lo', 'hi', 'y', 'x'),
    ('hi', 'lo', 'x', 'y'),
    ('y', 'x', 'hi', 'lo'),
    ('hi', 'lo', 'x', 'y'),
    ('hi', 'x', 'lo', 'y'),
    ('lo', 'y', 'hi', 'x'),
    ('hi', 'y', 'lo', 'x'),
    ('hi', 'x', 'y', 'lo'),
)
WAYS_IN = (
    ('lo', 'y', 'hi', 'x'),
    ('hi', 'x', 'y', 'lo'),
    ('hi', 'y', 'x', 'lo'),
    ('hi', 'lo', 'x', 'y'),
    ('hi', 'x', 'lo', 'y'),
    ('hi', 'y', 'lo', 'x'),
    ('hi', 'lo', 'x', 'y'),
    ('lo', 'hi', 'y', 'x'),
)
FRONT = 17
ORDER_OUT = (
    (6, 0), (2, 0), (2, 1), (0, 0), (5, 0), (3, 0), (6, 1), (-1, 0),
    (3, 1), (1, 0), (5, 1), (4, 0), (1, 1), (3, 2), (4, 1), (0, 1),
    (0, 2), (6, 2), (7, 0), (7, 1), (4, 2), (3, 3), (5, 2), (0, 3),
    (7, 2), (3, 4), (1, 2), (7, 3), (6, 3), (5, 3), (2, 2), (4, 3),
    (0, 4), (7, 4), (2, 3), (4, 4), (1, 3), (6, 4), (1, 4), (5, 4),
    (2, 4),
)
ORDER_IN = (
    (0, 0), (1, 0), (2, 0), (3, 0), (4, 0), (5, 0), (6, 0), (7, 0),
    (1, 1), (0, 1), (4, 1), (0, 2), (7, 1), (4, 2), (6, 1), (2, 1),
    (7, 2), (5, 1), (5, 2), (6, 2), (1, 2), (0, 3), (7, 3), (6, 3),
    (1, 3), (3, 1), (1, 4), (4, 3), (7, 4), (2, 2), (4, 4), (2, 3),
    (6, 4), (3, 2), (0, 4), (5, 3), (4, 5), (6, 5), (2, 4), (7, 5),
    (3, 3), (2, 5), (5, 4), (1, 5), (0, 5), (5, 5), (3, 4), (3, 5),
)


def coords():
    row = lax.axis_index("rows")
    rest = lax.rem(row, 4)
    return lax.div(row, 4), lax.div(rest, 2), lax.rem(rest, 2), lax.axis_index("img")


def neighbour(kind):
    z, x, c, y = coords()
    if kind == "c":
        c = 1 - c
    if kind == "x":
        x = 1 - x
    if kind == "y":
        y = 1 - y
    if kind == "lo":
        z = z + 1 - 2 * lax.rem(z, 2)
    if kind == "hi":
        z = lax.rem(z + 2, 4)
    return (z * 4 + x * 2 + c, y)


def place(way):
    z, x, c, y = coords()
    bits = {"x": x, "y": y, "lo": lax.rem(z, 2), "hi": lax.div(z, 2)}
    return sum(bits[kind] * 2**k for k, kind in enumerate(way))


def positions(slot, ways):
    owner, j = slot // 8, slot % 8
    z, x, c, y = owner // 8, owner // 4 % 2, owner // 2 % 2, owner % 2
    bits = {"x": x, "y": y, "lo": z % 2, "hi": z // 2}
    total = (c * 8 + j) * 16
    for kind, bit in bits.items():
        total = total + bit * jnp.asarray([2 ** way.index(kind) for way in ways], jnp.int32)[j]
    return total


def greet():
    barrier = pltpu.get_barrier_semaphore()
    for kind in ("c", "x", "y", "lo", "hi"):
        pl.semaphore_signal(barrier, inc=1, device_id=neighbour(kind), device_id_type=MESH)
    pl.semaphore_wait(barrier, 5)


def gather_kernel(
    master, tokens, triplane, modulation, out, both, turned, n1, n1_turned,
    own, wide, mine, x, shifts, others, spread, upright, lsem, csem, ssem, rsem, tsem,
):
    c = coords()[2]
    early = [
        pltpu.make_async_copy(source, target, lsem.at[i])
        for i, (source, target) in enumerate(
            ((master, wide), (tokens, mine), (triplane, x), (modulation, shifts))
        )
    ]
    for copy in early:
        copy.start()
    greet()
    cross = pltpu.make_async_remote_copy(
        tokens, others, tsem.at[0], tsem.at[1], device_id=neighbour("y"), device_id_type=MESH
    )
    early[0].wait()
    copies, keeps = {}, {}

    def start(j, k):
        base = place(WAYS_OUT[j])
        count = 2**k
        first = lax.div(base, count) * count if k < 4 else 0
        here = pl.ds(first, count)
        source = own.at[pl.ds(j, 1)] if k == 0 else out.at[c, j, here]
        copy = pltpu.make_async_remote_copy(
            source,
            out.at[c, j, here],
            ssem.at[j, k],
            rsem.at[j, k],
            device_id=neighbour((WAYS_OUT[j] + ("c",))[k]),
            device_id_type=MESH,
        )
        copy.start()
        copies[j, k] = copy

    for j, k in ORDER_OUT:
        if j < 0:
            cross.start()
        elif k == 0:
            own[j] = wide[j].astype(jnp.bfloat16)
            start(j, 0)
            keep = pltpu.make_async_copy(
                own.at[pl.ds(j, 1)], out.at[c, j, pl.ds(place(WAYS_OUT[j]), 1)], csem.at[j]
            )
            keep.start()
            keeps[j] = keep
        else:
            if k == 1:
                keeps[j].wait()
            copies[j, k - 1].wait_recv()
            start(j, k)
        if (j, k) == ORDER_OUT[FRONT]:
            row = pl.ds(lax.axis_index("rows"), 1)
            early[2].wait()
            early[3].wait()
            one = modulated_norm(
                x[...].astype(jnp.float32), shifts[0, row], shifts[1, row]
            )
            n1[...] = one.astype(jnp.bfloat16)
            n1_turned[...] = one.astype(jnp.bfloat16).T
        if (j, k) == ORDER_OUT[min(max(FRONT + 6, ORDER_OUT.index((-1, 0)) + 9), len(ORDER_OUT) - 1)]:
            half = tokens.shape[0]
            cross.wait()
            early[1].wait()
            spread[:half] = mine[...].astype(jnp.float32)
            spread[half:] = others[...].astype(jnp.float32)
            both[...] = spread[...].astype(jnp.bfloat16)
            upright[2 * half :] = jnp.zeros_like(upright[2 * half :])
            for i in range(tokens.shape[1] // BLOCK):
                lanes = slice(i * BLOCK, (i + 1) * BLOCK)
                upright[: 2 * half] = both[:, lanes]
                turned[lanes] = upright[...].T
    for j in range(8):
        copies[j, 4].wait_recv()
    for copy in copies.values():
        copy.wait_send()


def gather(master, tokens, x, modulation):
    anywhere, inside = pl.BlockSpec(memory_space=pl.ANY), pl.BlockSpec(memory_space=pltpu.VMEM)
    half, width = tokens.shape
    padded = -(-2 * half // 128) * 128
    bf = jnp.bfloat16
    return pl.pallas_call(
        gather_kernel,
        out_shape=[
            jax.ShapeDtypeStruct((2, 8, 16, BLOCK, BLOCK), bf),
            jax.ShapeDtypeStruct((2 * half, width), bf),
            jax.ShapeDtypeStruct((width, padded), bf),
            jax.ShapeDtypeStruct(x.shape, bf),
            jax.ShapeDtypeStruct(x.shape[::-1], bf),
        ],
        in_specs=[anywhere] * 4,
        out_specs=[anywhere] + [inside] * 4,
        scratch_shapes=[
            pltpu.VMEM((8, BLOCK, BLOCK), bf),
            pltpu.VMEM((8, BLOCK, BLOCK), jnp.float32),
            pltpu.VMEM((half, width), bf),
            pltpu.VMEM(x.shape, bf),
            pltpu.VMEM(modulation.shape, jnp.float32),
            pltpu.VMEM((half, width), bf),
            pltpu.VMEM((2 * half, width), jnp.float32),
            pltpu.VMEM((padded, BLOCK), bf),
            pltpu.SemaphoreType.DMA((4,)),
            pltpu.SemaphoreType.DMA((8,)),
            pltpu.SemaphoreType.DMA((8, 5)),
            pltpu.SemaphoreType.DMA((8, 5)),
            pltpu.SemaphoreType.DMA((2,)),
        ],
        compiler_params=pltpu.CompilerParams(
            collective_id=11, has_side_effects=True, vmem_limit_bytes=VLIM
        ),
    )(master, tokens, x, modulation)


def times(a, b, left, right):
    def product(one, two):
        return lax.dot_general(
            one, two, (((left,), (right,)), ((), ())), preferred_element_type=jnp.float32
        )

    a_high, b_high = a.astype(jnp.bfloat16), b.astype(jnp.bfloat16)
    a_low = (a - a_high.astype(jnp.float32)).astype(jnp.bfloat16)
    b_low = (b - b_high.astype(jnp.float32)).astype(jnp.bfloat16)
    return product(a_high, b_high) + (product(a_high, b_low) + product(a_low, b_high))


def scatter_kernel(grads, first, second, left, right, master, rates, *rest):
    outs = rest[:4]
    own, r0, r1, r2, r3, r4, held, made, lsem, ssem, rsem, hsem, osem = rest[4:]
    c = coords()[2]
    got = (r0, r1, r2, r3, r4)
    loads, copies, fetches, puts = [], {}, {}, {}
    for j in range(8):
        load = pltpu.make_async_copy(grads.at[c, j], own.at[j], lsem.at[j])
        load.start()
        loads.append(load)
    greet()

    def exchange(j, s, source, kind):
        copy = pltpu.make_async_remote_copy(
            source,
            got[s].at[j],
            ssem.at[j, s],
            rsem.at[j, s],
            device_id=neighbour(kind),
            device_id_type=MESH,
        )
        copy.start()
        copies[j, s] = copy

    def add(j, s):
        count = 16 >> s
        start = lax.div(place(WAYS_IN[j]), count) * count if s else 0

        def body(b, carry):
            own[j, start + b] = own[j, start + b] + got[s][j, b]
            return carry

        lax.fori_loop(0, count, body, 0)

    def send(j, s):
        count = 16 >> s
        half = lax.div(place(WAYS_IN[j]), count)
        other = (half + 1 - 2 * lax.rem(half, 2)) * count
        exchange(j, s, own.at[j, pl.ds(other, count)], WAYS_IN[j][4 - s])

    def fetch(turn, j):
        side = turn % 2
        fetches[turn] = [
            pltpu.make_async_copy(array.at[j], held.at[side, i], hsem.at[side, i])
            for i, array in enumerate((first, second, left, right, master))
        ]
        for copy in fetches[turn]:
            copy.start()

    def finish(turn, j):
        side = turn % 2
        for copy in fetches[turn]:
            copy.wait()
        if turn >= 2:
            for copy in puts[turn - 2]:
                copy.wait()
        base = place(WAYS_IN[j])
        used = rates[j, 1:2] > 0.0
        total = own[j, base].astype(jnp.float32) + r4[j, 0].astype(jnp.float32)
        total = jnp.where(used, total, 0.0)
        rotated = times(times(held[side, 2], total, 0, 0), held[side, 3], 1, 0)
        new_first = 0.5 * held[side, 0] + 0.5 * rotated
        new_second = 0.5 * held[side, 1] + 0.5 * rotated * rotated
        fix = 1.0 - 0.5**STEP
        unit = (new_first / fix) / (jnp.sqrt(new_second / fix) + 1e-08)
        update = times(times(held[side, 2], unit, 1, 0), held[side, 3], 1, 1)
        old = held[side, 4]
        new = jnp.where(used, old - rates[j, 0:1] * (update + 0.01 * old), 0.0)
        made[side, 0] = total
        made[side, 1] = jnp.where(used, new_first, 0.0)
        made[side, 2] = jnp.where(used, new_second, 0.0)
        made[side, 3] = new
        puts[turn] = [
            pltpu.make_async_copy(made.at[side, i], outs[i].at[j], osem.at[side, i])
            for i in range(4)
        ]
        for copy in puts[turn]:
            copy.start()

    ends = [j for j, s in ORDER_IN if s == 5]
    for turn in range(2):
        fetch(turn, ends[turn])
    turn = 0
    for j, s in ORDER_IN:
        if s == 0:
            exchange(j, 0, grads.at[1 - c, j], "c")
            continue
        if s == 1:
            loads[j].wait()
        copies[j, s - 1].wait_recv()
        if s < 5:
            add(j, s - 1)
            send(j, s)
        else:
            finish(turn, j)
            if turn < 6:
                fetch(turn + 2, ends[turn + 2])
            turn += 1
    for copy in puts[6] + puts[7]:
        copy.wait()
    for copy in copies.values():
        copy.wait_send()


def scatter(grads, first, second, left, right, master, rates):
    bf, wide, block = jnp.bfloat16, jnp.float32, (BLOCK, BLOCK)
    anywhere = pl.BlockSpec(memory_space=pl.ANY)
    return pl.pallas_call(
        scatter_kernel,
        out_shape=[jax.ShapeDtypeStruct((8,) + block, kind) for kind in (wide,) * 4],
        in_specs=[anywhere] * 6 + [pl.BlockSpec(memory_space=pltpu.VMEM)],
        out_specs=[anywhere] * 4,
        scratch_shapes=[pltpu.VMEM((8, count) + block, bf) for count in (16, 16, 8, 4, 2, 1)]
        + [
            pltpu.VMEM((2, 5) + block, wide),
            pltpu.VMEM((2, 4) + block, wide),
            pltpu.SemaphoreType.DMA((8,)),
            pltpu.SemaphoreType.DMA((8, 5)),
            pltpu.SemaphoreType.DMA((8, 5)),
            pltpu.SemaphoreType.DMA((2, 5)),
            pltpu.SemaphoreType.DMA((2, 4)),
        ],
        compiler_params=pltpu.CompilerParams(
            collective_id=12, has_side_effects=True, vmem_limit_bytes=54 * 1024 * 1024
        ),
    )(grads, first, second, left, right, master, rates)


highest = lax.Precision.HIGHEST
moment_decay = 0.5
LOW = jnp.bfloat16
WIDE = jnp.float32

def shapes_list():
    return [(D, D), (DIMG, D), (DIMG, D), (D, D), (D, D), (D, D), (D, D), (D, D), (D, FF), (FF, D)]


Q_CROSS, K_CROSS, V_CROSS, O_CROSS, Q_SELF, K_SELF, V_SELF, O_SELF, W_UP, W_DOWN = (
    int(v) for v in np.cumsum([0] + [a * b // BLOCK**2 for a, b in shapes_list()])[:10]
)


NBLK = W_DOWN + FF * D // BLOCK**2


def weight_scales():
    self_root = (2.0 * TOK_DEV) ** 0.5
    cross_root = (IMG_MAX / 2.0) ** 0.5
    return [
        D ** (-0.5),
        DIMG ** (-0.5),
        DIMG ** (-0.5),
        0.5 * cross_root * D ** (-0.5),
        D ** (-0.5),
        D ** (-0.5),
        D ** (-0.5),
        0.5 * self_root * D ** (-0.5),
        D ** (-0.5),
        2.0 * FF ** (-0.5),
    ]


def block_table(scales):
    pieces = []
    for shape_pair, scale_value in zip(shapes_list(), scales):
        amount = shape_pair[0] * shape_pair[1] // (BLOCK * BLOCK)
        pieces.append(np.full((amount,), scale_value, np.float32))
    return np.concatenate(pieces)


def low(v):
    return v.astype(LOW)


def dot(a, b):
    return jnp.dot(a, b, preferred_element_type=WIDE)


def dot_nt(a, b):
    return lax.dot_general(a, b, (((1,), (1,)), ((), ())), preferred_element_type=WIDE)


def part(k):
    return slice(k * BLOCK, (k + 1) * BLOCK)


def norm_parts(values):
    centered = values - jnp.mean(values, axis=-1, keepdims=True)
    variance = jnp.mean(centered * centered, axis=-1, keepdims=True)
    return centered, lax.rsqrt(variance + 1e-06)


def modulated_norm(values, shift, scale):
    centered, inverse = norm_parts(values)
    return centered * inverse * (1.0 + scale) + shift


def norm_back(values, scale, grad_normed):
    centered, inverse = norm_parts(values)
    unit = centered * inverse
    grad_unit = grad_normed * (1.0 + scale)
    return inverse * (
        grad_unit
        - jnp.mean(grad_unit, axis=-1, keepdims=True)
        - unit * jnp.mean(grad_unit * unit, axis=-1, keepdims=True)
    )


def halves(pair):
    lane = lax.broadcasted_iota(jnp.int32, pair.shape, 1)
    zero = jnp.zeros_like(pair)
    return jnp.where(lane < HEAD, pair, zero), jnp.where(lane < HEAD, zero, pair)


def fill_valid(valid, where, parts):
    cap = valid.shape[0] // parts
    slot = lax.broadcasted_iota(jnp.int32, (cap, 128), 0)
    for i in range(parts):
        number = slot * parts + where[2 * NBLK + 1 + i]
        limit = where[2 * NBLK + 1 + parts + where[2 * NBLK]]
        valid[i * cap : (i + 1) * cap] = (number < limit).astype(WIDE)


def group(n, width):
    return pl.ds(pl.multiple_of(n * width, width), width)


def of_row(shifts, where, k):
    return shifts[k, pl.ds(where[2 * NBLK], 1)]


def masked(scores, valid):
    if valid is None:
        return scores
    wide = jnp.concatenate([valid] * (scores.shape[1] // valid.shape[1]), axis=1)
    return jnp.where(wide > 0.0, scores, -1e30)


def columns(base, tall, wide):
    return [
        pl.BlockSpec((1, BLOCK, BLOCK), lambda n, where, i=i: (where[base + i * wide + n], 0, 0))
        for i in range(tall)
    ]


def rows(base, wide):
    return [
        pl.BlockSpec((1, BLOCK, BLOCK), lambda n, where, k=k: (where[base + n * wide + k], 0, 0))
        for k in range(wide)
    ]


def whole(shape, mode=None):
    return pl.BlockSpec(shape, lambda n, where: (0,) * len(shape), pipeline_mode=mode)


def stripe(height):
    return pl.BlockSpec((height, BLOCK), lambda n, where: (0, n))


def stacked(blocks, axis):
    return jnp.concatenate([block[0] for block in blocks], axis=axis)


def by_columns(left, blocks):
    return dot(left[...], stacked(blocks, 0))


def by_rows(left, blocks):
    return dot_nt(left[...], stacked(blocks, 1))


def attend_part(queries, keys, values_turned, weights, valid, count):
    outs, tops, totals = [], [], []
    tokens = queries.shape[0]
    scores = []
    for pair in range(2):
        lanes = slice(pair * 2 * HEAD, (pair + 1) * 2 * HEAD)
        both = jnp.concatenate(halves(queries[:, lanes]), axis=0)
        scores.append(masked(dot_nt(keys[:count, lanes], both), valid))
    for pair in range(2):
        top = jnp.max(scores[pair], axis=0, keepdims=True)
        exponent = jnp.exp(scores[pair] - top)
        total = jnp.sum(exponent, axis=0, keepdims=True)
        weights[pair, :count] = low(exponent)
        tops += [top[:, :tokens], top[:, tokens:]]
        totals += [total[:, :tokens], total[:, tokens:]]
    for pair in range(2):
        lanes = slice(pair * 2 * HEAD, (pair + 1) * 2 * HEAD)
        mixed = dot(values_turned[lanes], weights[pair])
        outs += [mixed[:HEAD, :tokens], mixed[HEAD:, tokens:]]
    return outs, tops, totals


def attend_end(outs, tops, totals):
    turned = jnp.concatenate([out / total for out, total in zip(outs, totals)], axis=0)
    logs = [top + jnp.log(total) for top, total in zip(tops, totals)]
    return low(turned.T), jnp.concatenate(logs + logs, axis=0)


def attend_back(queries, keys, values, keys_turned, mixed, grad_mixed, logs, probs, grads, valid, count):
    tokens = queries.shape[0]
    inner = (mixed.astype(WIDE) * grad_mixed.astype(WIDE)).T
    inner = jnp.concatenate(
        [jnp.sum(inner[head * HEAD : (head + 1) * HEAD], axis=0, keepdims=True) for head in range(4)],
        axis=1,
    )
    logs = jnp.concatenate([logs[head : head + 1] for head in range(4)], axis=1)
    grad_query, grad_key, grad_value = [], [], []
    for pair in range(2):
        kept = pair % grads.shape[0]
        lanes = slice(pair * 2 * HEAD, (pair + 1) * 2 * HEAD)
        side = slice(pair * 2 * tokens, (pair + 1) * 2 * tokens)
        both_queries = jnp.concatenate(halves(queries[:, lanes]), axis=0)
        both_mixed = jnp.concatenate(halves(grad_mixed[:, lanes]), axis=0)
        scores = masked(dot_nt(keys[:count, lanes], both_queries), valid)
        grad_full = dot_nt(values[:count, lanes], both_mixed)
        full = jnp.exp(scores - logs[:, side])
        grads[kept, :count] = low(full * (grad_full - inner[:, side]))
        probs[kept, :count] = low(full)
        turned = dot(keys_turned[lanes], grads[kept])
        grad_query += [turned[:HEAD, :tokens], turned[HEAD:, tokens:]]
        grad_key.append(dot(grads[kept, :count], both_queries))
        grad_value.append(dot(probs[kept, :count], both_mixed))
    grad_query = jnp.concatenate(grad_query, axis=0).T * HEAD ** (-0.5)
    return grad_query, jnp.concatenate(grad_key, axis=1), jnp.concatenate(grad_value, axis=1)


def send_blocks(stage, sems, side, store, where, numbers):
    return [
        pltpu.make_async_copy(stage.at[side, i], store.at[where[NBLK + number]], sems.at[side, i])
        for i, number in enumerate(numbers)
    ]


def keep_blocks(products, stage, sems, store, where, numbers):
    step, steps = pl.program_id(0), pl.num_programs(0)
    side = lax.rem(step, 2)

    @pl.when(step >= 2)
    def reuse():
        for copy in send_blocks(stage, sems, side, store, where, numbers):
            copy.wait()

    for i, product in enumerate(products()):
        stage[side, i] = product
    for copy in send_blocks(stage, sems, side, store, where, numbers):
        copy.start()

    @pl.when(step == steps - 1)
    def drain():
        for copy in send_blocks(stage, sems, 1 - side, store, where, numbers):
            copy.wait()
        for copy in send_blocks(stage, sems, side, store, where, numbers):
            copy.wait()


def cross_forward_kernel(parts, where, x, n1, tokens, shifts, *rest):
    q, k, v, o = rest[:4], rest[4:7], rest[7:10], rest[10:14]
    cq, ck, cv, co, logs, x1, n2, all_mixed, all_out, turned, weights, valid = rest[14:]
    n = pl.program_id(0)
    count = tokens.shape[0]

    @pl.when(n == 0)
    def first():
        turned[count:] = jnp.zeros_like(turned[count:])
        for pair in range(2):
            weights[pair, count:] = jnp.zeros_like(weights[pair, count:])
        fill_valid(valid, where, parts)

    queries = low(by_columns(n1, q)) * HEAD ** (-0.5)
    cq[...] = queries
    pair = low(dot(tokens[...], jnp.concatenate([stacked(k, 0), stacked(v, 0)], axis=1)))
    ck[...] = pair[:, :BLOCK]
    cv[...] = pair[:, BLOCK:]
    turned[:count] = pair[:, BLOCK:]
    mixed, log_total = attend_end(
        *attend_part(queries, ck, turned[...].T, weights, valid[...], count)
    )
    co[...] = mixed
    logs[0] = log_total
    all_mixed[:, group(n, BLOCK)] = mixed
    all_out[group(n, BLOCK)] = stacked(o, 1)

    @pl.when(n == 3)
    def last():
        after = x[...].astype(WIDE) + dot(all_mixed[...], all_out[...])
        x1[...] = after
        n2[...] = low(modulated_norm(after, of_row(shifts, where, 2), of_row(shifts, where, 3)))


def self_own_kernel(where, mine, *rest):
    q, k, v = rest[:4], rest[4:8], rest[8:12]
    turned, sq, sk, sv, mix, stats, weights = rest[12:]
    n = pl.program_id(0)

    @pl.when(n == 0)
    def first():
        turned[...] = mine[...].T

    all_three = low(
        dot(mine[...], jnp.concatenate([stacked(q, 0), stacked(k, 0), stacked(v, 0)], axis=1))
    )
    queries = all_three[:, :BLOCK] * HEAD ** (-0.5)
    sq[...] = queries
    sk[...] = all_three[:, BLOCK : 2 * BLOCK]
    sv[...] = all_three[:, 2 * BLOCK :]
    outs, tops, totals = attend_part(queries, sk, sv[...].T, weights, None, mine.shape[0])
    mix[...] = jnp.concatenate(outs, axis=0)
    stats[0] = jnp.concatenate(tops + totals, axis=0)


def self_other_kernel(where, x1, other, shifts, sq, mix, stats, *rest):
    k, v, o = rest[:4], rest[4:8], rest[8:12]
    turned, sk, sv, so, logs, x2, n3, all_mixed, all_out, weights = rest[12:]
    n = pl.program_id(0)

    @pl.when(n == 0)
    def first():
        turned[...] = other[...].T

    pair = low(dot(other[...], jnp.concatenate([stacked(k, 0), stacked(v, 0)], axis=1)))
    sk[...] = pair[:, :BLOCK]
    sv[...] = pair[:, BLOCK:]
    parts = attend_part(sq[...], sk, sv[...].T, weights, None, other.shape[0])
    outs, tops, totals = [], [], []
    for head, (out, top, amount) in enumerate(zip(*parts)):
        old_top, old_amount = stats[0, head : head + 1], stats[0, 4 + head : 5 + head]
        new_top = jnp.maximum(top, old_top)
        grow, keep = jnp.exp(top - new_top), jnp.exp(old_top - new_top)
        outs.append(out * grow + mix[head * HEAD : (head + 1) * HEAD] * keep)
        tops.append(new_top)
        totals.append(amount * grow + old_amount * keep)
    mixed, logs[0] = attend_end(outs, tops, totals)
    so[...] = mixed
    all_mixed[:, group(n, BLOCK)] = mixed
    all_out[group(n, BLOCK)] = stacked(o, 1)

    @pl.when(n == 3)
    def last():
        after = x1[...] + dot(all_mixed[...], all_out[...])
        x2[...] = after
        n3[...] = low(modulated_norm(after, of_row(shifts, where, 4), of_row(shifts, where, 5)))


def grid_of(blocks, across):
    return jnp.concatenate(
        [stacked(blocks[i : i + across], 1) for i in range(0, len(blocks), across)], axis=0
    )


def feed_early_kernel(where, cotangent, *rest):
    down, grad_act = rest[:16], rest[16]
    grad_act[...] = dot_nt(cotangent[...], grid_of(down, 4))


def feed_kernel(where, x2, n3, cotangent, shifts, grad_act, *rest):
    up, down = rest[:16], rest[16:32]
    layer_out, g2, act, eh, total, back = rest[32:]
    f = pl.program_id(0)

    @pl.when(f == 0)
    def first():
        total[...] = x2[...]
        back[...] = jnp.zeros_like(back)

    root = (2.0 / np.pi) ** 0.5
    ups = [stacked(up[j::4], 0) for j in range(4)]
    hiddens = [dot(n3[...], ups[j]) for j in range(4)]
    for j, hidden in enumerate(hiddens):
        square = hidden * hidden
        bent = jnp.tanh(hidden * (root + (0.044715 * root) * square))
        gate = 0.5 * bent + 0.5
        value = hidden * gate
        act[:, part(j)] = low(value)
        slope = gate + value * (1.0 - gate) * (2.0 * root + (6.0 * 0.044715 * root) * square)
        eh[:, part(j)] = low(grad_act[:, part(j)] * slope)
    total[...] += dot(act[...], grid_of(down, 4))
    back[...] += dot_nt(eh[...], jnp.concatenate(ups, axis=1))

    @pl.when(f == FF // BLOCK // 4 - 1)
    def last():
        layer_out[...] = low(total[...])
        g2[...] = cotangent[...].astype(WIDE) + norm_back(x2[...], of_row(shifts, where, 5), back[...])


def feed_late_kernel(where, n3, cotangent, act, eh, store, turned, stage, sems):
    f = pl.program_id(0)
    wide = FF // BLOCK

    @pl.when(f == 0)
    def first():
        turned[...] = n3[...].T

    def products():
        up = low(dot(turned[...], eh[...]))
        down = low(dot(act[...].T, cotangent[...]))
        return [up[part(i), part(j)] for j in range(2) for i in range(4)] + [
            down[part(j), part(i)] for j in range(2) for i in range(4)
        ]

    numbers = [W_UP + i * wide + f * 2 + j for j in range(2) for i in range(4)]
    numbers += [W_DOWN + (f * 2 + j) * 4 + i for j in range(2) for i in range(4)]
    keep_blocks(products, stage, sems, store, where, numbers)


def self_backward_kernel(where, g2, sq, k_own, k_other, v_own, v_other, so, logs, *rest):
    q, k, v, o = rest[:4], rest[4:8], rest[8:12], rest[12:16]
    own_back, other_back, dq, dk, dv, es, probs, grads, sk, sv, own_total, other_total = rest[16:]
    n = pl.program_id(0)
    here = g2.shape[0]
    both = 2 * here

    @pl.when(n == 0)
    def first():
        es[...] = low(g2[...])
        own_total[...] = jnp.zeros_like(own_total)
        other_total[...] = jnp.zeros_like(other_total)

    grad_mixed = low(by_rows(es, o))
    sk[:here] = k_own[...]
    sk[here:] = k_other[...]
    sv[:here] = v_own[...]
    sv[here:] = v_other[...]
    wide_dq, wide_dk, wide_dv = attend_back(
        sq, sk, sv, sk[...].T, so[...], grad_mixed, logs[0], probs, grads, None, both
    )
    dq[...] = low(wide_dq)
    dk[...] = low(wide_dk)
    dv[...] = low(wide_dv)
    key_values = jnp.concatenate([stacked(k, 0), stacked(v, 0)], axis=1)
    both_grads = jnp.concatenate([dk[...], dv[...]], axis=1)
    own_total[...] += dot_nt(
        jnp.concatenate([dq[...], both_grads[:here]], axis=1),
        jnp.concatenate([stacked(q, 0), key_values], axis=1),
    )
    other_total[...] += dot_nt(both_grads[here:], key_values)

    @pl.when(n == 3)
    def last():
        own_back[...] = own_total[...]
        other_back[...] = low(other_total[...])


def self_late_kernel(where, g2, own_turned, other_turned, dq, dk, dv, so, old, store, es, turned, stage, sems):
    n = pl.program_id(0)
    here = g2.shape[0]

    @pl.when(n == 0)
    def first():
        es[...] = low(g2[...])
        turned[:, :here] = own_turned[...]
        turned[:, here:] = other_turned[...]

    def products():
        query = low(dot(own_turned[...], dq[...]))
        pair = low(dot(turned[...], jnp.concatenate([dk[...], dv[...]], axis=1)))
        flat = low(dot(so[...].T, es[...]))
        blocks = [query[part(i)] for i in range(4)]
        blocks += [pair[part(i), part(j)] for j in range(2) for i in range(4)]
        return blocks + [flat[:, part(i)] for i in range(4)]

    numbers = [base + i * 4 + n for base in (Q_SELF, K_SELF, V_SELF) for i in range(4)]
    numbers += [O_SELF + n * 4 + i for i in range(4)]
    keep_blocks(products, stage, sems, store, where, numbers)


def cross_backward_kernel(
    parts, where, x, g2, x1, own_back, got_back, turned, shifts, normed_turned, cq, ck, cv, co, logs, *rest
):
    q, k, v, o = rest[:4], rest[4:7], rest[7:10], rest[10:14]
    grad_x, grad_own, grad_others, store, grad_tokens, ec, g1, probs, grads, x_total, keys_padded, rows_padded, valid, stage, sems = rest[15:]
    n = pl.program_id(0)
    count = ck.shape[0]

    @pl.when(n == 0)
    def first():
        value = g2[...] + norm_back(
            x1[...], of_row(shifts, where, 3), own_back[...] + got_back[...].astype(WIDE)
        )
        g1[...] = value
        ec[...] = low(value)
        x_total[...] = jnp.zeros_like(x_total)
        grad_tokens[...] = jnp.zeros_like(grad_tokens)
        keys_padded[count:] = jnp.zeros_like(keys_padded[count:])
        for i in range(2):
            grads[i, count:] = jnp.zeros_like(grads[i, count:])
        rows_padded[count:] = jnp.zeros_like(rows_padded[count:])
        fill_valid(valid, where, parts)

    grad_mixed = low(by_rows(ec, o))
    keys_padded[:count] = ck[...]
    dq, dk, dv = attend_back(
        cq, ck, cv, keys_padded[...].T, co[...], grad_mixed, logs[0], probs, grads, valid[...], count
    )
    dq = low(dq)
    rows_padded[:count, :BLOCK] = low(dk)
    rows_padded[:count, BLOCK:] = low(dv)
    x_total[...] += dot_nt(dq, stacked(q, 0))
    grad_tokens[...] += dot_nt(
        rows_padded[:count],
        jnp.concatenate([stacked(k, 0), stacked(v, 0)], axis=1),
    )

    def products():
        query = low(dot(normed_turned[...], dq))
        pair = low(dot(turned[...], rows_padded[...]))
        flat = low(dot(co[...].T, ec[...]))
        blocks = [query[part(i)] for i in range(4)]
        blocks += [pair[part(i), part(j)] for j in range(2) for i in range(3)]
        return blocks + [flat[:, part(i)] for i in range(4)]

    numbers = [Q_CROSS + i * 4 + n for i in range(4)]
    numbers += [base + i * 4 + n for base in (K_CROSS, V_CROSS) for i in range(3)]
    numbers += [O_CROSS + n * 4 + i for i in range(4)]
    keep_blocks(products, stage, sems, store, where, numbers)

    @pl.when(n == 3)
    def last():
        half = grad_own.shape[0]
        grad_own[...] = grad_tokens[:half]
        grad_others[...] = low(grad_tokens[half:])
        grad_x[...] = g1[...] + norm_back(x[...].astype(WIDE), of_row(shifts, where, 1), x_total[...])


def shape(*dims, kind=LOW):
    return jax.ShapeDtypeStruct(dims, kind)


def call(kernel, grid, where, ins, outs, scratch, products, aliases=None, room=32):
    moved = BLOCK * BLOCK * 2 * grid * 16
    return pl.pallas_call(
        kernel,
        grid_spec=pltpu.PrefetchScalarGridSpec(
            num_scalar_prefetch=1,
            grid=(grid,),
            in_specs=[spec for _, spec in ins],
            out_specs=[spec for _, spec in outs],
            scratch_shapes=scratch,
        ),
        out_shape=[struct for struct, _ in outs],
        input_output_aliases=aliases or {},
        compiler_params=pltpu.CompilerParams(vmem_limit_bytes=room * 1024 * 1024),
        cost_estimate=pl.CostEstimate(
            flops=int(2 * products), bytes_accessed=moved, transcendentals=0
        ),
    )(where, *[array for array, _ in ins])


def full(array):
    return (array, whole(array.shape, pl.Buffered(1)))


def of_object(modulation):
    return full(modulation)


def made(*dims, kind=LOW):
    return (shape(*dims, kind=kind), whole(dims))


def striped(height):
    return (shape(height, D), stripe(height))


LOG_SPEC = pl.BlockSpec((1, 8, TOK_DEV), lambda n, where: (n, 0, 0))
ANYWHERE = pl.BlockSpec(memory_space=pl.ANY)


def padded_to(count):
    return -(-count // 128) * 128


def cross_forward(where, store, x, n1, tokens, shifts, parts):
    here, count = x.shape[0], tokens.shape[0]
    padded = padded_to(count)
    specs = columns(Q_CROSS, 4, 4) + columns(K_CROSS, 3, 4) + columns(V_CROSS, 3, 4) + rows(O_CROSS, 4)
    return call(
        functools.partial(cross_forward_kernel, parts),
        4,
        where,
        [full(x), full(n1), full(tokens), of_object(shifts)] + [(store, spec) for spec in specs],
        [
            striped(here),
            striped(count),
            striped(count),
            striped(here),
            (shape(4, 8, here, kind=WIDE), LOG_SPEC),
            made(here, D, kind=WIDE),
            made(here, D),
        ],
        [
            pltpu.VMEM((here, D), LOW),
            pltpu.VMEM((D, D), LOW),
            pltpu.VMEM((padded, BLOCK), LOW),
            pltpu.VMEM((2, padded, 2 * here), LOW),
            pltpu.VMEM((count, 128), WIDE),
        ],
        here * D * D * 12,
        room=34,
    )


def tall(here):
    return pl.BlockSpec((BLOCK, here), lambda n, where: (n, 0))


def self_own(where, store, mine):
    here = mine.shape[0]
    specs = columns(Q_SELF, 4, 4) + columns(K_SELF, 4, 4) + columns(V_SELF, 4, 4)
    return call(
        self_own_kernel,
        4,
        where,
        [full(mine)] + [(store, spec) for spec in specs],
        [
            made(D, here),
            striped(here),
            striped(here),
            striped(here),
            (shape(D, here, kind=WIDE), tall(here)),
            (shape(4, 8, here, kind=WIDE), LOG_SPEC),
        ],
        [pltpu.VMEM((2, here, 2 * here), LOW)],
        here * D * D * 6,
    )


def self_other(where, store, x1, other, shifts, sq, mix, stats):
    here = x1.shape[0]
    specs = columns(K_SELF, 4, 4) + columns(V_SELF, 4, 4) + rows(O_SELF, 4)
    return call(
        self_other_kernel,
        4,
        where,
        [full(x1), full(other), of_object(shifts), (sq, stripe(here)), (mix, tall(here)), (stats, LOG_SPEC)]
        + [(store, spec) for spec in specs],
        [
            made(D, here),
            striped(here),
            striped(here),
            striped(here),
            (shape(4, 8, here, kind=WIDE), LOG_SPEC),
            made(here, D, kind=WIDE),
            made(here, D),
        ],
        [pltpu.VMEM((here, D), LOW), pltpu.VMEM((D, D), LOW), pltpu.VMEM((2, here, 2 * here), LOW)],
        here * D * D * 6,
    )


def feed_specs(height):
    wide = FF // BLOCK
    up = [
        pl.BlockSpec(
            (1, BLOCK, BLOCK),
            lambda n, where, i=i, j=j: (where[W_UP + i * wide + n * height + j], 0, 0),
        )
        for i in range(4)
        for j in range(height)
    ]
    down = [
        pl.BlockSpec(
            (1, BLOCK, BLOCK), lambda n, where, i=i: (where[W_DOWN + n * height * 4 + i], 0, 0)
        )
        for i in range(4 * height)
    ]
    return up, down


def broad(here, height):
    return pl.BlockSpec((here, height * BLOCK), lambda n, where: (0, n))


def feed_early(where, store, cotangent):
    here = cotangent.shape[0]
    return call(
        feed_early_kernel,
        FF // BLOCK // 4,
        where,
        [full(cotangent)] + [(store, spec) for spec in feed_specs(4)[1]],
        [(shape(here, FF, kind=WIDE), broad(here, 4))],
        [],
        here * D * FF,
    )[0]


def feed(where, store, x2, n3, cotangent, shifts, grad_act):
    here = x2.shape[0]
    up, down = feed_specs(4)
    return call(
        feed_kernel,
        FF // BLOCK // 4,
        where,
        [full(x2), full(n3), full(cotangent), of_object(shifts), (grad_act, broad(here, 4))]
        + [(store, spec) for spec in up + down],
        [
            made(here, D),
            made(here, D, kind=WIDE),
            (shape(here, FF), broad(here, 4)),
            (shape(here, FF), broad(here, 4)),
        ],
        [pltpu.VMEM((here, D), WIDE), pltpu.VMEM((here, D), WIDE)],
        here * D * FF * 3,
        room=32,
    )


def feed_late(where, n3, cotangent, act, eh, slots):
    here = n3.shape[0]
    return call(
        feed_late_kernel,
        FF // BLOCK // 2,
        where,
        [full(n3), full(cotangent), (act, broad(here, 2)), (eh, broad(here, 2))],
        [(shape(slots, BLOCK, BLOCK), ANYWHERE)],
        [
            pltpu.VMEM((D, here), LOW),
            pltpu.VMEM((2, 16, BLOCK, BLOCK), LOW),
            pltpu.SemaphoreType.DMA((2, 16)),
        ],
        here * D * FF * 2,
        room=26,
    )[0]


def self_backward(where, store, g2, sq, k_own, k_other, v_own, v_other, so, logs):
    here = g2.shape[0]
    specs = columns(Q_SELF, 4, 4) + columns(K_SELF, 4, 4) + columns(V_SELF, 4, 4) + rows(O_SELF, 4)
    ins = [full(g2)] + [(a, stripe(here)) for a in (sq, k_own, k_other, v_own, v_other, so)]
    ins += [(logs, LOG_SPEC)] + [(store, spec) for spec in specs]
    return call(
        self_backward_kernel,
        4,
        where,
        ins,
        [made(here, D, kind=WIDE), made(here, D), striped(here), striped(2 * here), striped(2 * here)],
        [
            pltpu.VMEM((here, D), LOW),
            pltpu.VMEM((1, 2 * here, 2 * here), LOW),
            pltpu.VMEM((1, 2 * here, 2 * here), LOW),
            pltpu.VMEM((2 * here, BLOCK), LOW),
            pltpu.VMEM((2 * here, BLOCK), LOW),
            pltpu.VMEM((here, D), WIDE),
            pltpu.VMEM((here, D), WIDE),
        ],
        here * D * D * 16,
        room=28,
    )


def self_late(where, grads, g2, own_turned, other_turned, dq, dk, dv, so):
    here = g2.shape[0]
    ins = [full(a) for a in (g2, own_turned, other_turned)]
    ins += [(a, stripe(a.shape[0])) for a in (dq, dk, dv, so)] + [(grads, ANYWHERE)]
    return call(
        self_late_kernel,
        4,
        where,
        ins,
        [(shape(*grads.shape), ANYWHERE)],
        [
            pltpu.VMEM((here, D), LOW),
            pltpu.VMEM((D, 2 * here), LOW),
            pltpu.VMEM((2, 16, BLOCK, BLOCK), LOW),
            pltpu.SemaphoreType.DMA((2, 16)),
        ],
        here * D * D * 6,
        {len(ins): 0},
        room=30,
    )[0]


def cross_backward(
    where, store, grads, x, g2, x1, own_back, got_back, turned, shifts, normed_turned, cq, ck, cv, co, logs, parts
):
    here, count = x.shape[0], ck.shape[0]
    padded = padded_to(count)
    specs = columns(Q_CROSS, 4, 4) + columns(K_CROSS, 3, 4) + columns(V_CROSS, 3, 4) + rows(O_CROSS, 4)
    ins = [full(a) for a in (x, g2, x1, own_back, got_back, turned)]
    ins += [of_object(shifts), full(normed_turned)]
    ins += [(a, stripe(a.shape[0])) for a in (cq, ck, cv, co)] + [(logs, LOG_SPEC)]
    ins += [(store, spec) for spec in specs] + [(grads, ANYWHERE)]
    return call(
        functools.partial(cross_backward_kernel, parts),
        4,
        where,
        ins,
        [
            made(here, D, kind=WIDE),
            made(count // parts, DIMG, kind=WIDE),
            made(count - count // parts, DIMG),
            (shape(*grads.shape), ANYWHERE),
        ],
        [
            pltpu.VMEM((count, DIMG), WIDE),
            pltpu.VMEM((here, D), LOW),
            pltpu.VMEM((here, D), WIDE),
            pltpu.VMEM((2, padded, 2 * here), LOW),
            pltpu.VMEM((2, padded, 2 * here), LOW),
            pltpu.VMEM((here, D), WIDE),
            pltpu.VMEM((padded, BLOCK), LOW),
            pltpu.VMEM((padded, 2 * BLOCK), LOW),
            pltpu.VMEM((count, 128), WIDE),
            pltpu.VMEM((2, 14, BLOCK, BLOCK), LOW),
            pltpu.SemaphoreType.DMA((2, 14)),
        ],
        here * D * D * 24,
        {len(ins): 3},
        room=40,
    )


def hand_on_kernel(*refs):
    count = len(refs) // 2
    for source, target in zip(refs[:count], refs[count:-1]):
        target[...] = source[...]
    refs[-1][...] = low(refs[count - 1][...])


def hand_on(arrays):
    specs = [
        pl.BlockSpec((a.shape[0] // 4,) + a.shape[1:], lambda i: (i, 0, 0)) for a in arrays
    ]
    structs = [jax.ShapeDtypeStruct(a.shape, a.dtype) for a in arrays]
    return pl.pallas_call(
        hand_on_kernel,
        grid=(4,),
        out_shape=structs + [jax.ShapeDtypeStruct(arrays[-1].shape, LOW)],
        in_specs=specs,
        out_specs=specs + specs[-1:],
        compiler_params=pltpu.CompilerParams(vmem_limit_bytes=VLIM),
    )(*arrays)


def partner(block, axis):
    size = lax.axis_size(axis)
    return lax.ppermute(block, axis, [(i, i ^ 1) for i in range(size)])


def soap_update(
    slot_grads,
    first_moment,
    second_moment,
    left_basis,
    right_basis,
    master_weights,
    slot_rates,
    slot_used,
):
    keep_mask = slot_used[:, None, None] > 0.0
    slot_grads = jnp.where(keep_mask, slot_grads, 0.0)
    rotated = jnp.matmul(
        jnp.matmul(jnp.swapaxes(left_basis, 1, 2), slot_grads, precision=highest),
        right_basis,
        precision=highest,
    )
    first_new = moment_decay * first_moment + (1.0 - moment_decay) * rotated
    second_new = moment_decay * second_moment + (1.0 - moment_decay) * rotated * rotated
    correction = 1.0 - moment_decay**STEP
    normalized = first_new / correction / (jnp.sqrt(second_new / correction) + 1e-08)
    rotated_back = jnp.matmul(
        jnp.matmul(left_basis, normalized, precision=highest),
        jnp.swapaxes(right_basis, 1, 2),
        precision=highest,
    )
    fresh_master = master_weights - slot_rates[:, None, None] * (
        rotated_back + 0.01 * master_weights
    )
    fresh_master = jnp.where(keep_mask, fresh_master, 0.0)
    return (
        slot_grads,
        jnp.where(keep_mask, first_new, 0.0),
        jnp.where(keep_mask, second_new, 0.0),
        fresh_master,
        fresh_master.astype(jnp.bfloat16),
    )


def shards(
    triplane,
    cotangent,
    image_tokens,
    modulation,
    image_counts,
    owner_slots,
    master_weights,
    first_moment,
    second_moment,
    left_basis,
    right_basis,
):
    img_size = lax.axis_size("img")
    rows_size = lax.axis_size("rows")
    img_index = lax.axis_index("img")
    flat_index = lax.axis_index("rows") * img_size + img_index
    object_index = flat_index // 2
    pair_index = img_index // 2
    groups = img_size // 2
    slot_cap = image_tokens.shape[0] // groups
    own_count = master_weights.shape[0]
    slot_total = rows_size * img_size * own_count
    fits = rows_size == 16 and img_size == 2 and own_count == 8
    modulation = jnp.swapaxes(modulation, 0, 1)
    info = [object_index[None]]
    if img_size == 2:
        info += [img_index[None], 1 - img_index[None]]
    else:
        info += [jnp.arange(img_size, dtype=jnp.int32)]
    info += [image_counts]
    if fits:
        store, tokens, tokens_turned, n1, n1_turned = gather(
            master_weights, image_tokens, triplane, modulation
        )
        store = store.reshape(-1, BLOCK, BLOCK)
        where = [positions(owner_slots, WAYS_OUT), positions(owner_slots, WAYS_IN)]
    else:
        store = lax.all_gather(master_weights.astype(LOW), ("rows", "img"), axis=0, tiled=True)
        where = [owner_slots, owner_slots]
        if img_size == 2:
            tokens = jnp.concatenate([image_tokens, partner(image_tokens, "img")], 0)
        else:
            tokens = lax.all_gather(image_tokens, "img", axis=0, tiled=True)
            tokens = tokens.reshape(img_size, groups, slot_cap, DIMG)
            tokens = lax.dynamic_index_in_dim(tokens, pair_index, 1, keepdims=False)
            tokens = tokens.reshape(img_size * slot_cap, DIMG)
        count = tokens.shape[0]
        tokens_turned = jnp.pad(tokens.T, ((0, 0), (0, padded_to(count) - count)))
        shifts = lax.dynamic_index_in_dim(modulation, object_index, 1, keepdims=False)
        n1 = low(modulated_norm(triplane.astype(WIDE), shifts[0], shifts[1]))
        n1_turned = n1.T
    where = jnp.concatenate([piece.astype(jnp.int32) for piece in where + info])

    cq, ck, cv, co, cross_logs, x1, n2 = cross_forward(
        where, store, triplane, n1, tokens, modulation, img_size
    )
    n2_other = partner(n2, "img")
    own_turned, sq, k_own, v_own, mix, stats = self_own(where, store, n2)
    grad_act = feed_early(where, store, cotangent)
    other_turned, k_other, v_other, so, self_logs, x2, n3 = self_other(
        where, store, x1, n2_other, modulation, sq, mix, stats
    )
    layer_out, g2, act, eh = feed(where, store, x2, n3, cotangent, modulation, grad_act)
    own_back, other_back, dq, dk, dv = self_backward(
        where, store, g2, sq, k_own, k_other, v_own, v_other, so, self_logs
    )
    got_back = partner(other_back, "img")
    grads = feed_late(where, n3, cotangent, act, eh, slot_total)
    grads = self_late(where, grads, g2, own_turned, other_turned, dq, dk, dv, so)
    grad_triplane, grad_own, grad_others, grads = cross_backward(
        where,
        store,
        grads,
        triplane,
        g2,
        x1,
        own_back,
        got_back,
        tokens_turned,
        modulation,
        n1_turned,
        cq,
        ck,
        cv,
        co,
        cross_logs,
        img_size,
    )
    if img_size == 2:
        grad_image = grad_own + partner(grad_others, "img").astype(WIDE)
    else:
        pick = (jnp.arange(groups, dtype=jnp.int32) == pair_index).astype(WIDE)
        grad_tokens = jnp.concatenate([grad_own, grad_others.astype(WIDE)], 0)
        spread = grad_tokens.reshape(img_size, 1, slot_cap, DIMG) * pick[None, :, None, None]
        grad_image = lax.psum_scatter(
            spread.reshape(img_size * groups * slot_cap, DIMG).astype(LOW),
            "img",
            scatter_dimension=0,
            tiled=True,
        ).astype(WIDE)
    my_slots = flat_index * own_count + jnp.arange(own_count, dtype=jnp.int32)
    matched = (owner_slots[:, None] == my_slots[None, :]).astype(WIDE)
    slot_used = jnp.sum(matched, axis=0)
    slot_rates = jnp.sum(matched * jnp.asarray(block_table(weight_scales()))[:, None], axis=0)
    state = (first_moment, second_moment, left_basis, right_basis, master_weights)
    if fits:
        rates = jnp.broadcast_to(
            jnp.stack([slot_rates, slot_used], 1)[:, :, None], (own_count, 2, BLOCK)
        )
        updated = hand_on(scatter(grads.reshape(2, 8, 16, BLOCK, BLOCK), *state, rates))
    else:
        used = jnp.zeros((slot_total,), jnp.bool_).at[owner_slots].set(True)
        grads = jnp.where(used[:, None, None], grads, jnp.zeros_like(grads))
        slot_grads = lax.psum_scatter(
            grads, ("rows", "img"), scatter_dimension=0, tiled=True
        ).astype(WIDE)
        updated = soap_update(slot_grads, *state, slot_rates, slot_used)
    return (layer_out, grad_triplane, grad_image) + tuple(updated)


def solution(mesh):
    flat = P(("rows", "img"), None)
    blocks = P(("rows", "img"), None, None)
    in_specs = (flat, flat, flat, P(), P(), P()) + (blocks,) * 5
    out_specs = (flat, flat, flat) + (blocks,) * 5
    return jax.shard_map(shards, mesh=mesh, in_specs=in_specs, out_specs=out_specs, check_vma=False)
```

```python
import functools

import jax
import jax.numpy as jnp
import numpy as np
from jax import lax
from jax.experimental import pallas as pl
from jax.experimental.pallas import tpu as pltpu
from jax.sharding import PartitionSpec as P

D = 1024
HEADS = 16
FF = 4096
DIMG = 768
TOK_DEV = 384
IMG_MAX = 1025
BLOCK = 256
STEP = 5
HEAD = D // HEADS

MESH = pl.DeviceIdType.MESH
VLIM = 60 * 1024 * 1024
WAYS_OUT = (
    ('lo', 'hi', 'y', 'x'),
    ('hi', 'lo', 'x', 'y'),
    ('y', 'x', 'hi', 'lo'),
    ('hi', 'lo', 'x', 'y'),
    ('hi', 'x', 'lo', 'y'),
    ('lo', 'y', 'hi', 'x'),
    ('hi', 'y', 'lo', 'x'),
    ('hi', 'x', 'y', 'lo'),
)
WAYS_IN = (
    ('lo', 'y', 'hi', 'x'),
    ('hi', 'x', 'y', 'lo'),
    ('hi', 'y', 'x', 'lo'),
    ('hi', 'lo', 'x', 'y'),
    ('hi', 'x', 'lo', 'y'),
    ('hi', 'y', 'lo', 'x'),
    ('hi', 'lo', 'x', 'y'),
    ('lo', 'hi', 'y', 'x'),
)
FRONT = 17
ORDER_OUT = (
    (6, 0), (2, 0), (2, 1), (0, 0), (5, 0), (3, 0), (6, 1), (-1, 0),
    (3, 1), (1, 0), (5, 1), (4, 0), (1, 1), (3, 2), (4, 1), (0, 1),
    (0, 2), (6, 2), (7, 0), (7, 1), (4, 2), (3, 3), (5, 2), (0, 3),
    (7, 2), (3, 4), (1, 2), (7, 3), (6, 3), (5, 3), (2, 2), (4, 3),
    (0, 4), (7, 4), (2, 3), (4, 4), (1, 3), (6, 4), (1, 4), (5, 4),
    (2, 4),
)
ORDER_IN = (
    (0, 0), (1, 0), (2, 0), (3, 0), (4, 0), (5, 0), (6, 0), (7, 0),
    (1, 1), (0, 1), (4, 1), (0, 2), (7, 1), (4, 2), (6, 1), (2, 1),
    (7, 2), (5, 1), (5, 2), (6, 2), (1, 2), (0, 3), (7, 3), (6, 3),
    (1, 3), (3, 1), (1, 4), (4, 3), (7, 4), (2, 2), (4, 4), (2, 3),
    (6, 4), (3, 2), (0, 4), (5, 3), (4, 5), (6, 5), (2, 4), (7, 5),
    (3, 3), (2, 5), (5, 4), (1, 5), (0, 5), (5, 5), (3, 4), (3, 5),
)


def coords():
    row = lax.axis_index("rows")
    rest = lax.rem(row, 4)
    return lax.div(row, 4), lax.div(rest, 2), lax.rem(rest, 2), lax.axis_index("img")


def neighbour(kind):
    z, x, c, y = coords()
    if kind == "c":
        c = 1 - c
    if kind == "x":
        x = 1 - x
    if kind == "y":
        y = 1 - y
    if kind == "lo":
        z = z + 1 - 2 * lax.rem(z, 2)
    if kind == "hi":
        z = lax.rem(z + 2, 4)
    return (z * 4 + x * 2 + c, y)


def place(way):
    z, x, c, y = coords()
    bits = {"x": x, "y": y, "lo": lax.rem(z, 2), "hi": lax.div(z, 2)}
    return sum(bits[kind] * 2**k for k, kind in enumerate(way))


def positions(slot, ways):
    owner, j = slot // 8, slot % 8
    z, x, c, y = owner // 8, owner // 4 % 2, owner // 2 % 2, owner % 2
    bits = {"x": x, "y": y, "lo": z % 2, "hi": z // 2}
    total = (c * 8 + j) * 16
    for kind, bit in bits.items():
        total = total + bit * jnp.asarray([2 ** way.index(kind) for way in ways], jnp.int32)[j]
    return total


def greet():
    barrier = pltpu.get_barrier_semaphore()
    for kind in ("c", "x", "y", "lo", "hi"):
        pl.semaphore_signal(barrier, inc=1, device_id=neighbour(kind), device_id_type=MESH)
    pl.semaphore_wait(barrier, 5)


def gather_kernel(
    master, tokens, triplane, modulation, out, both, turned, n1, n1_turned,
    own, wide, mine, x, shifts, others, spread, upright, lsem, csem, ssem, rsem, tsem,
):
    c = coords()[2]
    early = [
        pltpu.make_async_copy(source, target, lsem.at[i])
        for i, (source, target) in enumerate(
            ((master, wide), (tokens, mine), (triplane, x), (modulation, shifts))
        )
    ]
    for copy in early:
        copy.start()
    greet()
    cross = pltpu.make_async_remote_copy(
        tokens, others, tsem.at[0], tsem.at[1], device_id=neighbour("y"), device_id_type=MESH
    )
    early[0].wait()
    copies, keeps = {}, {}

    def start(j, k):
        base = place(WAYS_OUT[j])
        count = 2**k
        first = lax.div(base, count) * count if k < 4 else 0
        here = pl.ds(first, count)
        source = own.at[pl.ds(j, 1)] if k == 0 else out.at[c, j, here]
        copy = pltpu.make_async_remote_copy(
            source,
            out.at[c, j, here],
            ssem.at[j, k],
            rsem.at[j, k],
            device_id=neighbour((WAYS_OUT[j] + ("c",))[k]),
            device_id_type=MESH,
        )
        copy.start()
        copies[j, k] = copy

    for j, k in ORDER_OUT:
        if j < 0:
            cross.start()
        elif k == 0:
            own[j] = wide[j].astype(jnp.bfloat16)
            start(j, 0)
            keep = pltpu.make_async_copy(
                own.at[pl.ds(j, 1)], out.at[c, j, pl.ds(place(WAYS_OUT[j]), 1)], csem.at[j]
            )
            keep.start()
            keeps[j] = keep
        else:
            if k == 1:
                keeps[j].wait()
            copies[j, k - 1].wait_recv()
            start(j, k)
        if (j, k) == ORDER_OUT[FRONT]:
            row = pl.ds(lax.axis_index("rows"), 1)
            early[2].wait()
            early[3].wait()
            one = modulated_norm(
                x[...].astype(jnp.float32), shifts[0, row], shifts[1, row]
            )
            n1[...] = one.astype(jnp.bfloat16)
            n1_turned[...] = one.astype(jnp.bfloat16).T
        if (j, k) == ORDER_OUT[min(max(FRONT + 6, ORDER_OUT.index((-1, 0)) + 9), len(ORDER_OUT) - 1)]:
            half = tokens.shape[0]
            cross.wait()
            early[1].wait()
            spread[:half] = mine[...].astype(jnp.float32)
            spread[half:] = others[...].astype(jnp.float32)
            both[...] = spread[...].astype(jnp.bfloat16)
            upright[2 * half :] = jnp.zeros_like(upright[2 * half :])
            for i in range(tokens.shape[1] // BLOCK):
                lanes = slice(i * BLOCK, (i + 1) * BLOCK)
                upright[: 2 * half] = both[:, lanes]
                turned[lanes] = upright[...].T
    for j in range(8):
        copies[j, 4].wait_recv()
    for copy in copies.values():
        copy.wait_send()


def gather(master, tokens, x, modulation):
    anywhere, inside = pl.BlockSpec(memory_space=pl.ANY), pl.BlockSpec(memory_space=pltpu.VMEM)
    half, width = tokens.shape
    padded = -(-2 * half // 128) * 128
    bf = jnp.bfloat16
    return pl.pallas_call(
        gather_kernel,
        out_shape=[
            jax.ShapeDtypeStruct((2, 8, 16, BLOCK, BLOCK), bf),
            jax.ShapeDtypeStruct((2 * half, width), bf),
            jax.ShapeDtypeStruct((width, padded), bf),
            jax.ShapeDtypeStruct(x.shape, bf),
            jax.ShapeDtypeStruct(x.shape[::-1], bf),
        ],
        in_specs=[anywhere] * 4,
        out_specs=[anywhere] + [inside] * 4,
        scratch_shapes=[
            pltpu.VMEM((8, BLOCK, BLOCK), bf),
            pltpu.VMEM((8, BLOCK, BLOCK), jnp.float32),
            pltpu.VMEM((half, width), bf),
            pltpu.VMEM(x.shape, bf),
            pltpu.VMEM(modulation.shape, jnp.float32),
            pltpu.VMEM((half, width), bf),
            pltpu.VMEM((2 * half, width), jnp.float32),
            pltpu.VMEM((padded, BLOCK), bf),
            pltpu.SemaphoreType.DMA((4,)),
            pltpu.SemaphoreType.DMA((8,)),
            pltpu.SemaphoreType.DMA((8, 5)),
            pltpu.SemaphoreType.DMA((8, 5)),
            pltpu.SemaphoreType.DMA((2,)),
        ],
        compiler_params=pltpu.CompilerParams(
            collective_id=11, has_side_effects=True, vmem_limit_bytes=VLIM
        ),
    )(master, tokens, x, modulation)


def times(a, b, left, right):
    def product(one, two):
        return lax.dot_general(
            one, two, (((left,), (right,)), ((), ())), preferred_element_type=jnp.float32
        )

    a_high, b_high = a.astype(jnp.bfloat16), b.astype(jnp.bfloat16)
    a_low = (a - a_high.astype(jnp.float32)).astype(jnp.bfloat16)
    b_low = (b - b_high.astype(jnp.float32)).astype(jnp.bfloat16)
    return product(a_high, b_high) + (product(a_high, b_low) + product(a_low, b_high))


def scatter_kernel(grads, first, second, left, right, master, rates, *rest):
    outs = rest[:4]
    own, r0, r1, r2, r3, r4, held, made, lsem, ssem, rsem, hsem, osem = rest[4:]
    c = coords()[2]
    got = (r0, r1, r2, r3, r4)
    loads, copies, fetches, puts = [], {}, {}, {}
    for j in range(8):
        load = pltpu.make_async_copy(grads.at[c, j], own.at[j], lsem.at[j])
        load.start()
        loads.append(load)
    greet()

    def exchange(j, s, source, kind):
        copy = pltpu.make_async_remote_copy(
            source,
            got[s].at[j],
            ssem.at[j, s],
            rsem.at[j, s],
            device_id=neighbour(kind),
            device_id_type=MESH,
        )
        copy.start()
        copies[j, s] = copy

    def add(j, s):
        count = 16 >> s
        start = lax.div(place(WAYS_IN[j]), count) * count if s else 0

        def body(b, carry):
            own[j, start + b] = own[j, start + b] + got[s][j, b]
            return carry

        lax.fori_loop(0, count, body, 0)

    def send(j, s):
        count = 16 >> s
        half = lax.div(place(WAYS_IN[j]), count)
        other = (half + 1 - 2 * lax.rem(half, 2)) * count
        exchange(j, s, own.at[j, pl.ds(other, count)], WAYS_IN[j][4 - s])

    def fetch(turn, j):
        side = turn % 2
        fetches[turn] = [
            pltpu.make_async_copy(array.at[j], held.at[side, i], hsem.at[side, i])
            for i, array in enumerate((first, second, left, right, master))
        ]
        for copy in fetches[turn]:
            copy.start()

    def finish(turn, j):
        side = turn % 2
        for copy in fetches[turn]:
            copy.wait()
        if turn >= 2:
            for copy in puts[turn - 2]:
                copy.wait()
        base = place(WAYS_IN[j])
        used = rates[j, 1:2] > 0.0
        total = own[j, base].astype(jnp.float32) + r4[j, 0].astype(jnp.float32)
        total = jnp.where(used, total, 0.0)
        rotated = times(times(held[side, 2], total, 0, 0), held[side, 3], 1, 0)
        new_first = 0.5 * held[side, 0] + 0.5 * rotated
        new_second = 0.5 * held[side, 1] + 0.5 * rotated * rotated
        fix = 1.0 - 0.5**STEP
        unit = (new_first / fix) / (jnp.sqrt(new_second / fix) + 1e-08)
        update = times(times(held[side, 2], unit, 1, 0), held[side, 3], 1, 1)
        old = held[side, 4]
        new = jnp.where(used, old - rates[j, 0:1] * (update + 0.01 * old), 0.0)
        made[side, 0] = total
        made[side, 1] = jnp.where(used, new_first, 0.0)
        made[side, 2] = jnp.where(used, new_second, 0.0)
        made[side, 3] = new
        puts[turn] = [
            pltpu.make_async_copy(made.at[side, i], outs[i].at[j], osem.at[side, i])
            for i in range(4)
        ]
        for copy in puts[turn]:
            copy.start()

    ends = [j for j, s in ORDER_IN if s == 5]
    for turn in range(2):
        fetch(turn, ends[turn])
    turn = 0
    for j, s in ORDER_IN:
        if s == 0:
            exchange(j, 0, grads.at[1 - c, j], "c")
            continue
        if s == 1:
            loads[j].wait()
        copies[j, s - 1].wait_recv()
        if s < 5:
            add(j, s - 1)
            send(j, s)
        else:
            finish(turn, j)
            if turn < 6:
                fetch(turn + 2, ends[turn + 2])
            turn += 1
    for copy in puts[6] + puts[7]:
        copy.wait()
    for copy in copies.values():
        copy.wait_send()


def scatter(grads, first, second, left, right, master, rates):
    bf, wide, block = jnp.bfloat16, jnp.float32, (BLOCK, BLOCK)
    anywhere = pl.BlockSpec(memory_space=pl.ANY)
    return pl.pallas_call(
        scatter_kernel,
        out_shape=[jax.ShapeDtypeStruct((8,) + block, kind) for kind in (wide,) * 4],
        in_specs=[anywhere] * 6 + [pl.BlockSpec(memory_space=pltpu.VMEM)],
        out_specs=[anywhere] * 4,
        scratch_shapes=[pltpu.VMEM((8, count) + block, bf) for count in (16, 16, 8, 4, 2, 1)]
        + [
            pltpu.VMEM((2, 5) + block, wide),
            pltpu.VMEM((2, 4) + block, wide),
            pltpu.SemaphoreType.DMA((8,)),
            pltpu.SemaphoreType.DMA((8, 5)),
            pltpu.SemaphoreType.DMA((8, 5)),
            pltpu.SemaphoreType.DMA((2, 5)),
            pltpu.SemaphoreType.DMA((2, 4)),
        ],
        compiler_params=pltpu.CompilerParams(
            collective_id=12, has_side_effects=True, vmem_limit_bytes=54 * 1024 * 1024
        ),
    )(grads, first, second, left, right, master, rates)


highest = lax.Precision.HIGHEST
moment_decay = 0.5
LOW = jnp.bfloat16
WIDE = jnp.float32

def shapes_list():
    return [(D, D), (DIMG, D), (DIMG, D), (D, D), (D, D), (D, D), (D, D), (D, D), (D, FF), (FF, D)]


Q_CROSS, K_CROSS, V_CROSS, O_CROSS, Q_SELF, K_SELF, V_SELF, O_SELF, W_UP, W_DOWN = (
    int(v) for v in np.cumsum([0] + [a * b // BLOCK**2 for a, b in shapes_list()])[:10]
)


NBLK = W_DOWN + FF * D // BLOCK**2


def weight_scales():
    self_root = (2.0 * TOK_DEV) ** 0.5
    cross_root = (IMG_MAX / 2.0) ** 0.5
    return [
        D ** (-0.5),
        DIMG ** (-0.5),
        DIMG ** (-0.5),
        0.5 * cross_root * D ** (-0.5),
        D ** (-0.5),
        D ** (-0.5),
        D ** (-0.5),
        0.5 * self_root * D ** (-0.5),
        D ** (-0.5),
        2.0 * FF ** (-0.5),
    ]


def block_table(scales):
    pieces = []
    for shape_pair, scale_value in zip(shapes_list(), scales):
        amount = shape_pair[0] * shape_pair[1] // (BLOCK * BLOCK)
        pieces.append(np.full((amount,), scale_value, np.float32))
    return np.concatenate(pieces)


def low(v):
    return v.astype(LOW)


def dot(a, b):
    return jnp.dot(a, b, preferred_element_type=WIDE)


def dot_nt(a, b):
    return lax.dot_general(a, b, (((1,), (1,)), ((), ())), preferred_element_type=WIDE)


def part(k):
    return slice(k * BLOCK, (k + 1) * BLOCK)


def norm_parts(values):
    centered = values - jnp.mean(values, axis=-1, keepdims=True)
    variance = jnp.mean(centered * centered, axis=-1, keepdims=True)
    return centered, lax.rsqrt(variance + 1e-06)


def modulated_norm(values, shift, scale):
    centered, inverse = norm_parts(values)
    return centered * inverse * (1.0 + scale) + shift


def norm_back(values, scale, grad_normed):
    centered, inverse = norm_parts(values)
    unit = centered * inverse
    grad_unit = grad_normed * (1.0 + scale)
    return inverse * (
        grad_unit
        - jnp.mean(grad_unit, axis=-1, keepdims=True)
        - unit * jnp.mean(grad_unit * unit, axis=-1, keepdims=True)
    )


def halves(pair):
    lane = lax.broadcasted_iota(jnp.int32, pair.shape, 1)
    zero = jnp.zeros_like(pair)
    return jnp.where(lane < HEAD, pair, zero), jnp.where(lane < HEAD, zero, pair)


def fill_valid(valid, where, parts):
    cap = valid.shape[0] // parts
    slot = lax.broadcasted_iota(jnp.int32, (cap, 128), 0)
    for i in range(parts):
        number = slot * parts + where[2 * NBLK + 1 + i]
        limit = where[2 * NBLK + 1 + parts + where[2 * NBLK]]
        valid[i * cap : (i + 1) * cap] = (number < limit).astype(WIDE)


def group(n, width):
    return pl.ds(pl.multiple_of(n * width, width), width)


def of_row(shifts, where, k):
    return shifts[k, pl.ds(where[2 * NBLK], 1)]


def masked(scores, valid):
    if valid is None:
        return scores
    wide = jnp.concatenate([valid] * (scores.shape[1] // valid.shape[1]), axis=1)
    return jnp.where(wide > 0.0, scores, -1e30)


def columns(base, tall, wide):
    return [
        pl.BlockSpec((1, BLOCK, BLOCK), lambda n, where, i=i: (where[base + i * wide + n], 0, 0))
        for i in range(tall)
    ]


def rows(base, wide):
    return [
        pl.BlockSpec((1, BLOCK, BLOCK), lambda n, where, k=k: (where[base + n * wide + k], 0, 0))
        for k in range(wide)
    ]


def whole(shape, mode=None):
    return pl.BlockSpec(shape, lambda n, where: (0,) * len(shape), pipeline_mode=mode)


def stripe(height):
    return pl.BlockSpec((height, BLOCK), lambda n, where: (0, n))


def stacked(blocks, axis):
    return jnp.concatenate([block[0] for block in blocks], axis=axis)


def by_columns(left, blocks):
    return dot(left[...], stacked(blocks, 0))


def by_rows(left, blocks):
    return dot_nt(left[...], stacked(blocks, 1))


def attend_part(queries, keys, values_turned, weights, valid, count):
    outs, tops, totals = [], [], []
    tokens = queries.shape[0]
    scores = []
    for pair in range(2):
        lanes = slice(pair * 2 * HEAD, (pair + 1) * 2 * HEAD)
        both = jnp.concatenate(halves(queries[:, lanes]), axis=0)
        scores.append(masked(dot_nt(keys[:count, lanes], both), valid))
    for pair in range(2):
        top = jnp.max(scores[pair], axis=0, keepdims=True)
        exponent = jnp.exp(scores[pair] - top)
        total = jnp.sum(exponent, axis=0, keepdims=True)
        weights[pair, :count] = low(exponent)
        tops += [top[:, :tokens], top[:, tokens:]]
        totals += [total[:, :tokens], total[:, tokens:]]
    for pair in range(2):
        lanes = slice(pair * 2 * HEAD, (pair + 1) * 2 * HEAD)
        mixed = dot(values_turned[lanes], weights[pair])
        outs += [mixed[:HEAD, :tokens], mixed[HEAD:, tokens:]]
    return outs, tops, totals


def attend_end(outs, tops, totals):
    turned = jnp.concatenate([out / total for out, total in zip(outs, totals)], axis=0)
    logs = [top + jnp.log(total) for top, total in zip(tops, totals)]
    return low(turned.T), jnp.concatenate(logs + logs, axis=0)


def attend_back(queries, keys, values, keys_turned, mixed, grad_mixed, logs, probs, grads, valid, count):
    tokens = queries.shape[0]
    inner = (mixed.astype(WIDE) * grad_mixed.astype(WIDE)).T
    inner = jnp.concatenate(
        [jnp.sum(inner[head * HEAD : (head + 1) * HEAD], axis=0, keepdims=True) for head in range(4)],
        axis=1,
    )
    logs = jnp.concatenate([logs[head : head + 1] for head in range(4)], axis=1)
    grad_query, grad_key, grad_value = [], [], []
    for pair in range(2):
        kept = pair % grads.shape[0]
        lanes = slice(pair * 2 * HEAD, (pair + 1) * 2 * HEAD)
        side = slice(pair * 2 * tokens, (pair + 1) * 2 * tokens)
        both_queries = jnp.concatenate(halves(queries[:, lanes]), axis=0)
        both_mixed = jnp.concatenate(halves(grad_mixed[:, lanes]), axis=0)
        scores = masked(dot_nt(keys[:count, lanes], both_queries), valid)
        grad_full = dot_nt(values[:count, lanes], both_mixed)
        full = jnp.exp(scores - logs[:, side])
        grads[kept, :count] = low(full * (grad_full - inner[:, side]))
        probs[kept, :count] = low(full)
        turned = dot(keys_turned[lanes], grads[kept])
        grad_query += [turned[:HEAD, :tokens], turned[HEAD:, tokens:]]
        grad_key.append(dot(grads[kept, :count], both_queries))
        grad_value.append(dot(probs[kept, :count], both_mixed))
    grad_query = jnp.concatenate(grad_query, axis=0).T * HEAD ** (-0.5)
    return grad_query, jnp.concatenate(grad_key, axis=1), jnp.concatenate(grad_value, axis=1)


def send_blocks(stage, sems, side, store, where, numbers):
    return [
        pltpu.make_async_copy(stage.at[side, i], store.at[where[NBLK + number]], sems.at[side, i])
        for i, number in enumerate(numbers)
    ]


def keep_blocks(products, stage, sems, store, where, numbers):
    step, steps = pl.program_id(0), pl.num_programs(0)
    side = lax.rem(step, 2)

    @pl.when(step >= 2)
    def reuse():
        for copy in send_blocks(stage, sems, side, store, where, numbers):
            copy.wait()

    for i, product in enumerate(products()):
        stage[side, i] = product
    for copy in send_blocks(stage, sems, side, store, where, numbers):
        copy.start()

    @pl.when(step == steps - 1)
    def drain():
        for copy in send_blocks(stage, sems, 1 - side, store, where, numbers):
            copy.wait()
        for copy in send_blocks(stage, sems, side, store, where, numbers):
            copy.wait()


def cross_forward_kernel(parts, where, x, n1, tokens, shifts, *rest):
    q, k, v, o = rest[:4], rest[4:7], rest[7:10], rest[10:14]
    cq, ck, cv, co, logs, x1, n2, all_mixed, all_out, turned, weights, valid = rest[14:]
    n = pl.program_id(0)
    count = tokens.shape[0]

    @pl.when(n == 0)
    def first():
        turned[count:] = jnp.zeros_like(turned[count:])
        for pair in range(2):
            weights[pair, count:] = jnp.zeros_like(weights[pair, count:])
        fill_valid(valid, where, parts)

    queries = low(by_columns(n1, q)) * HEAD ** (-0.5)
    cq[...] = queries
    pair = low(dot(tokens[...], jnp.concatenate([stacked(k, 0), stacked(v, 0)], axis=1)))
    ck[...] = pair[:, :BLOCK]
    cv[...] = pair[:, BLOCK:]
    turned[:count] = pair[:, BLOCK:]
    mixed, log_total = attend_end(
        *attend_part(queries, ck, turned[...].T, weights, valid[...], count)
    )
    co[...] = mixed
    logs[0] = log_total
    all_mixed[:, group(n, BLOCK)] = mixed
    all_out[group(n, BLOCK)] = stacked(o, 1)

    @pl.when(n == 3)
    def last():
        after = x[...].astype(WIDE) + dot(all_mixed[...], all_out[...])
        x1[...] = after
        n2[...] = low(modulated_norm(after, of_row(shifts, where, 2), of_row(shifts, where, 3)))


def self_own_kernel(where, mine, *rest):
    q, k, v = rest[:4], rest[4:8], rest[8:12]
    turned, sq, sk, sv, mix, stats, weights = rest[12:]
    n = pl.program_id(0)

    @pl.when(n == 0)
    def first():
        turned[...] = mine[...].T

    all_three = low(
        dot(mine[...], jnp.concatenate([stacked(q, 0), stacked(k, 0), stacked(v, 0)], axis=1))
    )
    queries = all_three[:, :BLOCK] * HEAD ** (-0.5)
    sq[...] = queries
    sk[...] = all_three[:, BLOCK : 2 * BLOCK]
    sv[...] = all_three[:, 2 * BLOCK :]
    outs, tops, totals = attend_part(queries, sk, sv[...].T, weights, None, mine.shape[0])
    mix[...] = jnp.concatenate(outs, axis=0)
    stats[0] = jnp.concatenate(tops + totals, axis=0)


def self_other_kernel(where, x1, other, shifts, sq, mix, stats, *rest):
    k, v, o = rest[:4], rest[4:8], rest[8:12]
    turned, sk, sv, so, logs, x2, n3, all_mixed, all_out, weights = rest[12:]
    n = pl.program_id(0)

    @pl.when(n == 0)
    def first():
        turned[...] = other[...].T

    pair = low(dot(other[...], jnp.concatenate([stacked(k, 0), stacked(v, 0)], axis=1)))
    sk[...] = pair[:, :BLOCK]
    sv[...] = pair[:, BLOCK:]
    parts = attend_part(sq[...], sk, sv[...].T, weights, None, other.shape[0])
    outs, tops, totals = [], [], []
    for head, (out, top, amount) in enumerate(zip(*parts)):
        old_top, old_amount = stats[0, head : head + 1], stats[0, 4 + head : 5 + head]
        new_top = jnp.maximum(top, old_top)
        grow, keep = jnp.exp(top - new_top), jnp.exp(old_top - new_top)
        outs.append(out * grow + mix[head * HEAD : (head + 1) * HEAD] * keep)
        tops.append(new_top)
        totals.append(amount * grow + old_amount * keep)
    mixed, logs[0] = attend_end(outs, tops, totals)
    so[...] = mixed
    all_mixed[:, group(n, BLOCK)] = mixed
    all_out[group(n, BLOCK)] = stacked(o, 1)

    @pl.when(n == 3)
    def last():
        after = x1[...] + dot(all_mixed[...], all_out[...])
        x2[...] = after
        n3[...] = low(modulated_norm(after, of_row(shifts, where, 4), of_row(shifts, where, 5)))


def grid_of(blocks, across):
    return jnp.concatenate(
        [stacked(blocks[i : i + across], 1) for i in range(0, len(blocks), across)], axis=0
    )


def feed_early_kernel(where, cotangent, *rest):
    down, grad_act = rest[:16], rest[16]
    grad_act[...] = dot_nt(cotangent[...], grid_of(down, 4))


def feed_kernel(where, x2, n3, cotangent, shifts, grad_act, *rest):
    up, down = rest[:16], rest[16:32]
    layer_out, g2, act, eh, total, back = rest[32:]
    f = pl.program_id(0)

    @pl.when(f == 0)
    def first():
        total[...] = x2[...]
        back[...] = jnp.zeros_like(back)

    root = (2.0 / np.pi) ** 0.5
    ups = [stacked(up[j::4], 0) for j in range(4)]
    hiddens = [dot(n3[...], ups[j]) for j in range(4)]
    for j, hidden in enumerate(hiddens):
        square = hidden * hidden
        bent = jnp.tanh(hidden * (root + (0.044715 * root) * square))
        gate = 0.5 * bent + 0.5
        value = hidden * gate
        act[:, part(j)] = low(value)
        slope = gate + value * (1.0 - gate) * (2.0 * root + (6.0 * 0.044715 * root) * square)
        eh[:, part(j)] = low(grad_act[:, part(j)] * slope)
    total[...] += dot(act[...], grid_of(down, 4))
    back[...] += dot_nt(eh[...], jnp.concatenate(ups, axis=1))

    @pl.when(f == FF // BLOCK // 4 - 1)
    def last():
        layer_out[...] = low(total[...])
        g2[...] = cotangent[...].astype(WIDE) + norm_back(x2[...], of_row(shifts, where, 5), back[...])


def feed_late_kernel(where, n3, cotangent, act, eh, store, turned, stage, sems):
    f = pl.program_id(0)
    wide = FF // BLOCK

    @pl.when(f == 0)
    def first():
        turned[...] = n3[...].T

    def products():
        up = low(dot(turned[...], eh[...]))
        down = low(dot(act[...].T, cotangent[...]))
        return [up[part(i), part(j)] for j in range(2) for i in range(4)] + [
            down[part(j), part(i)] for j in range(2) for i in range(4)
        ]

    numbers = [W_UP + i * wide + f * 2 + j for j in range(2) for i in range(4)]
    numbers += [W_DOWN + (f * 2 + j) * 4 + i for j in range(2) for i in range(4)]
    keep_blocks(products, stage, sems, store, where, numbers)


def self_backward_kernel(where, g2, sq, k_own, k_other, v_own, v_other, so, logs, *rest):
    q, k, v, o = rest[:4], rest[4:8], rest[8:12], rest[12:16]
    own_back, other_back, dq, dk, dv, es, probs, grads, sk, sv, own_total, other_total = rest[16:]
    n = pl.program_id(0)
    here = g2.shape[0]
    both = 2 * here

    @pl.when(n == 0)
    def first():
        es[...] = low(g2[...])
        own_total[...] = jnp.zeros_like(own_total)
        other_total[...] = jnp.zeros_like(other_total)

    grad_mixed = low(by_rows(es, o))
    sk[:here] = k_own[...]
    sk[here:] = k_other[...]
    sv[:here] = v_own[...]
    sv[here:] = v_other[...]
    wide_dq, wide_dk, wide_dv = attend_back(
        sq, sk, sv, sk[...].T, so[...], grad_mixed, logs[0], probs, grads, None, both
    )
    dq[...] = low(wide_dq)
    dk[...] = low(wide_dk)
    dv[...] = low(wide_dv)
    key_values = jnp.concatenate([stacked(k, 0), stacked(v, 0)], axis=1)
    both_grads = jnp.concatenate([dk[...], dv[...]], axis=1)
    own_total[...] += dot_nt(
        jnp.concatenate([dq[...], both_grads[:here]], axis=1),
        jnp.concatenate([stacked(q, 0), key_values], axis=1),
    )
    other_total[...] += dot_nt(both_grads[here:], key_values)

    @pl.when(n == 3)
    def last():
        own_back[...] = own_total[...]
        other_back[...] = low(other_total[...])


def self_late_kernel(where, g2, own_turned, other_turned, dq, dk, dv, so, old, store, es, turned, stage, sems):
    n = pl.program_id(0)
    here = g2.shape[0]

    @pl.when(n == 0)
    def first():
        es[...] = low(g2[...])
        turned[:, :here] = own_turned[...]
        turned[:, here:] = other_turned[...]

    def products():
        query = low(dot(own_turned[...], dq[...]))
        pair = low(dot(turned[...], jnp.concatenate([dk[...], dv[...]], axis=1)))
        flat = low(dot(so[...].T, es[...]))
        blocks = [query[part(i)] for i in range(4)]
        blocks += [pair[part(i), part(j)] for j in range(2) for i in range(4)]
        return blocks + [flat[:, part(i)] for i in range(4)]

    numbers = [base + i * 4 + n for base in (Q_SELF, K_SELF, V_SELF) for i in range(4)]
    numbers += [O_SELF + n * 4 + i for i in range(4)]
    keep_blocks(products, stage, sems, store, where, numbers)


def cross_backward_kernel(
    parts, where, x, g2, x1, own_back, got_back, turned, shifts, normed_turned, cq, ck, cv, co, logs, *rest
):
    q, k, v, o = rest[:4], rest[4:7], rest[7:10], rest[10:14]
    grad_x, grad_own, grad_others, store, grad_tokens, ec, g1, probs, grads, x_total, keys_padded, rows_padded, valid, stage, sems = rest[15:]
    n = pl.program_id(0)
    count = ck.shape[0]

    @pl.when(n == 0)
    def first():
        value = g2[...] + norm_back(
            x1[...], of_row(shifts, where, 3), own_back[...] + got_back[...].astype(WIDE)
        )
        g1[...] = value
        ec[...] = low(value)
        x_total[...] = jnp.zeros_like(x_total)
        grad_tokens[...] = jnp.zeros_like(grad_tokens)
        keys_padded[count:] = jnp.zeros_like(keys_padded[count:])
        for i in range(2):
            grads[i, count:] = jnp.zeros_like(grads[i, count:])
        rows_padded[count:] = jnp.zeros_like(rows_padded[count:])
        fill_valid(valid, where, parts)

    grad_mixed = low(by_rows(ec, o))
    keys_padded[:count] = ck[...]
    dq, dk, dv = attend_back(
        cq, ck, cv, keys_padded[...].T, co[...], grad_mixed, logs[0], probs, grads, valid[...], count
    )
    dq = low(dq)
    rows_padded[:count, :BLOCK] = low(dk)
    rows_padded[:count, BLOCK:] = low(dv)
    x_total[...] += dot_nt(dq, stacked(q, 0))
    grad_tokens[...] += dot_nt(
        rows_padded[:count],
        jnp.concatenate([stacked(k, 0), stacked(v, 0)], axis=1),
    )

    def products():
        query = low(dot(normed_turned[...], dq))
        pair = low(dot(turned[...], rows_padded[...]))
        flat = low(dot(co[...].T, ec[...]))
        blocks = [query[part(i)] for i in range(4)]
        blocks += [pair[part(i), part(j)] for j in range(2) for i in range(3)]
        return blocks + [flat[:, part(i)] for i in range(4)]

    numbers = [Q_CROSS + i * 4 + n for i in range(4)]
    numbers += [base + i * 4 + n for base in (K_CROSS, V_CROSS) for i in range(3)]
    numbers += [O_CROSS + n * 4 + i for i in range(4)]
    keep_blocks(products, stage, sems, store, where, numbers)

    @pl.when(n == 3)
    def last():
        half = grad_own.shape[0]
        grad_own[...] = grad_tokens[:half]
        grad_others[...] = low(grad_tokens[half:])
        grad_x[...] = g1[...] + norm_back(x[...].astype(WIDE), of_row(shifts, where, 1), x_total[...])


def shape(*dims, kind=LOW):
    return jax.ShapeDtypeStruct(dims, kind)


def call(kernel, grid, where, ins, outs, scratch, products, aliases=None, room=32):
    moved = BLOCK * BLOCK * 2 * grid * 16
    return pl.pallas_call(
        kernel,
        grid_spec=pltpu.PrefetchScalarGridSpec(
            num_scalar_prefetch=1,
            grid=(grid,),
            in_specs=[spec for _, spec in ins],
            out_specs=[spec for _, spec in outs],
            scratch_shapes=scratch,
        ),
        out_shape=[struct for struct, _ in outs],
        input_output_aliases=aliases or {},
        compiler_params=pltpu.CompilerParams(vmem_limit_bytes=room * 1024 * 1024),
        cost_estimate=pl.CostEstimate(
            flops=int(2 * products), bytes_accessed=moved, transcendentals=0
        ),
    )(where, *[array for array, _ in ins])


def full(array):
    return (array, whole(array.shape, pl.Buffered(1)))


def of_object(modulation):
    return full(modulation)


def made(*dims, kind=LOW):
    return (shape(*dims, kind=kind), whole(dims))


def striped(height):
    return (shape(height, D), stripe(height))


LOG_SPEC = pl.BlockSpec((1, 8, TOK_DEV), lambda n, where: (n, 0, 0))
ANYWHERE = pl.BlockSpec(memory_space=pl.ANY)


def padded_to(count):
    return -(-count // 128) * 128


def cross_forward(where, store, x, n1, tokens, shifts, parts):
    here, count = x.shape[0], tokens.shape[0]
    padded = padded_to(count)
    specs = columns(Q_CROSS, 4, 4) + columns(K_CROSS, 3, 4) + columns(V_CROSS, 3, 4) + rows(O_CROSS, 4)
    return call(
        functools.partial(cross_forward_kernel, parts),
        4,
        where,
        [full(x), full(n1), full(tokens), of_object(shifts)] + [(store, spec) for spec in specs],
        [
            striped(here),
            striped(count),
            striped(count),
            striped(here),
            (shape(4, 8, here, kind=WIDE), LOG_SPEC),
            made(here, D, kind=WIDE),
            made(here, D),
        ],
        [
            pltpu.VMEM((here, D), LOW),
            pltpu.VMEM((D, D), LOW),
            pltpu.VMEM((padded, BLOCK), LOW),
            pltpu.VMEM((2, padded, 2 * here), LOW),
            pltpu.VMEM((count, 128), WIDE),
        ],
        here * D * D * 12,
        room=34,
    )


def tall(here):
    return pl.BlockSpec((BLOCK, here), lambda n, where: (n, 0))


def self_own(where, store, mine):
    here = mine.shape[0]
    specs = columns(Q_SELF, 4, 4) + columns(K_SELF, 4, 4) + columns(V_SELF, 4, 4)
    return call(
        self_own_kernel,
        4,
        where,
        [full(mine)] + [(store, spec) for spec in specs],
        [
            made(D, here),
            striped(here),
            striped(here),
            striped(here),
            (shape(D, here, kind=WIDE), tall(here)),
            (shape(4, 8, here, kind=WIDE), LOG_SPEC),
        ],
        [pltpu.VMEM((2, here, 2 * here), LOW)],
        here * D * D * 6,
    )


def self_other(where, store, x1, other, shifts, sq, mix, stats):
    here = x1.shape[0]
    specs = columns(K_SELF, 4, 4) + columns(V_SELF, 4, 4) + rows(O_SELF, 4)
    return call(
        self_other_kernel,
        4,
        where,
        [full(x1), full(other), of_object(shifts), (sq, stripe(here)), (mix, tall(here)), (stats, LOG_SPEC)]
        + [(store, spec) for spec in specs],
        [
            made(D, here),
            striped(here),
            striped(here),
            striped(here),
            (shape(4, 8, here, kind=WIDE), LOG_SPEC),
            made(here, D, kind=WIDE),
            made(here, D),
        ],
        [pltpu.VMEM((here, D), LOW), pltpu.VMEM((D, D), LOW), pltpu.VMEM((2, here, 2 * here), LOW)],
        here * D * D * 6,
    )


def feed_specs(height):
    wide = FF // BLOCK
    up = [
        pl.BlockSpec(
            (1, BLOCK, BLOCK),
            lambda n, where, i=i, j=j: (where[W_UP + i * wide + n * height + j], 0, 0),
        )
        for i in range(4)
        for j in range(height)
    ]
    down = [
        pl.BlockSpec(
            (1, BLOCK, BLOCK), lambda n, where, i=i: (where[W_DOWN + n * height * 4 + i], 0, 0)
        )
        for i in range(4 * height)
    ]
    return up, down


def broad(here, height):
    return pl.BlockSpec((here, height * BLOCK), lambda n, where: (0, n))


def feed_early(where, store, cotangent):
    here = cotangent.shape[0]
    return call(
        feed_early_kernel,
        FF // BLOCK // 4,
        where,
        [full(cotangent)] + [(store, spec) for spec in feed_specs(4)[1]],
        [(shape(here, FF, kind=WIDE), broad(here, 4))],
        [],
        here * D * FF,
    )[0]


def feed(where, store, x2, n3, cotangent, shifts, grad_act):
    here = x2.shape[0]
    up, down = feed_specs(4)
    return call(
        feed_kernel,
        FF // BLOCK // 4,
        where,
        [full(x2), full(n3), full(cotangent), of_object(shifts), (grad_act, broad(here, 4))]
        + [(store, spec) for spec in up + down],
        [
            made(here, D),
            made(here, D, kind=WIDE),
            (shape(here, FF), broad(here, 4)),
            (shape(here, FF), broad(here, 4)),
        ],
        [pltpu.VMEM((here, D), WIDE), pltpu.VMEM((here, D), WIDE)],
        here * D * FF * 3,
        room=32,
    )


def feed_late(where, n3, cotangent, act, eh, slots):
    here = n3.shape[0]
    return call(
        feed_late_kernel,
        FF // BLOCK // 2,
        where,
        [full(n3), full(cotangent), (act, broad(here, 2)), (eh, broad(here, 2))],
        [(shape(slots, BLOCK, BLOCK), ANYWHERE)],
        [
            pltpu.VMEM((D, here), LOW),
            pltpu.VMEM((2, 16, BLOCK, BLOCK), LOW),
            pltpu.SemaphoreType.DMA((2, 16)),
        ],
        here * D * FF * 2,
        room=26,
    )[0]


def self_backward(where, store, g2, sq, k_own, k_other, v_own, v_other, so, logs):
    here = g2.shape[0]
    specs = columns(Q_SELF, 4, 4) + columns(K_SELF, 4, 4) + columns(V_SELF, 4, 4) + rows(O_SELF, 4)
    ins = [full(g2)] + [(a, stripe(here)) for a in (sq, k_own, k_other, v_own, v_other, so)]
    ins += [(logs, LOG_SPEC)] + [(store, spec) for spec in specs]
    return call(
        self_backward_kernel,
        4,
        where,
        ins,
        [made(here, D, kind=WIDE), made(here, D), striped(here), striped(2 * here), striped(2 * here)],
        [
            pltpu.VMEM((here, D), LOW),
            pltpu.VMEM((1, 2 * here, 2 * here), LOW),
            pltpu.VMEM((1, 2 * here, 2 * here), LOW),
            pltpu.VMEM((2 * here, BLOCK), LOW),
            pltpu.VMEM((2 * here, BLOCK), LOW),
            pltpu.VMEM((here, D), WIDE),
            pltpu.VMEM((here, D), WIDE),
        ],
        here * D * D * 16,
        room=28,
    )


def self_late(where, grads, g2, own_turned, other_turned, dq, dk, dv, so):
    here = g2.shape[0]
    ins = [full(a) for a in (g2, own_turned, other_turned)]
    ins += [(a, stripe(a.shape[0])) for a in (dq, dk, dv, so)] + [(grads, ANYWHERE)]
    return call(
        self_late_kernel,
        4,
        where,
        ins,
        [(shape(*grads.shape), ANYWHERE)],
        [
            pltpu.VMEM((here, D), LOW),
            pltpu.VMEM((D, 2 * here), LOW),
            pltpu.VMEM((2, 16, BLOCK, BLOCK), LOW),
            pltpu.SemaphoreType.DMA((2, 16)),
        ],
        here * D * D * 6,
        {len(ins): 0},
        room=30,
    )[0]


def cross_backward(
    where, store, grads, x, g2, x1, own_back, got_back, turned, shifts, normed_turned, cq, ck, cv, co, logs, parts
):
    here, count = x.shape[0], ck.shape[0]
    padded = padded_to(count)
    specs = columns(Q_CROSS, 4, 4) + columns(K_CROSS, 3, 4) + columns(V_CROSS, 3, 4) + rows(O_CROSS, 4)
    ins = [full(a) for a in (x, g2, x1, own_back, got_back, turned)]
    ins += [of_object(shifts), full(normed_turned)]
    ins += [(a, stripe(a.shape[0])) for a in (cq, ck, cv, co)] + [(logs, LOG_SPEC)]
    ins += [(store, spec) for spec in specs] + [(grads, ANYWHERE)]
    return call(
        functools.partial(cross_backward_kernel, parts),
        4,
        where,
        ins,
        [
            made(here, D, kind=WIDE),
            made(count // parts, DIMG, kind=WIDE),
            made(count - count // parts, DIMG),
            (shape(*grads.shape), ANYWHERE),
        ],
        [
            pltpu.VMEM((count, DIMG), WIDE),
            pltpu.VMEM((here, D), LOW),
            pltpu.VMEM((here, D), WIDE),
            pltpu.VMEM((2, padded, 2 * here), LOW),
            pltpu.VMEM((2, padded, 2 * here), LOW),
            pltpu.VMEM((here, D), WIDE),
            pltpu.VMEM((padded, BLOCK), LOW),
            pltpu.VMEM((padded, 2 * BLOCK), LOW),
            pltpu.VMEM((count, 128), WIDE),
            pltpu.VMEM((2, 14, BLOCK, BLOCK), LOW),
            pltpu.SemaphoreType.DMA((2, 14)),
        ],
        here * D * D * 24,
        {len(ins): 3},
        room=40,
    )


def hand_on_kernel(*refs):
    count = len(refs) // 2
    for source, target in zip(refs[:count], refs[count:-1]):
        target[...] = source[...]
    refs[-1][...] = low(refs[count - 1][...])


def hand_on(arrays):
    specs = [
        pl.BlockSpec((a.shape[0] // 2,) + a.shape[1:], lambda i: (i, 0, 0)) for a in arrays
    ]
    structs = [jax.ShapeDtypeStruct(a.shape, a.dtype) for a in arrays]
    return pl.pallas_call(
        hand_on_kernel,
        grid=(2,),
        out_shape=structs + [jax.ShapeDtypeStruct(arrays[-1].shape, LOW)],
        in_specs=specs,
        out_specs=specs + specs[-1:],
        compiler_params=pltpu.CompilerParams(vmem_limit_bytes=VLIM),
    )(*arrays)


def partner(block, axis):
    size = lax.axis_size(axis)
    return lax.ppermute(block, axis, [(i, i ^ 1) for i in range(size)])


def soap_update(
    slot_grads,
    first_moment,
    second_moment,
    left_basis,
    right_basis,
    master_weights,
    slot_rates,
    slot_used,
):
    keep_mask = slot_used[:, None, None] > 0.0
    slot_grads = jnp.where(keep_mask, slot_grads, 0.0)
    rotated = jnp.matmul(
        jnp.matmul(jnp.swapaxes(left_basis, 1, 2), slot_grads, precision=highest),
        right_basis,
        precision=highest,
    )
    first_new = moment_decay * first_moment + (1.0 - moment_decay) * rotated
    second_new = moment_decay * second_moment + (1.0 - moment_decay) * rotated * rotated
    correction = 1.0 - moment_decay**STEP
    normalized = first_new / correction / (jnp.sqrt(second_new / correction) + 1e-08)
    rotated_back = jnp.matmul(
        jnp.matmul(left_basis, normalized, precision=highest),
        jnp.swapaxes(right_basis, 1, 2),
        precision=highest,
    )
    fresh_master = master_weights - slot_rates[:, None, None] * (
        rotated_back + 0.01 * master_weights
    )
    fresh_master = jnp.where(keep_mask, fresh_master, 0.0)
    return (
        slot_grads,
        jnp.where(keep_mask, first_new, 0.0),
        jnp.where(keep_mask, second_new, 0.0),
        fresh_master,
        fresh_master.astype(jnp.bfloat16),
    )


def shards(
    triplane,
    cotangent,
    image_tokens,
    modulation,
    image_counts,
    owner_slots,
    master_weights,
    first_moment,
    second_moment,
    left_basis,
    right_basis,
):
    img_size = lax.axis_size("img")
    rows_size = lax.axis_size("rows")
    img_index = lax.axis_index("img")
    flat_index = lax.axis_index("rows") * img_size + img_index
    object_index = flat_index // 2
    pair_index = img_index // 2
    groups = img_size // 2
    slot_cap = image_tokens.shape[0] // groups
    own_count = master_weights.shape[0]
    slot_total = rows_size * img_size * own_count
    fits = rows_size == 16 and img_size == 2 and own_count == 8
    modulation = jnp.swapaxes(modulation, 0, 1)
    info = [object_index[None]]
    if img_size == 2:
        info += [img_index[None], 1 - img_index[None]]
    else:
        info += [jnp.arange(img_size, dtype=jnp.int32)]
    info += [image_counts]
    if fits:
        store, tokens, tokens_turned, n1, n1_turned = gather(
            master_weights, image_tokens, triplane, modulation
        )
        store = store.reshape(-1, BLOCK, BLOCK)
        where = [positions(owner_slots, WAYS_OUT), positions(owner_slots, WAYS_IN)]
    else:
        store = lax.all_gather(master_weights.astype(LOW), ("rows", "img"), axis=0, tiled=True)
        where = [owner_slots, owner_slots]
        if img_size == 2:
            tokens = jnp.concatenate([image_tokens, partner(image_tokens, "img")], 0)
        else:
            tokens = lax.all_gather(image_tokens, "img", axis=0, tiled=True)
            tokens = tokens.reshape(img_size, groups, slot_cap, DIMG)
            tokens = lax.dynamic_index_in_dim(tokens, pair_index, 1, keepdims=False)
            tokens = tokens.reshape(img_size * slot_cap, DIMG)
        count = tokens.shape[0]
        tokens_turned = jnp.pad(tokens.T, ((0, 0), (0, padded_to(count) - count)))
        shifts = lax.dynamic_index_in_dim(modulation, object_index, 1, keepdims=False)
        n1 = low(modulated_norm(triplane.astype(WIDE), shifts[0], shifts[1]))
        n1_turned = n1.T
    where = jnp.concatenate([piece.astype(jnp.int32) for piece in where + info])

    cq, ck, cv, co, cross_logs, x1, n2 = cross_forward(
        where, store, triplane, n1, tokens, modulation, img_size
    )
    n2_other = partner(n2, "img")
    own_turned, sq, k_own, v_own, mix, stats = self_own(where, store, n2)
    grad_act = feed_early(where, store, cotangent)
    other_turned, k_other, v_other, so, self_logs, x2, n3 = self_other(
        where, store, x1, n2_other, modulation, sq, mix, stats
    )
    layer_out, g2, act, eh = feed(where, store, x2, n3, cotangent, modulation, grad_act)
    own_back, other_back, dq, dk, dv = self_backward(
        where, store, g2, sq, k_own, k_other, v_own, v_other, so, self_logs
    )
    got_back = partner(other_back, "img")
    grads = feed_late(where, n3, cotangent, act, eh, slot_total)
    grads = self_late(where, grads, g2, own_turned, other_turned, dq, dk, dv, so)
    grad_triplane, grad_own, grad_others, grads = cross_backward(
        where,
        store,
        grads,
        triplane,
        g2,
        x1,
        own_back,
        got_back,
        tokens_turned,
        modulation,
        n1_turned,
        cq,
        ck,
        cv,
        co,
        cross_logs,
        img_size,
    )
    if img_size == 2:
        grad_image = grad_own + partner(grad_others, "img").astype(WIDE)
    else:
        pick = (jnp.arange(groups, dtype=jnp.int32) == pair_index).astype(WIDE)
        grad_tokens = jnp.concatenate([grad_own, grad_others.astype(WIDE)], 0)
        spread = grad_tokens.reshape(img_size, 1, slot_cap, DIMG) * pick[None, :, None, None]
        grad_image = lax.psum_scatter(
            spread.reshape(img_size * groups * slot_cap, DIMG).astype(LOW),
            "img",
            scatter_dimension=0,
            tiled=True,
        ).astype(WIDE)
    my_slots = flat_index * own_count + jnp.arange(own_count, dtype=jnp.int32)
    matched = (owner_slots[:, None] == my_slots[None, :]).astype(WIDE)
    slot_used = jnp.sum(matched, axis=0)
    slot_rates = jnp.sum(matched * jnp.asarray(block_table(weight_scales()))[:, None], axis=0)
    state = (first_moment, second_moment, left_basis, right_basis, master_weights)
    if fits:
        rates = jnp.broadcast_to(
            jnp.stack([slot_rates, slot_used], 1)[:, :, None], (own_count, 2, BLOCK)
        )
        updated = hand_on(scatter(grads.reshape(2, 8, 16, BLOCK, BLOCK), *state, rates))
    else:
        used = jnp.zeros((slot_total,), jnp.bool_).at[owner_slots].set(True)
        grads = jnp.where(used[:, None, None], grads, jnp.zeros_like(grads))
        slot_grads = lax.psum_scatter(
            grads, ("rows", "img"), scatter_dimension=0, tiled=True
        ).astype(WIDE)
        updated = soap_update(slot_grads, *state, slot_rates, slot_used)
    return (layer_out, grad_triplane, grad_image) + tuple(updated)


def solution(mesh):
    flat = P(("rows", "img"), None)
    blocks = P(("rows", "img"), None, None)
    in_specs = (flat, flat, flat, P(), P(), P()) + (blocks,) * 5
    out_specs = (flat, flat, flat) + (blocks,) * 5
    return jax.shard_map(shards, mesh=mesh, in_specs=in_specs, out_specs=out_specs, check_vma=False)
```
